256 devices in a mesh: pipe: 16 (over y_lo, z), section: 4 (over y_hi, core), tensor: 4 (over x).
Axes of the slice: x: 4, y: 4 (y_hi: 2, y_lo: 2; y = y_hi * 2 + y_lo), z: 8, core: 2. Of those that a mesh axis runs over, the one named last changes fastest.
Arguments:
- section_input: bfloat16 [16, 4, 384, 2560], P('pipe', 'section', None, 'tensor'), may hold values from -120 to 120
- section_cotan: bfloat16 [16, 4, 384, 2560], P('pipe', 'section', None, 'tensor'), may hold values from -6 to 6
- weights: bfloat16 [6, 2560, 2560], P(None, 'pipe', 'tensor'), may hold values from -0.125 to 0.125
- section_cuts: int32 [3, 5], replicated, may hold values from 0 to 6, as said below
- pipe_template: int32 [16], replicated, may hold values from 0 to 2
Outputs:
- weight_grads: float32 [6, 2560, 2560], P(None, ('pipe', 'section'), 'tensor')
The draws below stay inside these ranges and needn't reach their ends.
Inputs may be any that keep to these rules, and one draw needn't show every extreme that they name: `section_cuts`: row t starts at 0 and ends with 6; each section holds 1 or 2 layers, and 2 sections of every template hold 2.
All inputs are finite; a program needn't handle non-finite values.
Results may differ from the reference program's by a relative error of at most 0.0039.
Values may be sent and summed in bfloat16 or wider, within the bound.
No kernel may reach another device: no remote copies, remote signals or barrier semaphores. Data moves between devices by JAX's collectives and lax.ppermute only.
A program may use at most 128 MiB of HBM per device.

```python
import math
import jax
import jax.numpy as jnp
from jax import lax

D = 2560
LAYERS = 6
TEMPLATES = 3
TOK = 384
PIPES = 16
SECTIONS = 4


def draw_section_input(key, part):
    subkeys = jax.random.split(key, 3)
    full_shape = (PIPES, SECTIONS, TOK, D)
    columns = jnp.exp(jax.random.uniform(subkeys[1], (D,), jnp.float32, 0.0, math.log(10.0)))
    row_scale = jnp.exp(jax.random.uniform(subkeys[2], (PIPES, SECTIONS, TOK, 1), jnp.float32, 0.0, math.log(3.0)))
    draws_base = jnp.clip(jax.random.normal(subkeys[0], full_shape, jnp.float32), -4.0, 4.0)
    return (draws_base * columns * row_scale).astype(jnp.bfloat16)


def draw_section_cuts(key, part):
    surplus = LAYERS - SECTIONS

    def single_template(template_index):
        ranking = jax.random.permutation(jax.random.fold_in(key, template_index), SECTIONS)
        section_sizes = 1 + (ranking < surplus).astype(jnp.int32)
        return jnp.concatenate([jnp.zeros((1,), jnp.int32), jnp.cumsum(section_sizes).astype(jnp.int32)])
    return jnp.stack([single_template(template_index) for template_index in range(TEMPLATES)])


def plant(array, rng, least, top_value):
    longest = array.shape.index(max(array.shape))
    spots = []
    for shift in (0, 1):
        where = [jax.random.randint(jax.random.fold_in(rng, axis), (), 0, length) for axis, length in enumerate(array.shape)]
        where[longest] = (where[longest] + shift) % array.shape[longest]
        spots.append(tuple(where))
    return array.at[spots[0]].set(least).at[spots[1]].set(top_value)


def block_scale(key, dims, cuts, smallest, largest):
    def one(position, blocks):
        steps = jax.random.uniform(jax.random.fold_in(jax.random.fold_in(key, 6), position), (blocks,), jnp.float32, smallest / len(cuts), largest / len(cuts))
        return jnp.repeat(jnp.exp(steps), dims[position] // blocks).reshape((-1,) + (1,) * (len(dims) - position - 1))

    level = one(*cuts[0])
    for cut in cuts[1:]:
        level = level * one(*cut)
    return level


def gaussian(key, shape, scale, most, cuts=(), kind=jnp.bfloat16):
    factor_of = block_scale(key, shape, cuts, -0.22, 0.18) if cuts else 1.0
    drawn = jax.random.normal(key, shape, jnp.float32) * scale * factor_of
    return jnp.minimum(jnp.maximum(drawn, -most), most).astype(kind)


def setup_inputs(seed: int = 0) -> dict:
    splits = jax.random.split(jax.random.key(seed), 6)
    return {
        "section_input": draw_section_input(jax.random.fold_in(splits[5], 71), 0),
        "section_cotan": gaussian(splits[1], (PIPES, SECTIONS, TOK, D), 1.0, 6.0, ((0, 16), (1, 4), (3, 4))),
        "weights": gaussian(splits[2], (LAYERS, D, D), D ** -0.5, 0.125, ((1, 16), (2, 4))),
        "section_cuts": draw_section_cuts(jax.random.fold_in(splits[5], 71), 0),
        "pipe_template": plant(jax.random.randint(splits[4], (PIPES,), 0, TEMPLATES), jax.random.fold_in(splits[4], 1), 0, TEMPLATES - 1).astype(jnp.int32),
    }


epsilon = 1e-05

def forward_rows(values):
    inv_rms = lax.rsqrt(lax.optimization_barrier(jnp.mean(values * values, axis=1, keepdims=True)) + epsilon)
    active = jax.nn.silu(values * inv_rms).astype(jnp.bfloat16)
    return (inv_rms, active)

def reference(section_input, section_cotan, weights, section_cuts, pipe_template):
    layers = weights.shape[0]

    def one_pipe(totals, pipe_items):
        inputs, cotans, template = pipe_items
        template_pick = (jnp.arange(TEMPLATES, dtype=jnp.int32) == template).astype(jnp.int32)
        bounds = lax.optimization_barrier(jnp.sum(template_pick[:, None] * section_cuts, axis=0)).astype(jnp.int32)
        for section_index in range(SECTIONS):
            first = bounds[section_index]
            section_stop = bounds[section_index + 1]
            second = jnp.minimum(first + 1, layers - 1).astype(jnp.int32)
            second_live = (first + 1 < section_stop).astype(jnp.float32)
            first_matrix = lax.dynamic_index_in_dim(weights, first, 0, keepdims=False)
            second_matrix = lax.dynamic_index_in_dim(weights, second, 0, keepdims=False)
            h_first = inputs[section_index].astype(jnp.float32)
            inv_first, active_first = forward_rows(h_first)
            raised = h_first + jnp.dot(active_first, first_matrix, preferred_element_type=jnp.float32)
            h_second = lax.optimization_barrier(raised.astype(jnp.bfloat16)).astype(jnp.float32)
            inv_second, active_second = forward_rows(h_second)
            cotan = cotans[section_index].astype(jnp.float32)
            cotan_low = cotans[section_index]
            grad_second = jnp.dot(active_second.T, cotan_low, preferred_element_type=jnp.float32) * second_live
            summed = jnp.dot(cotan_low, second_matrix.T, preferred_element_type=jnp.float32)
            normed = h_second * inv_second
            gate_sig = jax.nn.sigmoid(normed)
            d_norm = summed * gate_sig * (1.0 + normed * (1.0 - gate_sig))
            mean_term = lax.optimization_barrier(jnp.mean(h_second * d_norm, axis=1, keepdims=True))
            d_rows = inv_second * d_norm - h_second * inv_second * inv_second * inv_second * mean_term
            cotan_first = cotan + second_live * d_rows
            grad_first = jnp.dot(active_first.T, cotan_first.astype(jnp.bfloat16), preferred_element_type=jnp.float32)
            totals = totals.at[first].add(grad_first)
            totals = totals.at[second].add(grad_second)
        return (totals, None)
    totals = jnp.zeros((layers, D, D), jnp.float32)
    totals, _ = lax.scan(one_pipe, totals, (section_input, section_cotan, pipe_template))
    return totals
```

```python
import jax
import jax.numpy as jnp
from jax import lax
from jax.sharding import PartitionSpec as P

epsilon = 1e-05
bf16 = jnp.bfloat16
f32 = jnp.float32


def pick(array, index, axis=0):
    return lax.dynamic_index_in_dim(array, index, axis, keepdims=False)


def place(buffer, chunk, index, axis):
    return lax.dynamic_update_slice_in_dim(buffer, jnp.expand_dims(chunk, axis), index, axis)


def split_three(values):
    high = values.astype(bf16)
    rest = values - high.astype(f32)
    middle = rest.astype(bf16)
    low = (rest - middle.astype(f32)).astype(bf16)
    return high, middle, low


def silu(values):
    return values * jax.nn.sigmoid(values)


def shards(section_input, section_cotan, weights, section_cuts, pipe_template):
    pipes = lax.axis_size("pipe")
    sections = lax.axis_size("section")
    tensors = lax.axis_size("tensor")
    layers, stored, width = weights.shape
    tokens = section_input.shape[2]
    features = width * tensors
    fine = stored // sections
    lows, depth = 2, pipes // 2
    per_col = pipes // tensors
    piece = per_col * fine
    pipe_idx = lax.axis_index("pipe")
    low_idx, z_idx = pipe_idx // depth, pipe_idx % depth
    section_idx = lax.axis_index("section")
    high_idx, core_idx = section_idx // 2, section_idx % 2
    tensor_idx = lax.axis_index("tensor")

    def z_step(array, shift):
        pairs = [(y * depth + z, y * depth + (z + shift) % depth) for y in range(lows) for z in range(depth)]
        return lax.ppermute(array, "pipe", pairs)

    def y_swap(array):
        return lax.ppermute(array, "pipe", [(p, (p + depth) % pipes) for p in range(pipes)])

    def x_step(array, shift):
        return lax.ppermute(array, "tensor", [(t, (t + shift) % tensors) for t in range(tensors)])

    def core_swap(array):
        return lax.ppermute(array, "section", [(s, s ^ 1) for s in range(sections)])

    def high_swap(array):
        return lax.ppermute(array, "section", [(s, s ^ 2) for s in range(sections)])

    def sum_all(array):
        array = array + x_step(array, 1) + x_step(array, 2) + x_step(array, 3)
        array = array + core_swap(array)
        return array + high_swap(array)

    def gather_x(chunk, half_axis):
        buffer = jnp.zeros((chunk.shape[0], tensors, *chunk.shape[1:]), chunk.dtype)
        buffer = place(buffer, chunk, tensor_idx, 1)
        right, left = x_step(chunk, 1), x_step(chunk, -1)
        buffer = place(buffer, right, (tensor_idx - 1) % tensors, 1)
        buffer = place(buffer, left, (tensor_idx + 1) % tensors, 1)
        half = chunk.shape[half_axis] // 2
        far_a = x_step(lax.slice_in_dim(right, 0, half, axis=half_axis), 1)
        far_b = x_step(lax.slice_in_dim(left, half, 2 * half, axis=half_axis), -1)
        far = jnp.concatenate([far_a, far_b], axis=half_axis)
        return place(buffer, far, (tensor_idx + 2) % tensors, 1)

    def gather_section(chunk):
        other = high_swap(chunk)
        mine = core_swap(chunk)
        theirs = core_swap(other)
        buffer = jnp.zeros((sections, *chunk.shape), chunk.dtype)
        buffer = place(buffer, chunk, section_idx, 0)
        buffer = place(buffer, other, section_idx ^ 2, 0)
        buffer = place(buffer, mine, section_idx ^ 1, 0)
        return place(buffer, theirs, section_idx ^ 3, 0)

    cuts = pick(section_cuts, pick(pipe_template, pipe_idx))
    starts = [cuts[s] for s in range(sections)]
    live = [cuts[s + 1] > cuts[s] + 1 for s in range(sections)]
    live_int = [flag.astype(jnp.int32) for flag in live]
    live_sections = [
        sum(live_int[s] * s * (sum(live_int[:s]) == j) for s in range(sections)) for j in range(2)
    ]
    first_layers = [pick(cuts, s) for s in live_sections]

    shard = lax.dynamic_slice_in_dim(weights, section_idx * fine, fine, 1)
    with jax.named_scope("weights_gather"):
        other = y_swap(shard)
        is_low = low_idx == 0
        pair = jnp.stack([jnp.where(is_low, shard, other), jnp.where(is_low, other, shard)], axis=1)
        matrices = jnp.zeros((layers, lows, depth, fine, width), bf16)
        matrices = place(matrices, pair, z_idx, 2)
        right = left = pair
        for k in range(1, depth // 2):
            right, left = z_step(right, 1), z_step(left, -1)
            matrices = place(matrices, right, (z_idx - k) % depth, 2)
            matrices = place(matrices, left, (z_idx + k) % depth, 2)
        far = jnp.stack([z_step(right[:, 0], 1), z_step(left[:, 1], -1)], axis=1)
        matrices = place(matrices, far, (z_idx + depth // 2) % depth, 2)
        matrices = matrices.reshape(layers, pipes * fine, width)

    with jax.named_scope("spread_inputs"):
        h_cols = section_input[0, 0].T
        c_cols = section_cotan[0, 0].T
        h_wide = h_cols.astype(f32)
        squares = jnp.stack(split_three(jnp.sum(h_wide * h_wide, axis=0)))
        extra = jnp.zeros((16, tokens), bf16).at[:3].set(squares)
        blocks = h_cols.reshape(per_col, sections, fine, tokens).transpose(1, 0, 2, 3)
        blocks = blocks.reshape(sections, piece, tokens)
        blocks = jnp.concatenate([blocks, jnp.broadcast_to(extra, (sections, 16, tokens))], axis=1)
        mine = lax.all_to_all(blocks, "section", split_axis=0, concat_axis=0, tiled=True)
        spread = gather_x(mine, 0)
        cotans = gather_section(c_cols)

    h_pieces = mine[:, :piece]
    h_rows = spread[:, :, :piece].astype(f32)
    square_sum = jnp.sum(spread[:, :, piece : piece + 3].astype(f32), axis=(1, 2))
    inv_first = lax.rsqrt(square_sum / features + epsilon)[:, None, None, :]
    active_first = silu(h_rows * inv_first).astype(bf16).reshape(sections, tensors * piece, tokens)

    outs = [
        lax.dot_general(
            pick(matrices, first_layers[j]),
            pick(active_first, live_sections[j]),
            (((0,), (0,)), ((), ())),
            preferred_element_type=f32,
        )
        for j in range(2)
    ]
    partial = jnp.stack(outs).reshape(2, per_col, 2, 2, fine, tokens)
    with jax.named_scope("forward_sum"):
        partial = pick(partial, core_idx, 3) + core_swap(pick(partial, 1 - core_idx, 3).astype(bf16)).astype(f32)
        partial = pick(partial, high_idx, 2) + high_swap(pick(partial, 1 - high_idx, 2).astype(bf16)).astype(f32)
    raised = partial.reshape(2, piece, tokens)
    h_live = jnp.stack([pick(h_pieces, s) for s in live_sections]).astype(f32)
    h_low = (h_live + raised).astype(bf16)

    backs = [
        lax.dot_general(
            pick(matrices, first_layers[j] + 1),
            pick(cotans, live_sections[j]),
            (((1,), (0,)), ((), ())),
            preferred_element_type=f32,
        )
        for j in range(2)
    ]
    with jax.named_scope("backward_sum"):
        backs = jnp.stack([b.reshape(tensors, piece, tokens) for b in backs], axis=1).astype(bf16)
        received = lax.all_to_all(backs, "tensor", split_axis=0, concat_axis=0, tiled=True)
        summed = jnp.sum(received.astype(f32), axis=0)

    h_second = h_low.astype(f32)
    with jax.named_scope("second_norm"):
        second_squares = sum_all(jnp.sum(h_second * h_second, axis=1))
    inv_second = lax.rsqrt(second_squares / features + epsilon)
    inv = inv_second[:, None, :]
    with jax.named_scope("spread_second"):
        h_second_rows = gather_x(h_low, 0).astype(f32)
    active_second = silu(h_second_rows * inv[:, None]).astype(bf16).reshape(2, tensors * piece, tokens)
    normed = h_second * inv
    gate = jax.nn.sigmoid(normed)
    d_norm = summed * gate * (1.0 + normed * (1.0 - gate))
    with jax.named_scope("mean_term"):
        mean_term = (sum_all(jnp.sum(h_second * d_norm, axis=1)) / features)[:, None, :]
    d_rows = inv * d_norm - h_second * inv * inv * inv * mean_term
    by_fine = cotans.reshape(sections, per_col, sections, fine, tokens)
    own_cotan = jnp.stack([pick(pick(by_fine, s), section_idx, 1) for s in live_sections])
    cotan_first = (own_cotan.reshape(2, piece, tokens).astype(f32) + d_rows).astype(bf16)
    with jax.named_scope("spread_cotan"):
        gathered = gather_section(cotan_first.reshape(2, per_col, fine, tokens))
        cotan_live = gathered.transpose(1, 2, 0, 3, 4).reshape(2, width, tokens)

    lefts = jnp.concatenate([active_first, active_second])
    rights = jnp.concatenate([cotans, cotan_live])
    factors_a, factors_b = [], []
    for layer in range(layers):
        own = [(starts[s] <= layer) & (layer < cuts[s + 1]) for s in range(sections)]
        place_of = sum(own[s] * s for s in range(sections))
        order = sum(own[s] * sum(live_int[:s]) for s in range(sections))
        upper = sum(own[s] * (starts[s] < layer) for s in range(sections)) > 0
        lives = sum(own[s] * live_int[s] for s in range(sections)) > 0
        factors_a.append(pick(lefts, jnp.where(upper, sections + order, place_of)))
        factors_b.append(pick(rights, jnp.where(lives & ~upper, sections + order, place_of)))
    factor_a = jnp.stack(factors_a).reshape(layers, lows, depth, fine, tokens)
    factor_b = jnp.stack(factors_b)

    def block_grad(shift):
        rows = pick(factor_a, (z_idx + shift) % depth, 2).reshape(layers, lows * fine, tokens)
        grad = lax.dot_general(rows, factor_b, (((2,), (2,)), ((0,), (0,))), preferred_element_type=f32)
        return grad.reshape(layers, lows, fine, width)

    with jax.named_scope("grad_sum"):
        far = block_grad(depth // 2).astype(bf16)
        right = z_step(far[:, 0], 1).astype(f32)
        left = z_step(far[:, 1], -1).astype(f32)
        right = block_grad(depth // 2 - 1) + jnp.stack([right, jnp.zeros_like(right)], axis=1)
        left = block_grad(depth // 2 + 1) + jnp.stack([jnp.zeros_like(left), left], axis=1)
        for k in range(depth // 2 - 2, -1, -1):
            right_in = z_step(right.astype(bf16), 1).astype(f32)
            left_in = z_step(left.astype(bf16), -1).astype(f32)
            if k:
                right = block_grad(k) + right_in
                left = block_grad(depth - k) + left_in
        total = block_grad(0) + right_in + left_in
        return pick(total, low_idx, 1) + y_swap(pick(total, 1 - low_idx, 1).astype(bf16)).astype(f32)


def solution(mesh):
    in_specs = (
        P("pipe", "section", None, "tensor"),
        P("pipe", "section", None, "tensor"),
        P(None, "pipe", "tensor"),
        P(),
        P(),
    )
    out_specs = P(None, ("pipe", "section"), "tensor")
    return jax.shard_map(shards, mesh=mesh, in_specs=in_specs, out_specs=out_specs, check_vma=False)
```

```python
import functools

import jax
import jax.numpy as jnp
from jax import lax
from jax.experimental import pallas as pl
from jax.experimental.pallas import tpu as pltpu
from jax.sharding import PartitionSpec as P

epsilon = 1e-05
bf16 = jnp.bfloat16
f32 = jnp.float32
extra_rows = 16

FIRST, LIVE, LIVE_REL, HOME, UPPER, ORDER, HOME_REL, RAISED, BLOCK, SELF = 0, 2, 4, 6, 12, 18, 24, 30, 36, 44
DISTANCE = (4, 3, 5, 2, 6, 1, 7, 0)
Z, LOW, SECTION, TENSOR = SELF, SELF + 1, SELF + 2, SELF + 3
PLAN = 48


def silu(values):
    return values * jax.nn.sigmoid(values)


def split_three(values):
    high = values.astype(bf16)
    rest = values - high.astype(f32)
    middle = rest.astype(bf16)
    low = (rest - middle.astype(f32)).astype(bf16)
    return high, middle, low


def plan_kernel(layers, sections, depth, cuts_ref, template_ref, self_ref, plan_ref):
    pipe, section, tensor = self_ref[0], self_ref[1], self_ref[2]
    template = template_ref[pipe]
    cuts = [cuts_ref[template, s] for s in range(sections + 1)]
    live = [jnp.where(cuts[s + 1] > cuts[s] + 1, 1, 0) for s in range(sections)]
    before = [sum(live[:s], jnp.int32(0)) for s in range(sections)]
    for j in range(2):
        here = [jnp.where((live[s] == 1) & (before[s] == j), 1, 0) for s in range(sections)]
        which = sum(here[s] * s for s in range(sections))
        plan_ref[FIRST + j] = sum(here[s] * cuts[s] for s in range(sections))
        plan_ref[LIVE + j] = which
        plan_ref[LIVE_REL + j] = which ^ section
    for layer in range(layers):
        own = [jnp.where((cuts[s] <= layer) & (layer < cuts[s + 1]), 1, 0) for s in range(sections)]
        home = sum(own[s] * s for s in range(sections))
        upper = sum(own[s] * jnp.where(cuts[s] < layer, 1, 0) for s in range(sections))
        alive = sum(own[s] * live[s] for s in range(sections))
        order = sum(own[s] * before[s] for s in range(sections))
        plan_ref[HOME + layer] = home
        plan_ref[UPPER + layer] = upper
        plan_ref[ORDER + layer] = jnp.minimum(order, 1)
        plan_ref[HOME_REL + layer] = home ^ section
        plan_ref[RAISED + layer] = alive * (1 - upper)
    z = pipe & (depth - 1)
    for i, distance in enumerate(DISTANCE):
        plan_ref[BLOCK + i] = (z + distance) & (depth - 1)
    plan_ref[Z] = z
    plan_ref[LOW] = jnp.where(pipe < depth, 0, 1)
    plan_ref[SECTION] = section
    plan_ref[TENSOR] = tensor


def rows_of(tensor_index):
    return (tensor_index & 1) * 8 + (tensor_index >> 1)


def active_kernel(fine, piece, tensors, features, given, plan_ref, *refs):
    own_ref, right_ref, left_ref, far_a_ref, far_b_ref = refs[:5]
    inv_ref = refs[5] if given else None
    out_ref, scratch = refs[-2:]
    half = pl.program_id(0) * 2 < pl.num_programs(0)
    chunks = [
        own_ref[0].astype(f32),
        left_ref[0].astype(f32),
        jnp.where(half, far_a_ref[0].astype(f32), far_b_ref[0].astype(f32)),
        right_ref[0].astype(f32),
    ]
    if given:
        inv = inv_ref[0]
    else:
        total = sum(c[piece : piece + 1] + c[piece + 1 : piece + 2] + c[piece + 2 : piece + 3] for c in chunks)
        inv = lax.rsqrt(total / features + epsilon)
    for away, chunk in enumerate(chunks):
        active = silu(chunk[:piece] * inv)
        base = rows_of((plan_ref[TENSOR] + away) & (tensors - 1)) * fine
        for part in range(piece // fine):
            at = pl.multiple_of(base + part * 2 * fine, 8)
            scratch[pl.ds(at, fine), :] = active[part * fine : (part + 1) * fine]
    out_ref[0] = scratch[...].astype(bf16).reshape(out_ref.shape[1:])


def layers_kernel(fine, piece, tensors, plan_ref, w1_ref, w2_ref, a_ref, c_ref, h_ref, keep_ref, send_ref, h_out_ref, own_ref, d_out_ref, scratch):
    per = piece // fine
    tall = w1_ref.shape[1] * w1_ref.shape[2]
    width, tokens = c_ref.shape[1:]
    active = a_ref[0].reshape(tall, tokens)
    scratch[...] = lax.dot_general(
        w1_ref[0].reshape(tall, width), active, (((0,), (0,)), ((), ())), preferred_element_type=f32
    )
    for away in range(4):
        to = plan_ref[SECTION] ^ away
        parts = [scratch[pl.ds(pl.multiple_of((to + q * per) * fine, 8), fine), :] for q in range(width // piece)]
        block = jnp.concatenate(parts, axis=0)
        if away & 1:
            send_ref[away >> 1, 0] = block.astype(bf16)
        else:
            keep_ref[away >> 1, 0] = block
    h_out_ref[0] = h_ref[0][:piece]
    scratch[...] = jnp.dot(w2_ref[0].reshape(tall, width), c_ref[0], preferred_element_type=f32)
    for away in range(tensors):
        base = rows_of((plan_ref[TENSOR] + away) & (tensors - 1))
        parts = [scratch[pl.ds(pl.multiple_of((base + 2 * q) * fine, 8), fine), :] for q in range(per)]
        block = jnp.concatenate(parts, axis=0)
        if away:
            d_out_ref[away - 1, 0] = block.astype(bf16)
        else:
            own_ref[0] = block


def cotan_kernel(fine, piece, plan_ref, *refs):
    u_refs, h_refs = refs[:4], refs[4:8]
    scale_ref, c_ref, out_ref, scratch = refs[8:]
    scale = scale_ref[0]
    per = 4
    for away in range(4):
        at_section = plan_ref[SECTION] ^ away
        block = u_refs[away][0].astype(f32) - h_refs[away][0].astype(f32) * scale
        for q in range(piece // fine):
            at = pl.multiple_of((q * per + at_section) * fine, 8)
            scratch[pl.ds(at, fine), :] = block[q * fine : (q + 1) * fine]
    out_ref[0] = (c_ref[0].astype(f32) + scratch[...]).astype(bf16)


def block_product(layer, plan_ref, a1_ref, a2_ref, c_ref, g_ref):
    rows = jnp.where(plan_ref[UPPER + layer] == 1, a2_ref[0, 0], a1_ref[0, 0])
    columns = jnp.where(plan_ref[RAISED + layer] == 1, g_ref[0], c_ref[0])
    return lax.dot_general(rows, columns, (((1,), (1,)), ((), ())), preferred_element_type=f32)


def grad_kernel(base, fine, kind, plan_ref, a1_ref, a2_ref, c_ref, g_ref, *refs):
    total = block_product(base + pl.program_id(0), plan_ref, a1_ref, a2_ref, c_ref, g_ref)
    if kind == "upper_half":
        total = total + jnp.concatenate([refs[0][0].astype(f32), jnp.zeros((fine, total.shape[1]), f32)], axis=0)
    elif kind == "lower_half":
        total = total + jnp.concatenate([jnp.zeros((fine, total.shape[1]), f32), refs[0][0].astype(f32)], axis=0)
    elif kind == "add":
        total = total + refs[0][0].astype(f32)
    elif kind == "last":
        total = total + refs[0][0].astype(f32) + refs[1][0].astype(f32)
    if kind == "last":
        keep_ref, send_ref, scratch = refs[2:]
        split_rows(fine, total, plan_ref, keep_ref, send_ref, scratch)
    else:
        refs[-1][0] = total.astype(bf16)


def split_rows(fine, total, plan_ref, keep_ref, send_ref, scratch):
    scratch[...] = total
    low = plan_ref[LOW]
    keep_ref[...] = scratch[pl.ds(pl.multiple_of(low * fine, 8), fine), :].reshape(keep_ref.shape)
    sent = scratch[pl.ds(pl.multiple_of((1 - low) * fine, 8), fine), :]
    send_ref[...] = sent.astype(bf16).reshape(send_ref.shape)


def early_kernel(base, fine, plan_ref, a1_ref, a2_ref, c_ref, g_ref, keep_ref, send_ref, scratch):
    total = block_product(base + pl.program_id(0), plan_ref, a1_ref, a2_ref, c_ref, g_ref)
    split_rows(fine, total, plan_ref, keep_ref, send_ref, scratch)


def shards(section_input, section_cotan, weights, section_cuts, pipe_template):
    pipes = lax.axis_size("pipe")
    sections = lax.axis_size("section")
    tensors = lax.axis_size("tensor")
    layers, stored, width = weights.shape
    tokens = section_input.shape[2]
    features = width * tensors
    fine = stored // sections
    depth = pipes // 2
    tall = pipes * fine
    per_col = pipes // tensors
    piece = per_col * fine
    pipe_idx = lax.axis_index("pipe")
    low_is_zero = pipe_idx < depth
    z_idx = pipe_idx & (depth - 1)
    section_idx = lax.axis_index("section")
    tensor_idx = lax.axis_index("tensor")
    params = pltpu.CompilerParams(vmem_limit_bytes=48 * 1024 * 1024)

    def z_step(array, shift):
        pairs = [(y * depth + z, y * depth + (z + shift) % depth) for y in range(2) for z in range(depth)]
        return lax.ppermute(array, "pipe", pairs)

    def y_swap(array):
        return lax.ppermute(array, "pipe", [(p, (p + depth) % pipes) for p in range(pipes)])

    def x_step(array, shift):
        return lax.ppermute(array, "tensor", [(t, (t + shift) % tensors) for t in range(tensors)])

    def section_swap(array, bits):
        return lax.ppermute(array, "section", [(s, s ^ bits) for s in range(sections)])

    def sum_all(array):
        array = array + x_step(array, 1) + x_step(array, 2) + x_step(array, 3)
        return array + section_swap(array, 1) + section_swap(array, 2) + section_swap(array, 3)

    def gather_x(chunk):
        right, left = x_step(chunk, 1), x_step(chunk, -1)
        half = chunk.shape[0] // 2
        return chunk, right, left, x_step(right[:half], 1), x_step(left[half:], -1)

    def gather_section(chunk):
        other = section_swap(chunk, 2)
        return chunk, section_swap(chunk, 1), other, section_swap(other, 1)

    def grid(steps, ins, outs, scratch=()):
        return pltpu.PrefetchScalarGridSpec(
            num_scalar_prefetch=1, grid=steps, in_specs=ins, out_specs=outs, scratch_shapes=list(scratch)
        )

    with jax.named_scope("plan"):
        me = jnp.stack([pipe_idx, section_idx, tensor_idx]).astype(jnp.int32)
        smem = pl.BlockSpec(memory_space=pltpu.SMEM)
        plan = pl.pallas_call(
            functools.partial(plan_kernel, layers, sections, depth),
            out_shape=jax.ShapeDtypeStruct((PLAN,), jnp.int32),
            in_specs=[smem, smem, smem],
            out_specs=smem,
        )(section_cuts, pipe_template, me)

    with jax.named_scope("spread_inputs"):
        h_cols = section_input[0, 0].T
        h_wide = h_cols.astype(f32)
        squares = jnp.stack(split_three(jnp.sum(h_wide * h_wide, axis=0)))
        extra = jnp.concatenate([squares, jnp.zeros((extra_rows - 3, tokens), bf16)], axis=0)
        blocks = h_cols.reshape(per_col, sections, fine, tokens).transpose(1, 0, 2, 3)
        blocks = blocks.reshape(sections, piece, tokens)
        blocks = jnp.concatenate([blocks, jnp.broadcast_to(extra, (sections, extra_rows, tokens))], axis=1)
        mine = lax.all_to_all(blocks, "section", split_axis=0, concat_axis=0, tiled=True)
        spread = gather_x(mine)
        cotans = jnp.stack(gather_section(section_cotan[0, 0].T))

    split = 4
    shard = lax.dynamic_slice_in_dim(weights, section_idx * fine, fine, 1, allow_negative_indices=False)
    with jax.named_scope("weights_gather"):

        def both(own, other):
            return jnp.where(low_is_zero, jnp.concatenate([own, other], axis=1), jnp.concatenate([other, own], axis=1))

        def place(buffer, chunk, layer, shift):
            at = (z_idx + shift) & (depth - 1)
            return lax.dynamic_update_slice(buffer, chunk[:, None], (layer, at, 0, 0), allow_negative_indices=False)

        pair = both(shard, y_swap(shard))
        matrices = place(jnp.zeros((layers, depth, 2 * fine, width), bf16), pair, 0, 0)
        right = left = pair[:split]
        thin_right = thin_left = shard[split:]
        for k in range(1, depth // 2):
            thin_right, thin_left = z_step(thin_right, 1), z_step(thin_left, -1)
            right, left = z_step(right, 1), z_step(left, -1)
            across = y_swap(jnp.stack([thin_right, thin_left]))
            matrices = place(matrices, right, 0, -k)
            matrices = place(matrices, left, 0, k)
            matrices = place(matrices, both(thin_right, across[0]), split, -k)
            matrices = place(matrices, both(thin_left, across[1]), split, k)
        thin = jnp.concatenate([z_step(thin_right[:1], 1), z_step(thin_left[1:], -1)], axis=0)
        far = jnp.concatenate([z_step(right[: split // 2], 1), z_step(left[split // 2 :], -1)], axis=0)
        matrices = place(matrices, both(thin, y_swap(thin)), split, depth // 2)
        matrices = place(matrices, far, 0, depth // 2)

    def active(chunks, inv):
        count, rows = chunks[0].shape[:2]
        half = count // 2
        block = (1, rows, tokens)
        ins = [pl.BlockSpec(block, lambda i, plan: (i, 0, 0))] * 3
        ins.append(pl.BlockSpec(block, lambda i, plan: (jnp.minimum(i, half - 1), 0, 0)))
        ins.append(pl.BlockSpec(block, lambda i, plan: (jnp.maximum(i - half, 0), 0, 0)))
        given = [] if inv is None else [inv.reshape(count, 1, tokens)]
        ins += [pl.BlockSpec((1, 1, tokens), lambda i, plan: (i, 0, 0)) for _ in given]
        return pl.pallas_call(
            functools.partial(active_kernel, fine, piece, tensors, features, bool(given)),
            out_shape=jax.ShapeDtypeStruct((count, depth, 2 * fine, tokens), bf16),
            grid_spec=grid(
                (count,),
                ins,
                pl.BlockSpec((1, depth, 2 * fine, tokens), lambda i, plan: (i, 0, 0, 0)),
                [pltpu.VMEM((tall, tokens), f32)],
            ),
            compiler_params=params,
            cost_estimate=pl.CostEstimate(flops=0, bytes_accessed=count * tall * tokens * 4, transcendentals=count * tall * tokens),
        )(plan, *chunks, *given)

    with jax.named_scope("first_active"):
        active_first = active(spread, None)

    with jax.named_scope("layer_products"):
        wide = (1, depth, 2 * fine, width)
        cut = (1, piece, tokens)
        keep, send, h_live, back_own, back = pl.pallas_call(
            functools.partial(layers_kernel, fine, piece, tensors),
            out_shape=[
                jax.ShapeDtypeStruct((2, 2, piece, tokens), f32),
                jax.ShapeDtypeStruct((2, 2, piece, tokens), bf16),
                jax.ShapeDtypeStruct((2, piece, tokens), bf16),
                jax.ShapeDtypeStruct((2, piece, tokens), f32),
                jax.ShapeDtypeStruct((tensors - 1, 2, piece, tokens), bf16),
            ],
            grid_spec=grid(
                (2,),
                [
                    pl.BlockSpec(wide, lambda j, plan: (plan[FIRST + j], 0, 0, 0)),
                    pl.BlockSpec(wide, lambda j, plan: (plan[FIRST + j] + 1, 0, 0, 0)),
                    pl.BlockSpec((1, depth, 2 * fine, tokens), lambda j, plan: (plan[LIVE + j], 0, 0, 0)),
                    pl.BlockSpec((1, width, tokens), lambda j, plan: (plan[LIVE_REL + j], 0, 0)),
                    pl.BlockSpec((1, piece + extra_rows, tokens), lambda j, plan: (plan[LIVE + j], 0, 0)),
                ],
                [
                    pl.BlockSpec((2, *cut), lambda j, plan: (0, j, 0, 0)),
                    pl.BlockSpec((2, *cut), lambda j, plan: (0, j, 0, 0)),
                    pl.BlockSpec(cut, lambda j, plan: (j, 0, 0)),
                    pl.BlockSpec(cut, lambda j, plan: (j, 0, 0)),
                    pl.BlockSpec((tensors - 1, *cut), lambda j, plan: (0, j, 0, 0)),
                ],
                [pltpu.VMEM((tall, tokens), f32)],
            ),
            compiler_params=params,
            cost_estimate=pl.CostEstimate(flops=8 * tall * width * tokens, bytes_accessed=4 * tall * width * 2, transcendentals=0),
        )(plan, matrices, matrices, active_first, cotans, mine)

    with jax.named_scope("forward_sum"):
        partial = keep + section_swap(send, 1).astype(f32)
        raised = partial[0] + section_swap(partial[1].astype(bf16), 2).astype(f32)
        h_low = (h_live.astype(f32) + raised).astype(bf16)
    with jax.named_scope("backward_sum"):
        summed = back_own + x_step(back[0], 1).astype(f32) + x_step(back[2], 3).astype(f32) + x_step(back[1], 2).astype(f32)

    h_second = h_low.astype(f32)
    with jax.named_scope("second_norm"):
        inv_second = lax.rsqrt(sum_all(jnp.sum(h_second * h_second, axis=1)) / features + epsilon)
    with jax.named_scope("spread_second"):
        second_chunks = gather_x(h_low)
        h_around = gather_section(h_low)
    inv = inv_second[:, None, :]
    normed = h_second * inv
    gate = jax.nn.sigmoid(normed)
    d_norm = summed * gate * (1.0 + normed * (1.0 - gate))
    with jax.named_scope("spread_cotan"):
        u_around = gather_section((inv * d_norm).astype(bf16))
    with jax.named_scope("mean_term"):
        mean_term = sum_all(jnp.sum(h_second * d_norm, axis=1)) / features
        scale = inv_second * inv_second * inv_second * mean_term
    with jax.named_scope("second_active"):
        active_second = active(second_chunks, inv_second)
    with jax.named_scope("cotan_live"):
        around = pl.BlockSpec((1, piece, tokens), lambda j, plan: (j, 0, 0))
        cotan_live = pl.pallas_call(
            functools.partial(cotan_kernel, fine, piece),
            out_shape=jax.ShapeDtypeStruct((2, width, tokens), bf16),
            grid_spec=grid(
                (2,),
                [around] * 8
                + [
                    pl.BlockSpec((1, 1, tokens), lambda j, plan: (j, 0, 0)),
                    pl.BlockSpec((1, width, tokens), lambda j, plan: (plan[LIVE_REL + j], 0, 0)),
                ],
                pl.BlockSpec((1, width, tokens), lambda j, plan: (j, 0, 0)),
                [pltpu.VMEM((width, tokens), f32)],
            ),
            compiler_params=params,
        )(plan, *u_around, *h_around, scale.reshape(2, 1, tokens), cotans)

    factors = (active_first, active_second, cotans, cotan_live)
    half = layers // 2

    def factor_specs(base, block_of):
        return [
            pl.BlockSpec((1, 1, 2 * fine, tokens), lambda *a: (a[-1][HOME + base + a[0]], block_of(*a), 0, 0)),
            pl.BlockSpec((1, 1, 2 * fine, tokens), lambda *a: (a[-1][ORDER + base + a[0]], block_of(*a), 0, 0)),
            pl.BlockSpec((1, width, tokens), lambda *a: (a[-1][HOME_REL + base + a[0]], 0, 0)),
            pl.BlockSpec((1, width, tokens), lambda *a: (a[-1][ORDER + base + a[0]], 0, 0)),
        ]

    def cost(blocks):
        return pl.CostEstimate(
            flops=blocks * half * 4 * fine * width * tokens, bytes_accessed=half * width * tokens * 4, transcendentals=0
        )

    def grad(kind, distance, *received):
        index = BLOCK + DISTANCE.index(distance % depth)
        low_spec = lambda rows: pl.BlockSpec((1, rows, width), lambda i, plan: (i, 0, 0))
        if kind == "last":
            shapes = [jax.ShapeDtypeStruct((half, fine, width), f32), jax.ShapeDtypeStruct((half, fine, width), bf16)]
            outs, scratch = [low_spec(fine)] * 2, [pltpu.VMEM((2 * fine, width), f32)]
        else:
            shapes, outs, scratch = jax.ShapeDtypeStruct((half, 2 * fine, width), bf16), low_spec(2 * fine), []
        return pl.pallas_call(
            functools.partial(grad_kernel, 0, fine, kind),
            out_shape=shapes,
            grid_spec=grid(
                (half,),
                factor_specs(0, lambda i, plan: plan[index]) + [low_spec(r.shape[1]) for r in received],
                outs,
                scratch,
            ),
            compiler_params=params,
            cost_estimate=cost(1),
        )(plan, *factors, *received)

    def early(start, count):
        spec = pl.BlockSpec((1, 1, fine, width), lambda i, n, plan: (i, n, 0, 0))
        return pl.pallas_call(
            functools.partial(early_kernel, half, fine),
            out_shape=[
                jax.ShapeDtypeStruct((half, count, fine, width), f32),
                jax.ShapeDtypeStruct((half, count, fine, width), bf16),
            ],
            grid_spec=grid(
                (half, count),
                factor_specs(half, lambda i, n, plan: plan[BLOCK + start + n]),
                [spec, spec],
                [pltpu.VMEM((2 * fine, width), f32)],
            ),
            compiler_params=params,
            cost_estimate=cost(count),
        )(plan, *factors)

    with jax.named_scope("grad_sum"):
        keep_a, send_a = early(0, 4)
        swap_a = y_swap(send_a)
        far = grad("plain", 4)
        far_right, far_left = z_step(far[:, :fine], 1), z_step(far[:, fine:], -1)
        keep_b, send_b = early(4, 4)
        swap_b = y_swap(send_b)
        right = z_step(grad("upper_half", 3, far_right), 1)
        left = z_step(grad("lower_half", -3, far_left), -1)
        near_a = keep_a + swap_a.astype(f32)
        up = z_step(near_a[:, 0].astype(bf16), 1)
        down = z_step(near_a[:, 2].astype(bf16), -1)
        right = z_step(grad("add", 2, right), 1)
        left = z_step(grad("add", -2, left), -1)
        near_b = keep_b + swap_b.astype(f32)
        up = z_step((near_a[:, 1] + up.astype(f32)).astype(bf16), 1)
        down = z_step((near_b[:, 0] + down.astype(f32)).astype(bf16), -1)
        right = z_step(grad("add", 1, right), 1)
        left = z_step(grad("add", -1, left), -1)
        up = z_step((near_a[:, 3] + up.astype(f32)).astype(bf16), 1)
        down = z_step((near_b[:, 2] + down.astype(f32)).astype(bf16), -1)
        keep_low, send_low = grad("last", 0, right, left)
        low = keep_low + y_swap(send_low).astype(f32)
        up = z_step((near_b[:, 1] + up.astype(f32)).astype(bf16), 1)
        high = near_b[:, 3] + up.astype(f32) + down.astype(f32)
        return jnp.concatenate([low, high], axis=0)


def solution(mesh):
    in_specs = (
        P("pipe", "section", None, "tensor"),
        P("pipe", "section", None, "tensor"),
        P(None, "pipe", "tensor"),
        P(),
        P(),
    )
    out_specs = P(None, ("pipe", "section"), "tensor")
    return jax.shard_map(shards, mesh=mesh, in_specs=in_specs, out_specs=out_specs, check_vma=False)
```

```python
import functools

import jax
import jax.numpy as jnp
from jax import lax
from jax.experimental import pallas as pl
from jax.experimental.pallas import tpu as pltpu
from jax.sharding import PartitionSpec as P

epsilon = 1e-05
bf16 = jnp.bfloat16
f32 = jnp.float32
extra_rows = 16

FIRST, LIVE, HOME, SELF = 0, 2, 4, 10
Z, LOW, SECTION, TENSOR = SELF, SELF + 1, SELF + 2, SELF + 3
PLAN = 16


def silu(values):
    return values * jax.nn.sigmoid(values)


def split_three(values):
    high = values.astype(bf16)
    rest = values - high.astype(f32)
    middle = rest.astype(bf16)
    low = (rest - middle.astype(f32)).astype(bf16)
    return high, middle, low


def plan_kernel(layers, sections, depth, cuts_ref, template_ref, self_ref, plan_ref):
    pipe, section, tensor = self_ref[0], self_ref[1], self_ref[2]
    template = template_ref[pipe]
    cuts = [cuts_ref[template, s] for s in range(sections + 1)]
    live = [jnp.where(cuts[s + 1] > cuts[s] + 1, 1, 0) for s in range(sections)]
    before = [sum(live[:s], jnp.int32(0)) for s in range(sections)]
    for j in range(2):
        here = [jnp.where((live[s] == 1) & (before[s] == j), 1, 0) for s in range(sections)]
        plan_ref[FIRST + j] = sum(here[s] * cuts[s] for s in range(sections))
        plan_ref[LIVE + j] = sum(here[s] * s for s in range(sections))
    for layer in range(layers):
        own = [jnp.where((cuts[s] <= layer) & (layer < cuts[s + 1]), 1, 0) for s in range(sections)]
        plan_ref[HOME + layer] = sum(own[s] * s for s in range(sections))
    plan_ref[Z] = pipe & (depth - 1)
    plan_ref[LOW] = jnp.where(pipe < depth, 0, 1)
    plan_ref[SECTION] = section
    plan_ref[TENSOR] = tensor


def row_of(plan_ref, tensor_index, part):
    z = (tensor_index & 1) * 4 + part
    return ((z - plan_ref[Z]) & 7) * 2 + ((tensor_index >> 1) ^ plan_ref[LOW])


def spread_rows(fine, piece, plan_ref, tensor_index, values, scratch):
    for part in range(piece // fine):
        at = pl.multiple_of(row_of(plan_ref, tensor_index, part) * fine, 8)
        scratch[pl.ds(at, fine), :] = values[part * fine : (part + 1) * fine]


def early_kernel(fine, piece, tensors, features, plan_ref, rows_ref, c_ref, a_out_ref, c_out_ref, scratch):
    chunks = [rows_ref[t, 0].astype(f32) for t in range(tensors)]
    total = sum(c[piece : piece + 1] + c[piece + 1 : piece + 2] + c[piece + 2 : piece + 3] for c in chunks)
    inv = lax.rsqrt(total / features + epsilon)
    for t, chunk in enumerate(chunks):
        spread_rows(fine, piece, plan_ref, t, silu(chunk[:piece] * inv), scratch)
    a_out_ref[0] = scratch[...].astype(bf16).reshape(a_out_ref.shape[1:])
    c_out_ref[...] = c_ref[...]


def second_kernel(fine, piece, tensors, plan_ref, rows_ref, inv_ref, held_ref, a_out_ref, scratch):
    for t in range(tensors):
        values = rows_ref[t, 0][:piece].astype(f32)
        spread_rows(fine, piece, plan_ref, t, silu(values * inv_ref[0]), scratch)
    a_out_ref[0] = scratch[...].astype(bf16).reshape(a_out_ref.shape[1:])


def layers_kernel(fine, piece, tensors, plan_ref, w1_ref, w2_ref, a_ref, c_ref, h_ref, keep_ref, send_ref, h_out_ref, own_ref, d_out_ref, scratch):
    per = piece // fine
    tall = w1_ref.shape[1] * w1_ref.shape[2]
    width, tokens = c_ref.shape[1:]
    active = a_ref[0].reshape(tall, tokens)
    scratch[...] = lax.dot_general(
        w1_ref[0].reshape(tall, width), active, (((0,), (0,)), ((), ())), preferred_element_type=f32
    )
    for away in range(4):
        to = plan_ref[SECTION] ^ away
        parts = [scratch[pl.ds(pl.multiple_of((to + q * per) * fine, 8), fine), :] for q in range(width // piece)]
        block = jnp.concatenate(parts, axis=0)
        if away & 1:
            send_ref[away >> 1, 0] = block.astype(bf16)
        else:
            keep_ref[away >> 1, 0] = block
    h_out_ref[0] = h_ref[0][:piece]
    scratch[...] = jnp.dot(w2_ref[0].reshape(tall, width), c_ref[0], preferred_element_type=f32)
    for away in range(tensors):
        to = (plan_ref[TENSOR] + away) & (tensors - 1)
        parts = [
            scratch[pl.ds(pl.multiple_of(row_of(plan_ref, to, part) * fine, 8), fine), :] for part in range(per)
        ]
        block = jnp.concatenate(parts, axis=0)
        if away:
            d_out_ref[away - 1, 0] = block.astype(bf16)
        else:
            own_ref[0] = block


def own_cotan_kernel(fine, piece, plan_ref, c_ref, out_ref, scratch):
    per = piece // fine
    scratch[...] = c_ref[0].astype(f32)
    parts = [
        scratch[pl.ds(pl.multiple_of((q * per + plan_ref[SECTION]) * fine, 8), fine), :]
        for q in range(c_ref.shape[1] // piece)
    ]
    out_ref[0] = jnp.concatenate(parts, axis=0)


def cotan_kernel(fine, piece, plan_ref, *refs):
    out_ref, scratch = refs[-2:]
    per = piece // fine
    for away in range(4):
        at_section = plan_ref[SECTION] ^ away
        block = refs[away][0].astype(f32)
        for q in range(per):
            at = pl.multiple_of((q * per + at_section) * fine, 8)
            scratch[pl.ds(at, fine), :] = block[q * fine : (q + 1) * fine]
    out_ref[0] = scratch[...].astype(bf16)


def shards(section_input, section_cotan, weights, section_cuts, pipe_template):
    pipes = lax.axis_size("pipe")
    sections = lax.axis_size("section")
    tensors = lax.axis_size("tensor")
    layers, stored, width = weights.shape
    tokens = section_input.shape[2]
    features = width * tensors
    fine = stored // sections
    depth = pipes // 2
    tall = pipes * fine
    per_col = pipes // tensors
    piece = per_col * fine
    half = layers // 2
    pipe_idx = lax.axis_index("pipe")
    section_idx = lax.axis_index("section")
    tensor_idx = lax.axis_index("tensor")
    params = pltpu.CompilerParams(vmem_limit_bytes=48 * 1024 * 1024)

    def z_step(array, shift):
        pairs = [(y * depth + z, y * depth + (z + shift) % depth) for y in range(2) for z in range(depth)]
        return lax.ppermute(array, "pipe", pairs)

    def y_swap(array):
        return lax.ppermute(array, "pipe", [(p, (p + depth) % pipes) for p in range(pipes)])

    def x_step(array, shift):
        return lax.ppermute(array, "tensor", [(t, (t + shift) % tensors) for t in range(tensors)])

    def section_swap(array, bits):
        return lax.ppermute(array, "section", [(s, s ^ bits) for s in range(sections)])

    def sum_all(array):
        array = array + x_step(array, 1) + x_step(array, 2) + x_step(array, 3)
        array = array + section_swap(array, 1)
        return array + section_swap(array, 2)

    def gather_section(chunk):
        other = section_swap(chunk, 2)
        return chunk, section_swap(chunk, 1), other, section_swap(other, 1)

    def grid(steps, ins, outs, scratch=()):
        return pltpu.PrefetchScalarGridSpec(
            num_scalar_prefetch=1, grid=steps, in_specs=ins, out_specs=outs, scratch_shapes=list(scratch)
        )

    with jax.named_scope("plan"):
        me = jnp.stack([pipe_idx, section_idx, tensor_idx]).astype(jnp.int32)
        smem = pl.BlockSpec(memory_space=pltpu.SMEM)
        plan = pl.pallas_call(
            functools.partial(plan_kernel, layers, sections, depth),
            out_shape=jax.ShapeDtypeStruct((PLAN,), jnp.int32),
            in_specs=[smem, smem, smem],
            out_specs=smem,
        )(section_cuts, pipe_template, me)

    with jax.named_scope("spread_inputs"):
        h_cols = section_input[0, 0].T
        h_wide = h_cols.astype(f32)
        squares = jnp.stack(split_three(jnp.sum(h_wide * h_wide, axis=0)))
        extra = jnp.concatenate([squares, jnp.zeros((extra_rows - 3, tokens), bf16)], axis=0)
        blocks = h_cols.reshape(per_col, sections, fine, tokens).transpose(1, 0, 2, 3)
        blocks = blocks.reshape(sections, piece, tokens)
        blocks = jnp.concatenate([blocks, jnp.broadcast_to(extra, (sections, extra_rows, tokens))], axis=1)
        mine = lax.all_to_all(blocks, "section", split_axis=0, concat_axis=0, tiled=True)
        spread = lax.all_gather(mine, "tensor", axis=0)
        cotans = lax.all_gather(section_cotan[0, 0].T, "section", axis=0)

    shard = lax.dynamic_slice_in_dim(weights, section_idx * fine, fine, 1, allow_negative_indices=False)
    with jax.named_scope("weights_gather"):

        def place(buffer, chunk, layer, away):
            return lax.dynamic_update_slice(buffer, chunk[:, None], (layer, away % depth, 0, 0))

        pair = jnp.concatenate([shard, y_swap(shard)], axis=1)
        matrices = place(jnp.zeros((layers, depth, 2 * fine, width), bf16), pair, 0, 0)
        right = left = pair
        for k in range(1, depth // 2):
            right, left = z_step(right, 1), z_step(left, -1)
            matrices = place(place(matrices, right, 0, -k), left, 0, k)
        far_right, far_left = z_step(right[:half], 1), z_step(left[half:], -1)
        matrices = place(place(matrices, far_right, 0, depth // 2), far_left, half, depth // 2)

    wide = (1, depth, 2 * fine, width)
    rows = (1, depth, 2 * fine, tokens)
    cols = (1, width, tokens)
    cut = (1, piece, tokens)
    with jax.named_scope("early_factors"):
        factor_a, factor_b = pl.pallas_call(
            functools.partial(early_kernel, fine, piece, tensors, features),
            out_shape=[
                jax.ShapeDtypeStruct((layers, depth, 2 * fine, tokens), bf16),
                jax.ShapeDtypeStruct((layers, width, tokens), bf16),
            ],
            grid_spec=grid(
                (layers,),
                [
                    pl.BlockSpec((tensors, 1, piece + extra_rows, tokens), lambda i, plan: (0, plan[HOME + i], 0, 0)),
                    pl.BlockSpec(cols, lambda i, plan: (plan[HOME + i], 0, 0)),
                ],
                [pl.BlockSpec(rows, lambda i, plan: (i, 0, 0, 0)), pl.BlockSpec(cols, lambda i, plan: (i, 0, 0))],
                [pltpu.VMEM((tall, tokens), f32)],
            ),
            compiler_params=params,
        )(plan, spread, cotans)

    with jax.named_scope("layer_products"):
        keep, send, h_live, back_own, back = pl.pallas_call(
            functools.partial(layers_kernel, fine, piece, tensors),
            out_shape=[
                jax.ShapeDtypeStruct((2, 2, piece, tokens), f32),
                jax.ShapeDtypeStruct((2, 2, piece, tokens), bf16),
                jax.ShapeDtypeStruct((2, piece, tokens), bf16),
                jax.ShapeDtypeStruct((2, piece, tokens), f32),
                jax.ShapeDtypeStruct((tensors - 1, 2, piece, tokens), bf16),
            ],
            grid_spec=grid(
                (2,),
                [
                    pl.BlockSpec(wide, lambda j, plan: (plan[FIRST + j], 0, 0, 0)),
                    pl.BlockSpec(wide, lambda j, plan: (plan[FIRST + j] + 1, 0, 0, 0)),
                    pl.BlockSpec(rows, lambda j, plan: (plan[FIRST + j], 0, 0, 0)),
                    pl.BlockSpec(cols, lambda j, plan: (plan[FIRST + j], 0, 0)),
                    pl.BlockSpec((1, piece + extra_rows, tokens), lambda j, plan: (plan[LIVE + j], 0, 0)),
                ],
                [
                    pl.BlockSpec((2, *cut), lambda j, plan: (0, j, 0, 0)),
                    pl.BlockSpec((2, *cut), lambda j, plan: (0, j, 0, 0)),
                    pl.BlockSpec(cut, lambda j, plan: (j, 0, 0)),
                    pl.BlockSpec(cut, lambda j, plan: (j, 0, 0)),
                    pl.BlockSpec((tensors - 1, *cut), lambda j, plan: (0, j, 0, 0)),
                ],
                [pltpu.VMEM((tall, tokens), f32)],
            ),
            compiler_params=params,
            cost_estimate=pl.CostEstimate(flops=8 * tall * width * tokens, bytes_accessed=4 * tall * width * 2, transcendentals=0),
        )(plan, matrices, matrices, factor_a, factor_b, mine)
    with jax.named_scope("own_cotan"):
        own_cotan = pl.pallas_call(
            functools.partial(own_cotan_kernel, fine, piece),
            out_shape=jax.ShapeDtypeStruct((2, piece, tokens), f32),
            grid_spec=grid(
                (2,),
                [pl.BlockSpec(cols, lambda j, plan: (plan[FIRST + j], 0, 0))],
                pl.BlockSpec(cut, lambda j, plan: (j, 0, 0)),
                [pltpu.VMEM((width, tokens), f32)],
            ),
            compiler_params=params,
        )(plan, factor_b)

    with jax.named_scope("forward_sum"):
        partial = keep + section_swap(send, 1).astype(f32)
        raised = partial[0] + section_swap(partial[1].astype(bf16), 2).astype(f32)
        h_low = (h_live.astype(f32) + raised).astype(bf16)
    with jax.named_scope("backward_sum"):
        summed = back_own + x_step(back[0], 1).astype(f32) + x_step(back[2], 3).astype(f32) + x_step(back[1], 2).astype(f32)

    h_second = h_low.astype(f32)
    with jax.named_scope("second_norm"):
        inv_second = lax.rsqrt(sum_all(jnp.sum(h_second * h_second, axis=1)) / features + epsilon)
    with jax.named_scope("spread_second"):
        padded = jnp.concatenate([h_low, jnp.zeros((2, extra_rows, tokens), bf16)], axis=1)
        second_rows = lax.all_gather(padded, "tensor", axis=0)
    inv = inv_second[:, None, :]
    normed = h_second * inv
    gate = jax.nn.sigmoid(normed)
    d_norm = summed * gate * (1.0 + normed * (1.0 - gate))
    with jax.named_scope("mean_term"):
        mean_term = (sum_all(jnp.sum(h_second * d_norm, axis=1)) / features)[:, None, :]
    d_rows = inv * d_norm - h_second * inv * inv * inv * mean_term
    with jax.named_scope("spread_cotan"):
        around = gather_section((own_cotan + d_rows).astype(bf16))
    with jax.named_scope("cotan_live"):
        factor_b = pl.pallas_call(
            functools.partial(cotan_kernel, fine, piece),
            out_shape=jax.ShapeDtypeStruct((layers, width, tokens), bf16),
            grid_spec=grid(
                (2,),
                [pl.BlockSpec(cut, lambda j, plan: (j, 0, 0))] * 4 + [pl.BlockSpec(memory_space=pl.ANY)],
                pl.BlockSpec(cols, lambda j, plan: (plan[FIRST + j], 0, 0)),
                [pltpu.VMEM((width, tokens), f32)],
            ),
            input_output_aliases={5: 0},
            compiler_params=params,
        )(plan, *around, factor_b)
    with jax.named_scope("second_active"):
        factor_a = pl.pallas_call(
            functools.partial(second_kernel, fine, piece, tensors),
            out_shape=jax.ShapeDtypeStruct((layers, depth, 2 * fine, tokens), bf16),
            grid_spec=grid(
                (2,),
                [
                    pl.BlockSpec((tensors, 1, piece + extra_rows, tokens), lambda j, plan: (0, j, 0, 0)),
                    pl.BlockSpec((1, 1, tokens), lambda j, plan: (j, 0, 0)),
                    pl.BlockSpec(memory_space=pl.ANY),
                ],
                pl.BlockSpec(rows, lambda j, plan: (plan[FIRST + j] + 1, 0, 0, 0)),
                [pltpu.VMEM((tall, tokens), f32)],
            ),
            input_output_aliases={3: 0},
            compiler_params=params,
        )(plan, second_rows, inv_second.reshape(2, 1, tokens), factor_a)

    def block_grad(away):
        return lax.dot_general(
            factor_a[:, away % depth], factor_b, (((2,), (2,)), ((0,), (0,))), preferred_element_type=f32
        )

    with jax.named_scope("grad_sum"):
        far = block_grad(depth // 2).astype(bf16)
        right = z_step(far[:half], 1).astype(f32)
        left = z_step(far[half:], -1).astype(f32)
        right = block_grad(depth // 2 - 1) + jnp.concatenate([right, jnp.zeros_like(right)])
        left = block_grad(1 - depth // 2) + jnp.concatenate([jnp.zeros_like(left), left])
        for k in range(depth // 2 - 2, -1, -1):
            right_in = z_step(right.astype(bf16), 1).astype(f32)
            left_in = z_step(left.astype(bf16), -1).astype(f32)
            if k:
                right = block_grad(k) + right_in
                left = block_grad(-k) + left_in
        total = block_grad(0) + right_in + left_in
        return total[:, :fine] + y_swap(total[:, fine:].astype(bf16)).astype(f32)


def solution(mesh):
    in_specs = (
        P("pipe", "section", None, "tensor"),
        P("pipe", "section", None, "tensor"),
        P(None, "pipe", "tensor"),
        P(),
        P(),
    )
    out_specs = P(None, ("pipe", "section"), "tensor")
    return jax.shard_map(shards, mesh=mesh, in_specs=in_specs, out_specs=out_specs, check_vma=False)
```

```python
import functools

import jax
import jax.numpy as jnp
from jax import lax
from jax.experimental import pallas as pl
from jax.experimental.pallas import tpu as pltpu
from jax.sharding import PartitionSpec as P

epsilon = 1e-05
bf16 = jnp.bfloat16
f32 = jnp.float32
extra_rows = 16

FIRST, LIVE, HOME, SELF = 0, 2, 4, 10
Z, LOW, SECTION, TENSOR = SELF, SELF + 1, SELF + 2, SELF + 3
PLAN = 16


def silu(values):
    return values * jax.nn.sigmoid(values)


def split_three(values):
    high = values.astype(bf16)
    rest = values - high.astype(f32)
    middle = rest.astype(bf16)
    low = (rest - middle.astype(f32)).astype(bf16)
    return high, middle, low


def plan_kernel(layers, sections, depth, cuts_ref, template_ref, self_ref, plan_ref):
    pipe, section, tensor = self_ref[0], self_ref[1], self_ref[2]
    template = template_ref[pipe]
    cuts = [cuts_ref[template, s] for s in range(sections + 1)]
    live = [jnp.where(cuts[s + 1] > cuts[s] + 1, 1, 0) for s in range(sections)]
    before = [sum(live[:s], jnp.int32(0)) for s in range(sections)]
    for j in range(2):
        here = [jnp.where((live[s] == 1) & (before[s] == j), 1, 0) for s in range(sections)]
        plan_ref[FIRST + j] = sum(here[s] * cuts[s] for s in range(sections))
        plan_ref[LIVE + j] = sum(here[s] * s for s in range(sections)) ^ section
    for layer in range(layers):
        own = [jnp.where((cuts[s] <= layer) & (layer < cuts[s + 1]), 1, 0) for s in range(sections)]
        plan_ref[HOME + layer] = sum(own[s] * s for s in range(sections)) ^ section
    plan_ref[Z] = pipe & (depth - 1)
    plan_ref[LOW] = jnp.where(pipe < depth, 0, 1)
    plan_ref[SECTION] = section
    plan_ref[TENSOR] = tensor


def row_of(plan_ref, tensor_index, part):
    z = (tensor_index & 1) * 4 + part
    return ((z - plan_ref[Z]) & 7) * 2 + ((tensor_index >> 1) ^ plan_ref[LOW])


def spread_rows(fine, piece, plan_ref, tensor_index, values, scratch):
    for part in range(piece // fine):
        at = pl.multiple_of(row_of(plan_ref, tensor_index, part) * fine, 8)
        scratch[pl.ds(at, fine), :] = values[part * fine : (part + 1) * fine]


def early_kernel(fine, piece, tensors, features, plan_ref, rows_ref, *refs):
    a_out_ref, c_out_ref, scratch = refs[-3:]
    chunks = [rows_ref[t, 0].astype(f32) for t in range(tensors)]
    total = sum(c[piece : piece + 1] + c[piece + 1 : piece + 2] + c[piece + 2 : piece + 3] for c in chunks)
    inv = lax.rsqrt(total / features + epsilon)
    for t, chunk in enumerate(chunks):
        spread_rows(fine, piece, plan_ref, t, silu(chunk[:piece] * inv), scratch)
    a_out_ref[0] = scratch[...].astype(bf16).reshape(a_out_ref.shape[1:])
    distance = plan_ref[HOME + pl.program_id(0)]
    for away in range(4):

        @pl.when(distance == away)
        def _(away=away):
            c_out_ref[0] = refs[away][...]


def second_kernel(fine, piece, tensors, plan_ref, rows_ref, inv_ref, held_ref, a_out_ref, scratch):
    for t in range(tensors):
        values = rows_ref[t, 0][:piece].astype(f32)
        spread_rows(fine, piece, plan_ref, t, silu(values * inv_ref[0]), scratch)
    a_out_ref[0] = scratch[...].astype(bf16).reshape(a_out_ref.shape[1:])


def layers_kernel(fine, piece, tensors, plan_ref, w1_ref, w2_ref, a_ref, c_ref, h_ref, keep_ref, send_ref, h_out_ref, c_out_ref, own_ref, d_out_ref, scratch):
    per = piece // fine
    tall = w1_ref.shape[0] * w1_ref.shape[2]
    width, tokens = c_ref.shape[1:]
    active = a_ref[0].reshape(tall, tokens)
    scratch[...] = lax.dot_general(
        w1_ref[:, 0].reshape(tall, width), active, (((0,), (0,)), ((), ())), preferred_element_type=f32
    )
    for away in range(4):
        to = plan_ref[SECTION] ^ away
        parts = [scratch[pl.ds(pl.multiple_of((to + q * per) * fine, 8), fine), :] for q in range(width // piece)]
        block = jnp.concatenate(parts, axis=0)
        if away & 1:
            send_ref[away >> 1, 0] = block.astype(bf16)
        else:
            keep_ref[away >> 1, 0] = block
    h_out_ref[0] = h_ref[0][:piece]
    scratch[...] = c_ref[0].astype(f32)
    parts = [
        scratch[pl.ds(pl.multiple_of((plan_ref[SECTION] + q * per) * fine, 8), fine), :] for q in range(width // piece)
    ]
    c_out_ref[0] = jnp.concatenate(parts, axis=0)
    scratch[...] = jnp.dot(w2_ref[:, 0].reshape(tall, width), c_ref[0], preferred_element_type=f32)
    for away in range(tensors):
        to = (plan_ref[TENSOR] + away) & (tensors - 1)
        parts = [
            scratch[pl.ds(pl.multiple_of(row_of(plan_ref, to, part) * fine, 8), fine), :] for part in range(per)
        ]
        block = jnp.concatenate(parts, axis=0)
        if away:
            d_out_ref[away - 1, 0] = block.astype(bf16)
        else:
            own_ref[0] = block


def cotan_kernel(fine, piece, plan_ref, *refs):
    out_ref, scratch = refs[-2:]
    per = piece // fine
    for away in range(4):
        at_section = plan_ref[SECTION] ^ away
        block = refs[away][0].astype(f32)
        for q in range(per):
            at = pl.multiple_of((q * per + at_section) * fine, 8)
            scratch[pl.ds(at, fine), :] = block[q * fine : (q + 1) * fine]
    out_ref[0] = scratch[...].astype(bf16)


def shards(section_input, section_cotan, weights, section_cuts, pipe_template):
    pipes = lax.axis_size("pipe")
    sections = lax.axis_size("section")
    tensors = lax.axis_size("tensor")
    layers, stored, width = weights.shape
    tokens = section_input.shape[2]
    features = width * tensors
    fine = stored // sections
    depth = pipes // 2
    tall = pipes * fine
    per_col = pipes // tensors
    piece = per_col * fine
    half = layers // 2
    pipe_idx = lax.axis_index("pipe")
    section_idx = lax.axis_index("section")
    tensor_idx = lax.axis_index("tensor")
    params = pltpu.CompilerParams(vmem_limit_bytes=48 * 1024 * 1024)

    def z_step(array, shift):
        pairs = [(y * depth + z, y * depth + (z + shift) % depth) for y in range(2) for z in range(depth)]
        return lax.ppermute(array, "pipe", pairs)

    def y_swap(array):
        return lax.ppermute(array, "pipe", [(p, (p + depth) % pipes) for p in range(pipes)])

    def x_step(array, shift):
        return lax.ppermute(array, "tensor", [(t, (t + shift) % tensors) for t in range(tensors)])

    def section_swap(array, bits):
        return lax.ppermute(array, "section", [(s, s ^ bits) for s in range(sections)])

    def sum_all(array):
        array = array + x_step(array, 1) + x_step(array, 2) + x_step(array, 3)
        array = array + section_swap(array, 1)
        return array + section_swap(array, 2)

    def gather_section(chunk):
        other = section_swap(chunk, 2)
        return chunk, section_swap(chunk, 1), other, section_swap(other, 1)

    def after(array, other):
        return lax.optimization_barrier((array, other))[0]

    def grid(steps, ins, outs, scratch=()):
        return pltpu.PrefetchScalarGridSpec(
            num_scalar_prefetch=1, grid=steps, in_specs=ins, out_specs=outs, scratch_shapes=list(scratch)
        )

    with jax.named_scope("plan"):
        me = jnp.stack([pipe_idx, section_idx, tensor_idx]).astype(jnp.int32)
        smem = pl.BlockSpec(memory_space=pltpu.SMEM)
        plan = pl.pallas_call(
            functools.partial(plan_kernel, layers, sections, depth),
            out_shape=jax.ShapeDtypeStruct((PLAN,), jnp.int32),
            in_specs=[smem, smem, smem],
            out_specs=smem,
        )(section_cuts, pipe_template, me)

    def place(buffer, chunk, layer, away):
        return lax.dynamic_update_slice(buffer, chunk[None], (away % depth, layer, 0, 0))

    shard = lax.dynamic_slice_in_dim(weights, section_idx * fine, fine, 1, allow_negative_indices=False)
    with jax.named_scope("weights_gather"):
        across = y_swap(shard)
        pair = jnp.concatenate([shard, across], axis=1)
        matrices = place(jnp.zeros((depth, layers, 2 * fine, width), bf16), pair, 0, 0)
        chains = [(pair[:half], pair[:half]), (pair[half:], pair[half:])]
        for k in range(1, depth // 2):
            for c, (right, left) in enumerate(chains):
                right, left = z_step(right, 1), z_step(left, -1)
                chains[c] = right, left
                matrices = place(place(matrices, right, c * half, -k), left, c * half, k)

    with jax.named_scope("spread_inputs"):
        h_cols = section_input[0, 0].T
        h_wide = h_cols.astype(f32)
        squares = jnp.stack(split_three(jnp.sum(h_wide * h_wide, axis=0)))
        extra = jnp.concatenate([squares, jnp.zeros((extra_rows - 3, tokens), bf16)], axis=0)
        blocks = h_cols.reshape(per_col, sections, fine, tokens).transpose(1, 0, 2, 3)
        blocks = blocks.reshape(sections, piece, tokens)
        blocks = jnp.concatenate([blocks, jnp.broadcast_to(extra, (sections, extra_rows, tokens))], axis=1)
        blocks = after(blocks, across)
        block_for = [
            lax.dynamic_index_in_dim(blocks, section_idx ^ bits, 0, keepdims=False, allow_negative_indices=False)
            for bits in range(sections)
        ]
        mine = jnp.stack([block_for[0]] + [section_swap(block_for[bits], bits) for bits in range(1, sections)])
        spread = lax.all_gather(mine, "tensor", axis=0)
        cotans = gather_section(section_cotan[0, 0].T)

    wide = (depth, 1, 2 * fine, width)
    rows = (1, depth, 2 * fine, tokens)
    cols = (1, width, tokens)
    cut = (1, piece, tokens)
    with jax.named_scope("early_factors"):
        factor_a, factor_b = pl.pallas_call(
            functools.partial(early_kernel, fine, piece, tensors, features),
            out_shape=[
                jax.ShapeDtypeStruct((layers, depth, 2 * fine, tokens), bf16),
                jax.ShapeDtypeStruct((layers, width, tokens), bf16),
            ],
            grid_spec=grid(
                (layers,),
                [
                    pl.BlockSpec((tensors, 1, piece + extra_rows, tokens), lambda i, plan: (0, plan[HOME + i], 0, 0)),
                ]
                + [pl.BlockSpec((width, tokens), lambda i, plan: (0, 0))] * 4,
                [pl.BlockSpec(rows, lambda i, plan: (i, 0, 0, 0)), pl.BlockSpec(cols, lambda i, plan: (i, 0, 0))],
                [pltpu.VMEM((tall, tokens), f32)],
            ),
            compiler_params=params,
        )(plan, spread, *cotans)

    with jax.named_scope("weights_gather"):
        far_right = z_step(after(chains[0][0], factor_a), 1)
        far_left = z_step(after(chains[1][1], factor_a), -1)
        matrices = place(place(matrices, far_right, 0, depth // 2), far_left, half, depth // 2)

    with jax.named_scope("layer_products"):
        keep, send, h_live, own_cotan, back_own, back = pl.pallas_call(
            functools.partial(layers_kernel, fine, piece, tensors),
            out_shape=[
                jax.ShapeDtypeStruct((2, 2, piece, tokens), f32),
                jax.ShapeDtypeStruct((2, 2, piece, tokens), bf16),
                jax.ShapeDtypeStruct((2, piece, tokens), bf16),
                jax.ShapeDtypeStruct((2, piece, tokens), f32),
                jax.ShapeDtypeStruct((2, piece, tokens), f32),
                jax.ShapeDtypeStruct((tensors - 1, 2, piece, tokens), bf16),
            ],
            grid_spec=grid(
                (2,),
                [
                    pl.BlockSpec(wide, lambda j, plan: (0, plan[FIRST + j], 0, 0)),
                    pl.BlockSpec(wide, lambda j, plan: (0, plan[FIRST + j] + 1, 0, 0)),
                    pl.BlockSpec(rows, lambda j, plan: (plan[FIRST + j], 0, 0, 0)),
                    pl.BlockSpec(cols, lambda j, plan: (plan[FIRST + j], 0, 0)),
                    pl.BlockSpec((1, piece + extra_rows, tokens), lambda j, plan: (plan[LIVE + j], 0, 0)),
                ],
                [
                    pl.BlockSpec((2, *cut), lambda j, plan: (0, j, 0, 0)),
                    pl.BlockSpec((2, *cut), lambda j, plan: (0, j, 0, 0)),
                    pl.BlockSpec(cut, lambda j, plan: (j, 0, 0)),
                    pl.BlockSpec(cut, lambda j, plan: (j, 0, 0)),
                    pl.BlockSpec(cut, lambda j, plan: (j, 0, 0)),
                    pl.BlockSpec((tensors - 1, *cut), lambda j, plan: (0, j, 0, 0)),
                ],
                [pltpu.VMEM((tall, tokens), f32)],
            ),
            compiler_params=params,
            cost_estimate=pl.CostEstimate(flops=8 * tall * width * tokens, bytes_accessed=4 * tall * width * 2, transcendentals=0),
        )(plan, matrices, matrices, factor_a, factor_b, mine)
    with jax.named_scope("forward_sum"):
        partial = keep + section_swap(send, 1).astype(f32)
        raised = partial[0] + section_swap(partial[1].astype(bf16), 2).astype(f32)
        h_low = (h_live.astype(f32) + raised).astype(bf16)
    with jax.named_scope("backward_sum"):
        summed = back_own + x_step(back[0], 1).astype(f32) + x_step(back[2], 3).astype(f32) + x_step(back[1], 2).astype(f32)

    h_second = h_low.astype(f32)
    with jax.named_scope("second_norm"):
        inv_second = lax.rsqrt(sum_all(after(jnp.sum(h_second * h_second, axis=1), summed)) / features + epsilon)
    with jax.named_scope("spread_second"):
        padded = jnp.concatenate([h_low, jnp.zeros((2, extra_rows, tokens), bf16)], axis=1)
        second_rows = lax.all_gather(padded, "tensor", axis=0)
    inv = inv_second[:, None, :]
    normed = h_second * inv
    gate = jax.nn.sigmoid(normed)
    d_norm = summed * gate * (1.0 + normed * (1.0 - gate))
    with jax.named_scope("mean_term"):
        mean_term = (sum_all(jnp.sum(h_second * d_norm, axis=1)) / features)[:, None, :]
    d_rows = inv * d_norm - h_second * inv * inv * inv * mean_term
    with jax.named_scope("spread_cotan"):
        around = gather_section((own_cotan + d_rows).astype(bf16))
    with jax.named_scope("cotan_live"):
        factor_b = pl.pallas_call(
            functools.partial(cotan_kernel, fine, piece),
            out_shape=jax.ShapeDtypeStruct((layers, width, tokens), bf16),
            grid_spec=grid(
                (2,),
                [pl.BlockSpec(cut, lambda j, plan: (j, 0, 0))] * 4 + [pl.BlockSpec(memory_space=pl.ANY)],
                pl.BlockSpec(cols, lambda j, plan: (plan[FIRST + j], 0, 0)),
                [pltpu.VMEM((width, tokens), f32)],
            ),
            input_output_aliases={5: 0},
            compiler_params=params,
        )(plan, *around, factor_b)
    with jax.named_scope("second_active"):
        factor_a = pl.pallas_call(
            functools.partial(second_kernel, fine, piece, tensors),
            out_shape=jax.ShapeDtypeStruct((layers, depth, 2 * fine, tokens), bf16),
            grid_spec=grid(
                (2,),
                [
                    pl.BlockSpec((tensors, 1, piece + extra_rows, tokens), lambda j, plan: (0, j, 0, 0)),
                    pl.BlockSpec((1, 1, tokens), lambda j, plan: (j, 0, 0)),
                    pl.BlockSpec(memory_space=pl.ANY),
                ],
                pl.BlockSpec(rows, lambda j, plan: (plan[FIRST + j] + 1, 0, 0, 0)),
                [pltpu.VMEM((tall, tokens), f32)],
            ),
            input_output_aliases={3: 0},
            compiler_params=params,
        )(plan, second_rows, inv_second.reshape(2, 1, tokens), factor_a)

    def block_grad(c, away):
        part = slice(c * half, (c + 1) * half)
        return lax.dot_general(
            factor_a[part, away % depth], factor_b[part], (((2,), (2,)), ((0,), (0,))), preferred_element_type=f32
        )

    with jax.named_scope("grad_sum"):
        last = depth // 2
        far = [z_step(block_grad(c, last).astype(bf16), 1 - 2 * c) for c in range(2)]
        chains = [[far[0], None], [None, far[1]]]
        for k in range(last - 1, 0, -1):
            for c in range(2):
                for side in range(2):
                    shift = 1 - 2 * side
                    total = block_grad(c, k * shift)
                    if chains[c][side] is not None:
                        total = total + chains[c][side].astype(f32)
                    chains[c][side] = z_step(total.astype(bf16), shift)
        totals = [block_grad(c, 0) + chains[c][0].astype(f32) + chains[c][1].astype(f32) for c in range(2)]
        swapped = [y_swap(t[:, fine:].astype(bf16)).astype(f32) for t in totals]
        return jnp.concatenate([t[:, :fine] + other for t, other in zip(totals, swapped)])


def solution(mesh):
    in_specs = (
        P("pipe", "section", None, "tensor"),
        P("pipe", "section", None, "tensor"),
        P(None, "pipe", "tensor"),
        P(),
        P(),
    )
    out_specs = P(None, ("pipe", "section"), "tensor")
    return jax.shard_map(shards, mesh=mesh, in_specs=in_specs, out_specs=out_specs, check_vma=False)
```

```python
import functools

import jax
import jax.numpy as jnp
from jax import lax
from jax.experimental import pallas as pl
from jax.experimental.pallas import tpu as pltpu
from jax.sharding import PartitionSpec as P

epsilon = 1e-05
bf16 = jnp.bfloat16
f32 = jnp.float32
extra_rows = 16

FIRST, LIVE, HOME, SELF = 0, 2, 4, 10
Z, LOW, SECTION, TENSOR = SELF, SELF + 1, SELF + 2, SELF + 3
PLAN = 16


def silu(values):
    return values * jax.nn.sigmoid(values)


def split_three(values):
    high = values.astype(bf16)
    rest = values - high.astype(f32)
    middle = rest.astype(bf16)
    low = (rest - middle.astype(f32)).astype(bf16)
    return high, middle, low


def plan_kernel(layers, sections, depth, cuts_ref, template_ref, self_ref, plan_ref):
    pipe, section, tensor = self_ref[0], self_ref[1], self_ref[2]
    template = template_ref[pipe]
    cuts = [cuts_ref[template, s] for s in range(sections + 1)]
    live = [jnp.where(cuts[s + 1] > cuts[s] + 1, 1, 0) for s in range(sections)]
    before = [sum(live[:s], jnp.int32(0)) for s in range(sections)]
    for j in range(2):
        here = [jnp.where((live[s] == 1) & (before[s] == j), 1, 0) for s in range(sections)]
        plan_ref[FIRST + j] = sum(here[s] * cuts[s] for s in range(sections))
        plan_ref[LIVE + j] = sum(here[s] * s for s in range(sections)) ^ section
    for layer in range(layers):
        own = [jnp.where((cuts[s] <= layer) & (layer < cuts[s + 1]), 1, 0) for s in range(sections)]
        plan_ref[HOME + layer] = sum(own[s] * s for s in range(sections)) ^ section
    plan_ref[Z] = pipe & (depth - 1)
    plan_ref[LOW] = jnp.where(pipe < depth, 0, 1)
    plan_ref[SECTION] = section
    plan_ref[TENSOR] = tensor


def row_of(plan_ref, tensor_index, part):
    z = (tensor_index & 1) * 4 + part
    return ((z - plan_ref[Z]) & 7) * 2 + ((tensor_index >> 1) ^ plan_ref[LOW])


def spread_rows(fine, piece, plan_ref, tensor_index, values, scratch):
    for part in range(piece // fine):
        at = pl.multiple_of(row_of(plan_ref, tensor_index, part) * fine, 8)
        scratch[pl.ds(at, fine), :] = values[part * fine : (part + 1) * fine]


def early_kernel(fine, piece, tensors, features, plan_ref, own_ref, left_ref, right_ref, far_a_ref, far_b_ref, c_ref, a_out_ref, c_out_ref, scratch):
    near = plan_ref[HOME + pl.program_id(0)] < 2
    far = jnp.where(near, far_a_ref[0].astype(f32), far_b_ref[0].astype(f32))
    chunks = [own_ref[0].astype(f32), left_ref[0].astype(f32), far, right_ref[0].astype(f32)]
    total = sum(c[piece : piece + 1] + c[piece + 1 : piece + 2] + c[piece + 2 : piece + 3] for c in chunks)
    inv = lax.rsqrt(total / features + epsilon)
    for away, chunk in enumerate(chunks):
        at_tensor = (plan_ref[TENSOR] + away) & (tensors - 1)
        spread_rows(fine, piece, plan_ref, at_tensor, silu(chunk[:piece] * inv), scratch)
    a_out_ref[0] = scratch[...].astype(bf16).reshape(a_out_ref.shape[1:])
    c_out_ref[...] = c_ref[...]


def late_kernel(fine, piece, tensors, plan_ref, *refs):
    piece_refs, rows_ref, inv_ref = refs[:4], refs[4], refs[5]
    a_out_ref, c_out_ref, a_scratch, c_scratch = refs[-4:]
    per = piece // fine
    for away in range(4):
        at_section = plan_ref[SECTION] ^ away
        block = piece_refs[away][0].astype(f32)
        for q in range(per):
            at = pl.multiple_of((q * per + at_section) * fine, 8)
            c_scratch[pl.ds(at, fine), :] = block[q * fine : (q + 1) * fine]
    c_out_ref[0] = c_scratch[...].astype(bf16)
    for t in range(tensors):
        values = rows_ref[t, 0][:piece].astype(f32)
        spread_rows(fine, piece, plan_ref, t, silu(values * inv_ref[0]), a_scratch)
    a_out_ref[0] = a_scratch[...].astype(bf16).reshape(a_out_ref.shape[1:])


def layers_kernel(fine, piece, tensors, plan_ref, w1_ref, w2_ref, a_ref, c_ref, h_ref, keep_ref, send_ref, h_out_ref, c_out_ref, own_ref, d_out_ref, scratch):
    per = piece // fine
    tall = w1_ref.shape[0] * w1_ref.shape[2]
    width, tokens = c_ref.shape[1:]
    active = a_ref[0].reshape(tall, tokens)
    scratch[...] = lax.dot_general(
        w1_ref[:, 0].reshape(tall, width), active, (((0,), (0,)), ((), ())), preferred_element_type=f32
    )
    for away in range(4):
        to = plan_ref[SECTION] ^ away
        parts = [scratch[pl.ds(pl.multiple_of((to + q * per) * fine, 8), fine), :] for q in range(width // piece)]
        block = jnp.concatenate(parts, axis=0)
        if away & 1:
            send_ref[away >> 1, 0] = block.astype(bf16)
        else:
            keep_ref[away >> 1, 0] = block
    h_out_ref[0] = h_ref[0][:piece]
    scratch[...] = c_ref[0].astype(f32)
    parts = [
        scratch[pl.ds(pl.multiple_of((plan_ref[SECTION] + q * per) * fine, 8), fine), :] for q in range(width // piece)
    ]
    c_out_ref[0] = jnp.concatenate(parts, axis=0)
    scratch[...] = jnp.dot(w2_ref[:, 0].reshape(tall, width), c_ref[0], preferred_element_type=f32)
    for away in range(tensors):
        to = (plan_ref[TENSOR] + away) & (tensors - 1)
        parts = [
            scratch[pl.ds(pl.multiple_of(row_of(plan_ref, to, part) * fine, 8), fine), :] for part in range(per)
        ]
        block = jnp.concatenate(parts, axis=0)
        if away:
            d_out_ref[away - 1, 0] = block.astype(bf16)
        else:
            own_ref[0] = block


def shards(section_input, section_cotan, weights, section_cuts, pipe_template):
    pipes = lax.axis_size("pipe")
    sections = lax.axis_size("section")
    tensors = lax.axis_size("tensor")
    layers, stored, width = weights.shape
    tokens = section_input.shape[2]
    features = width * tensors
    fine = stored // sections
    depth = pipes // 2
    tall = pipes * fine
    per_col = pipes // tensors
    piece = per_col * fine
    half = layers // 2
    pipe_idx = lax.axis_index("pipe")
    section_idx = lax.axis_index("section")
    tensor_idx = lax.axis_index("tensor")
    params = pltpu.CompilerParams(vmem_limit_bytes=48 * 1024 * 1024)

    def z_step(array, shift):
        pairs = [(y * depth + z, y * depth + (z + shift) % depth) for y in range(2) for z in range(depth)]
        return lax.ppermute(array, "pipe", pairs)

    def y_swap(array):
        return lax.ppermute(array, "pipe", [(p, (p + depth) % pipes) for p in range(pipes)])

    def x_step(array, shift):
        return lax.ppermute(array, "tensor", [(t, (t + shift) % tensors) for t in range(tensors)])

    def section_swap(array, bits):
        return lax.ppermute(array, "section", [(s, s ^ bits) for s in range(sections)])

    def sum_all(array):
        array = array + x_step(array, 1) + x_step(array, 2) + x_step(array, 3)
        array = array + section_swap(array, 1)
        return array + section_swap(array, 2)

    def gather_section(chunk):
        other = section_swap(chunk, 2)
        return chunk, section_swap(chunk, 1), other, section_swap(other, 1)

    def gather_x(chunk):
        right, left = x_step(chunk, 1), x_step(chunk, -1)
        mid = chunk.shape[0] // 2
        return chunk, left, right, x_step(right[:mid], 1), x_step(left[mid:], -1)

    def after(array, other):
        return lax.optimization_barrier((array, other))[0]

    def grid(steps, ins, outs, scratch=()):
        return pltpu.PrefetchScalarGridSpec(
            num_scalar_prefetch=1, grid=steps, in_specs=ins, out_specs=outs, scratch_shapes=list(scratch)
        )

    with jax.named_scope("plan"):
        me = jnp.stack([pipe_idx, section_idx, tensor_idx]).astype(jnp.int32)
        smem = pl.BlockSpec(memory_space=pltpu.SMEM)
        plan = pl.pallas_call(
            functools.partial(plan_kernel, layers, sections, depth),
            out_shape=jax.ShapeDtypeStruct((PLAN,), jnp.int32),
            in_specs=[smem, smem, smem],
            out_specs=smem,
        )(section_cuts, pipe_template, me)

    def place(buffer, chunk, layer, away):
        return lax.dynamic_update_slice(buffer, chunk[None], (away % depth, layer, 0, 0))

    shard = lax.dynamic_slice_in_dim(weights, section_idx * fine, fine, 1, allow_negative_indices=False)
    with jax.named_scope("weights_gather"):
        across = y_swap(shard)
        pair = jnp.concatenate([shard, across], axis=1)
        matrices = place(jnp.zeros((depth, layers, 2 * fine, width), bf16), pair, 0, 0)
        chains = [(pair[:half], pair[:half]), (pair[half:], pair[half:])]
        for k in range(1, depth // 2 - 1):
            for c, (right, left) in enumerate(chains):
                right, left = z_step(right, 1), z_step(left, -1)
                chains[c] = right, left
                matrices = place(place(matrices, right, c * half, -k), left, c * half, k)

    with jax.named_scope("spread_inputs"):
        h_cols = section_input[0, 0].T
        h_wide = h_cols.astype(f32)
        squares = jnp.stack(split_three(jnp.sum(h_wide * h_wide, axis=0)))
        extra = jnp.concatenate([squares, jnp.zeros((extra_rows - 3, tokens), bf16)], axis=0)
        blocks = h_cols.reshape(per_col, sections, fine, tokens).transpose(1, 0, 2, 3)
        blocks = blocks.reshape(sections, piece, tokens)
        blocks = jnp.concatenate([blocks, jnp.broadcast_to(extra, (sections, extra_rows, tokens))], axis=1)
        block_for = [
            lax.dynamic_index_in_dim(blocks, section_idx ^ bits, 0, keepdims=False, allow_negative_indices=False)
            for bits in range(sections)
        ]
        mine = jnp.stack([block_for[0]] + [section_swap(block_for[bits], bits) for bits in range(1, sections)])
        spread = gather_x(mine)
        cotans = lax.all_gather(section_cotan[0, 0].T, "section", axis=0)

    wide = (depth, 1, 2 * fine, width)
    rows = (1, depth, 2 * fine, tokens)
    cols = (1, width, tokens)
    cut = (1, piece, tokens)
    chunk = (1, piece + extra_rows, tokens)
    with jax.named_scope("early_factors"):
        factor_a, factor_b = pl.pallas_call(
            functools.partial(early_kernel, fine, piece, tensors, features),
            out_shape=[
                jax.ShapeDtypeStruct((layers, depth, 2 * fine, tokens), bf16),
                jax.ShapeDtypeStruct((layers, width, tokens), bf16),
            ],
            grid_spec=grid(
                (layers,),
                [pl.BlockSpec(chunk, lambda i, plan: (plan[HOME + i], 0, 0))] * 3
                + [
                    pl.BlockSpec(chunk, lambda i, plan: (jnp.minimum(plan[HOME + i], 1), 0, 0)),
                    pl.BlockSpec(chunk, lambda i, plan: (jnp.maximum(plan[HOME + i] - 2, 0), 0, 0)),
                    pl.BlockSpec(cols, lambda i, plan: (plan[HOME + i] ^ plan[SECTION], 0, 0)),
                ],
                [pl.BlockSpec(rows, lambda i, plan: (i, 0, 0, 0)), pl.BlockSpec(cols, lambda i, plan: (i, 0, 0))],
                [pltpu.VMEM((tall, tokens), f32)],
            ),
            compiler_params=params,
        )(plan, *spread, cotans)

    with jax.named_scope("weights_gather"):
        k = depth // 2 - 1
        for c, (right, left) in enumerate(chains):
            right, left = z_step(right, 1), z_step(after(left, factor_a) if c else left, -1)
            chains[c] = right, left
            matrices = place(place(matrices, right, c * half, -k), left, c * half, k)
        far_right, far_left = z_step(chains[0][0], 1), z_step(chains[1][1], -1)
        matrices = place(place(matrices, far_right, 0, depth // 2), far_left, half, depth // 2)

    with jax.named_scope("layer_products"):
        keep, send, h_live, own_cotan, back_own, back = pl.pallas_call(
            functools.partial(layers_kernel, fine, piece, tensors),
            out_shape=[
                jax.ShapeDtypeStruct((2, 2, piece, tokens), f32),
                jax.ShapeDtypeStruct((2, 2, piece, tokens), bf16),
                jax.ShapeDtypeStruct((2, piece, tokens), bf16),
                jax.ShapeDtypeStruct((2, piece, tokens), f32),
                jax.ShapeDtypeStruct((2, piece, tokens), f32),
                jax.ShapeDtypeStruct((tensors - 1, 2, piece, tokens), bf16),
            ],
            grid_spec=grid(
                (2,),
                [
                    pl.BlockSpec(wide, lambda j, plan: (0, plan[FIRST + j], 0, 0)),
                    pl.BlockSpec(wide, lambda j, plan: (0, plan[FIRST + j] + 1, 0, 0)),
                    pl.BlockSpec(rows, lambda j, plan: (plan[FIRST + j], 0, 0, 0)),
                    pl.BlockSpec(cols, lambda j, plan: (plan[FIRST + j], 0, 0)),
                    pl.BlockSpec((1, piece + extra_rows, tokens), lambda j, plan: (plan[LIVE + j], 0, 0)),
                ],
                [
                    pl.BlockSpec((2, *cut), lambda j, plan: (0, j, 0, 0)),
                    pl.BlockSpec((2, *cut), lambda j, plan: (0, j, 0, 0)),
                    pl.BlockSpec(cut, lambda j, plan: (j, 0, 0)),
                    pl.BlockSpec(cut, lambda j, plan: (j, 0, 0)),
                    pl.BlockSpec(cut, lambda j, plan: (j, 0, 0)),
                    pl.BlockSpec((tensors - 1, *cut), lambda j, plan: (0, j, 0, 0)),
                ],
                [pltpu.VMEM((tall, tokens), f32)],
            ),
            compiler_params=params,
            cost_estimate=pl.CostEstimate(flops=8 * tall * width * tokens, bytes_accessed=4 * tall * width * 2, transcendentals=0),
        )(plan, matrices, matrices, factor_a, factor_b, mine)
    with jax.named_scope("forward_sum"):
        partial = keep + section_swap(send, 1).astype(f32)
        raised = partial[0] + section_swap(partial[1].astype(bf16), 2).astype(f32)
        h_low = (h_live.astype(f32) + raised).astype(bf16)
    with jax.named_scope("backward_sum"):
        summed = back_own + x_step(back[0], 1).astype(f32) + x_step(back[2], 3).astype(f32) + x_step(back[1], 2).astype(f32)

    h_second = h_low.astype(f32)
    padded = jnp.concatenate([h_low, jnp.zeros((2, extra_rows, tokens), bf16)], axis=1)
    with jax.named_scope("spread_second"):
        second_rows = lax.all_gather(padded, "tensor", axis=0)
    with jax.named_scope("second_norm"):
        squares = after(jnp.sum(h_second * h_second, axis=1), (summed, padded))
        inv_second = lax.rsqrt(sum_all(squares) / features + epsilon)
    inv = inv_second[:, None, :]
    normed = h_second * inv
    gate = jax.nn.sigmoid(normed)
    d_norm = summed * gate * (1.0 + normed * (1.0 - gate))
    with jax.named_scope("mean_term"):
        mean_term = (sum_all(jnp.sum(h_second * d_norm, axis=1)) / features)[:, None, :]
    d_rows = inv * d_norm - h_second * inv * inv * inv * mean_term
    with jax.named_scope("spread_cotan"):
        around = gather_section((own_cotan + d_rows).astype(bf16))
    with jax.named_scope("late_factors"):
        factor_a, factor_b = pl.pallas_call(
            functools.partial(late_kernel, fine, piece, tensors),
            out_shape=[
                jax.ShapeDtypeStruct((layers, depth, 2 * fine, tokens), bf16),
                jax.ShapeDtypeStruct((layers, width, tokens), bf16),
            ],
            grid_spec=grid(
                (2,),
                [pl.BlockSpec(cut, lambda j, plan: (j, 0, 0))] * 4
                + [
                    pl.BlockSpec((tensors, 1, piece + extra_rows, tokens), lambda j, plan: (0, j, 0, 0)),
                    pl.BlockSpec((1, 1, tokens), lambda j, plan: (j, 0, 0)),
                    pl.BlockSpec(memory_space=pl.ANY),
                    pl.BlockSpec(memory_space=pl.ANY),
                ],
                [
                    pl.BlockSpec(rows, lambda j, plan: (plan[FIRST + j] + 1, 0, 0, 0)),
                    pl.BlockSpec(cols, lambda j, plan: (plan[FIRST + j], 0, 0)),
                ],
                [pltpu.VMEM((tall, tokens), f32), pltpu.VMEM((width, tokens), f32)],
            ),
            input_output_aliases={7: 0, 8: 1},
            compiler_params=params,
        )(plan, *around, second_rows, inv_second.reshape(2, 1, tokens), factor_a, factor_b)

    def block_grad(c, away):
        part = slice(c * half, (c + 1) * half)
        return lax.dot_general(
            factor_a[part, away % depth], factor_b[part], (((2,), (2,)), ((0,), (0,))), preferred_element_type=f32
        )

    with jax.named_scope("grad_sum"):
        last = depth // 2
        far = [z_step(block_grad(c, last).astype(bf16), 1 - 2 * c) for c in range(2)]
        chains = [[far[0], None], [None, far[1]]]
        for k in range(last - 1, 0, -1):
            for c in range(2):
                for side in range(2):
                    shift = 1 - 2 * side
                    total = block_grad(c, k * shift)
                    if chains[c][side] is not None:
                        total = total + chains[c][side].astype(f32)
                    chains[c][side] = z_step(total.astype(bf16), shift)
        totals = [block_grad(c, 0) + chains[c][0].astype(f32) + chains[c][1].astype(f32) for c in range(2)]
        swapped = [y_swap(t[:, fine:].astype(bf16)).astype(f32) for t in totals]
        return jnp.concatenate([t[:, :fine] + other for t, other in zip(totals, swapped)])


def solution(mesh):
    in_specs = (
        P("pipe", "section", None, "tensor"),
        P("pipe", "section", None, "tensor"),
        P(None, "pipe", "tensor"),
        P(),
        P(),
    )
    out_specs = P(None, ("pipe", "section"), "tensor")
    return jax.shard_map(shards, mesh=mesh, in_specs=in_specs, out_specs=out_specs, check_vma=False)
```

```python
import functools

import jax
import jax.numpy as jnp
from jax import lax
from jax.experimental import pallas as pl
from jax.experimental.pallas import tpu as pltpu
from jax.sharding import PartitionSpec as P

epsilon = 1e-05
bf16 = jnp.bfloat16
f32 = jnp.float32
extra_rows = 16

FIRST, LIVE, HOME, SELF = 0, 2, 4, 10
Z, LOW, SECTION, TENSOR = SELF, SELF + 1, SELF + 2, SELF + 3
PLAN = 16


def silu(values):
    return values * jax.nn.sigmoid(values)


def split_three(values):
    high = values.astype(bf16)
    rest = values - high.astype(f32)
    middle = rest.astype(bf16)
    low = (rest - middle.astype(f32)).astype(bf16)
    return high, middle, low


def plan_kernel(layers, sections, depth, cuts_ref, template_ref, self_ref, plan_ref):
    pipe, section, tensor = self_ref[0], self_ref[1], self_ref[2]
    template = template_ref[pipe]
    cuts = [cuts_ref[template, s] for s in range(sections + 1)]
    live = [jnp.where(cuts[s + 1] > cuts[s] + 1, 1, 0) for s in range(sections)]
    before = [sum(live[:s], jnp.int32(0)) for s in range(sections)]
    for j in range(2):
        here = [jnp.where((live[s] == 1) & (before[s] == j), 1, 0) for s in range(sections)]
        plan_ref[FIRST + j] = sum(here[s] * cuts[s] for s in range(sections))
        plan_ref[LIVE + j] = sum(here[s] * s for s in range(sections)) ^ section
    for layer in range(layers):
        own = [jnp.where((cuts[s] <= layer) & (layer < cuts[s + 1]), 1, 0) for s in range(sections)]
        plan_ref[HOME + layer] = sum(own[s] * s for s in range(sections)) ^ section
    plan_ref[Z] = pipe & (depth - 1)
    plan_ref[LOW] = jnp.where(pipe < depth, 0, 1)
    plan_ref[SECTION] = section
    plan_ref[TENSOR] = tensor


def row_of(plan_ref, tensor_index, part):
    z = (tensor_index & 1) * 4 + part
    return ((z - plan_ref[Z]) & 7) * 2 + ((tensor_index >> 1) ^ plan_ref[LOW])


def spread_rows(fine, piece, plan_ref, tensor_index, values, scratch):
    for part in range(piece // fine):
        at = pl.multiple_of(row_of(plan_ref, tensor_index, part) * fine, 8)
        scratch[pl.ds(at, fine), :] = values[part * fine : (part + 1) * fine]


def early_kernel(fine, piece, tensors, features, plan_ref, rows_ref, *refs):
    a_out_ref, c_out_ref, scratch = refs[-3:]
    chunks = [rows_ref[t, 0].astype(f32) for t in range(tensors)]
    total = sum(c[piece : piece + 1] + c[piece + 1 : piece + 2] + c[piece + 2 : piece + 3] for c in chunks)
    inv = lax.rsqrt(total / features + epsilon)
    for t, chunk in enumerate(chunks):
        spread_rows(fine, piece, plan_ref, t, silu(chunk[:piece] * inv), scratch)
    a_out_ref[0] = scratch[...].astype(bf16).reshape(a_out_ref.shape[1:])
    distance = plan_ref[HOME + pl.program_id(0)]
    for away in range(4):

        @pl.when(distance == away)
        def _(away=away):
            c_out_ref[0] = refs[away][...]


def late_kernel(fine, piece, tensors, plan_ref, *refs):
    piece_refs, rows_ref, inv_ref = refs[:4], refs[4], refs[5]
    a_out_ref, c_out_ref, a_scratch, c_scratch = refs[-4:]
    per = piece // fine
    for away in range(4):
        at_section = plan_ref[SECTION] ^ away
        block = piece_refs[away][0].astype(f32)
        for q in range(per):
            at = pl.multiple_of((q * per + at_section) * fine, 8)
            c_scratch[pl.ds(at, fine), :] = block[q * fine : (q + 1) * fine]
    c_out_ref[0] = c_scratch[...].astype(bf16)
    for t in range(tensors):
        values = rows_ref[t, 0][:piece].astype(f32)
        spread_rows(fine, piece, plan_ref, t, silu(values * inv_ref[0]), a_scratch)
    a_out_ref[0] = a_scratch[...].astype(bf16).reshape(a_out_ref.shape[1:])


def layers_kernel(fine, piece, tensors, plan_ref, w1_ref, w2_ref, a_ref, c_ref, h_ref, keep_ref, send_ref, h_out_ref, c_out_ref, own_ref, d_out_ref, scratch):
    per = piece // fine
    tall = w1_ref.shape[0] * w1_ref.shape[2]
    width, tokens = c_ref.shape[1:]
    active = a_ref[0].reshape(tall, tokens)
    scratch[...] = lax.dot_general(
        w1_ref[:, 0].reshape(tall, width), active, (((0,), (0,)), ((), ())), preferred_element_type=f32
    )
    for away in range(4):
        to = plan_ref[SECTION] ^ away
        parts = [scratch[pl.ds(pl.multiple_of((to + q * per) * fine, 8), fine), :] for q in range(width // piece)]
        block = jnp.concatenate(parts, axis=0)
        if away & 1:
            send_ref[away >> 1, 0] = block.astype(bf16)
        else:
            keep_ref[away >> 1, 0] = block
    h_out_ref[0] = h_ref[0][:piece]
    scratch[...] = c_ref[0].astype(f32)
    parts = [
        scratch[pl.ds(pl.multiple_of((plan_ref[SECTION] + q * per) * fine, 8), fine), :] for q in range(width // piece)
    ]
    c_out_ref[0] = jnp.concatenate(parts, axis=0)
    scratch[...] = jnp.dot(w2_ref[:, 0].reshape(tall, width), c_ref[0], preferred_element_type=f32)
    for away in range(tensors):
        to = (plan_ref[TENSOR] + away) & (tensors - 1)
        parts = [
            scratch[pl.ds(pl.multiple_of(row_of(plan_ref, to, part) * fine, 8), fine), :] for part in range(per)
        ]
        block = jnp.concatenate(parts, axis=0)
        if away:
            d_out_ref[away - 1, 0] = block.astype(bf16)
        else:
            own_ref[0] = block


def shards(section_input, section_cotan, weights, section_cuts, pipe_template):
    pipes = lax.axis_size("pipe")
    sections = lax.axis_size("section")
    tensors = lax.axis_size("tensor")
    layers, stored, width = weights.shape
    tokens = section_input.shape[2]
    features = width * tensors
    fine = stored // sections
    depth = pipes // 2
    tall = pipes * fine
    per_col = pipes // tensors
    piece = per_col * fine
    half = layers // 2
    pipe_idx = lax.axis_index("pipe")
    section_idx = lax.axis_index("section")
    tensor_idx = lax.axis_index("tensor")
    params = pltpu.CompilerParams(vmem_limit_bytes=48 * 1024 * 1024)

    def z_step(array, shift):
        pairs = [(y * depth + z, y * depth + (z + shift) % depth) for y in range(2) for z in range(depth)]
        return lax.ppermute(array, "pipe", pairs)

    def y_swap(array):
        return lax.ppermute(array, "pipe", [(p, (p + depth) % pipes) for p in range(pipes)])

    def x_step(array, shift):
        return lax.ppermute(array, "tensor", [(t, (t + shift) % tensors) for t in range(tensors)])

    def section_swap(array, bits):
        return lax.ppermute(array, "section", [(s, s ^ bits) for s in range(sections)])

    def sum_all(array):
        array = array + x_step(array, 1) + x_step(array, 2) + x_step(array, 3)
        array = array + section_swap(array, 1)
        return array + section_swap(array, 2)

    def gather_section(chunk):
        other = section_swap(chunk, 2)
        return chunk, section_swap(chunk, 1), other, section_swap(other, 1)

    def after(array, other):
        return lax.optimization_barrier((array, other))[0]

    def grid(steps, ins, outs, scratch=()):
        return pltpu.PrefetchScalarGridSpec(
            num_scalar_prefetch=1, grid=steps, in_specs=ins, out_specs=outs, scratch_shapes=list(scratch)
        )

    with jax.named_scope("plan"):
        me = jnp.stack([pipe_idx, section_idx, tensor_idx]).astype(jnp.int32)
        smem = pl.BlockSpec(memory_space=pltpu.SMEM)
        plan = pl.pallas_call(
            functools.partial(plan_kernel, layers, sections, depth),
            out_shape=jax.ShapeDtypeStruct((PLAN,), jnp.int32),
            in_specs=[smem, smem, smem],
            out_specs=smem,
        )(section_cuts, pipe_template, me)

    def place(buffer, chunk, low, away):
        return lax.dynamic_update_slice(buffer, chunk[None], (away % depth, 0, low * fine, 0))

    shard = lax.dynamic_slice_in_dim(weights, section_idx * fine, fine, 1, allow_negative_indices=False)
    with jax.named_scope("weights_gather"):
        across = y_swap(shard)
        matrices = jnp.zeros((depth, layers, 2 * fine, width), bf16)
        chains = [(shard, shard), (across, across)]
        for low, (chunk, _) in enumerate(chains):
            matrices = place(matrices, chunk, low, 0)
        for k in range(1, depth // 2):
            for low, (right, left) in enumerate(chains):
                right, left = z_step(right, 1), z_step(left, -1)
                chains[low] = right, left
                matrices = place(place(matrices, right, low, -k), left, low, k)
            if k == 1:
                ring_runs = chains[0][0]
        far_right, far_left = z_step(chains[0][0], 1), z_step(chains[1][1], -1)
        matrices = place(place(matrices, far_right, 0, depth // 2), far_left, 1, depth // 2)

    with jax.named_scope("spread_inputs"):
        h_cols = section_input[0, 0].T
        h_wide = h_cols.astype(f32)
        squares = jnp.stack(split_three(jnp.sum(h_wide * h_wide, axis=0)))
        extra = jnp.concatenate([squares, jnp.zeros((extra_rows - 3, tokens), bf16)], axis=0)
        blocks = h_cols.reshape(per_col, sections, fine, tokens).transpose(1, 0, 2, 3)
        blocks = blocks.reshape(sections, piece, tokens)
        blocks = jnp.concatenate([blocks, jnp.broadcast_to(extra, (sections, extra_rows, tokens))], axis=1)
        blocks = after(blocks, across)
        block_for = [
            lax.dynamic_index_in_dim(blocks, section_idx ^ bits, 0, keepdims=False, allow_negative_indices=False)
            for bits in range(sections)
        ]
        mine = jnp.stack([block_for[0]] + [section_swap(block_for[bits], bits) for bits in range(1, sections)])
        spread = lax.all_gather(mine, "tensor", axis=0)
        cotans = gather_section(after(section_cotan, ring_runs)[0, 0].T)

    wide = (depth, 1, 2 * fine, width)
    rows = (1, depth, 2 * fine, tokens)
    cols = (1, width, tokens)
    cut = (1, piece, tokens)
    with jax.named_scope("early_factors"):
        factor_a, factor_b = pl.pallas_call(
            functools.partial(early_kernel, fine, piece, tensors, features),
            out_shape=[
                jax.ShapeDtypeStruct((layers, depth, 2 * fine, tokens), bf16),
                jax.ShapeDtypeStruct((layers, width, tokens), bf16),
            ],
            grid_spec=grid(
                (layers,),
                [
                    pl.BlockSpec((tensors, 1, piece + extra_rows, tokens), lambda i, plan: (0, plan[HOME + i], 0, 0)),
                ]
                + [pl.BlockSpec((width, tokens), lambda i, plan: (0, 0))] * 4,
                [pl.BlockSpec(rows, lambda i, plan: (i, 0, 0, 0)), pl.BlockSpec(cols, lambda i, plan: (i, 0, 0))],
                [pltpu.VMEM((tall, tokens), f32)],
            ),
            compiler_params=params,
        )(plan, spread, *cotans)

    with jax.named_scope("layer_products"):
        keep, send, h_live, own_cotan, back_own, back = pl.pallas_call(
            functools.partial(layers_kernel, fine, piece, tensors),
            out_shape=[
                jax.ShapeDtypeStruct((2, 2, piece, tokens), f32),
                jax.ShapeDtypeStruct((2, 2, piece, tokens), bf16),
                jax.ShapeDtypeStruct((2, piece, tokens), bf16),
                jax.ShapeDtypeStruct((2, piece, tokens), f32),
                jax.ShapeDtypeStruct((2, piece, tokens), f32),
                jax.ShapeDtypeStruct((tensors - 1, 2, piece, tokens), bf16),
            ],
            grid_spec=grid(
                (2,),
                [
                    pl.BlockSpec(wide, lambda j, plan: (0, plan[FIRST + j], 0, 0)),
                    pl.BlockSpec(wide, lambda j, plan: (0, plan[FIRST + j] + 1, 0, 0)),
                    pl.BlockSpec(rows, lambda j, plan: (plan[FIRST + j], 0, 0, 0)),
                    pl.BlockSpec(cols, lambda j, plan: (plan[FIRST + j], 0, 0)),
                    pl.BlockSpec((1, piece + extra_rows, tokens), lambda j, plan: (plan[LIVE + j], 0, 0)),
                ],
                [
                    pl.BlockSpec((2, *cut), lambda j, plan: (0, j, 0, 0)),
                    pl.BlockSpec((2, *cut), lambda j, plan: (0, j, 0, 0)),
                    pl.BlockSpec(cut, lambda j, plan: (j, 0, 0)),
                    pl.BlockSpec(cut, lambda j, plan: (j, 0, 0)),
                    pl.BlockSpec(cut, lambda j, plan: (j, 0, 0)),
                    pl.BlockSpec((tensors - 1, *cut), lambda j, plan: (0, j, 0, 0)),
                ],
                [pltpu.VMEM((tall, tokens), f32)],
            ),
            compiler_params=params,
            cost_estimate=pl.CostEstimate(flops=8 * tall * width * tokens, bytes_accessed=4 * tall * width * 2, transcendentals=0),
        )(plan, matrices, matrices, factor_a, factor_b, mine)
    with jax.named_scope("forward_sum"):
        partial = keep + section_swap(send, 1).astype(f32)
        raised = partial[0] + section_swap(partial[1].astype(bf16), 2).astype(f32)
        h_low = (h_live.astype(f32) + raised).astype(bf16)
    with jax.named_scope("backward_sum"):
        summed = back_own + x_step(back[0], 1).astype(f32) + x_step(back[2], 3).astype(f32) + x_step(back[1], 2).astype(f32)

    h_second = h_low.astype(f32)
    padded = jnp.concatenate([h_low, jnp.zeros((2, extra_rows, tokens), bf16)], axis=1)
    with jax.named_scope("spread_second"):
        second_rows = lax.all_gather(padded, "tensor", axis=0)
    with jax.named_scope("second_norm"):
        squares = after(jnp.sum(h_second * h_second, axis=1), (summed, padded))
        inv_second = lax.rsqrt(sum_all(squares) / features + epsilon)
    inv = inv_second[:, None, :]
    normed = h_second * inv
    gate = jax.nn.sigmoid(normed)
    d_norm = summed * gate * (1.0 + normed * (1.0 - gate))
    with jax.named_scope("mean_term"):
        mean_term = (sum_all(jnp.sum(h_second * d_norm, axis=1)) / features)[:, None, :]
    d_rows = inv * d_norm - h_second * inv * inv * inv * mean_term
    with jax.named_scope("spread_cotan"):
        around = gather_section((own_cotan + d_rows).astype(bf16))
    with jax.named_scope("late_factors"):
        factor_a, factor_b = pl.pallas_call(
            functools.partial(late_kernel, fine, piece, tensors),
            out_shape=[
                jax.ShapeDtypeStruct((layers, depth, 2 * fine, tokens), bf16),
                jax.ShapeDtypeStruct((layers, width, tokens), bf16),
            ],
            grid_spec=grid(
                (2,),
                [pl.BlockSpec(cut, lambda j, plan: (j, 0, 0))] * 4
                + [
                    pl.BlockSpec((tensors, 1, piece + extra_rows, tokens), lambda j, plan: (0, j, 0, 0)),
                    pl.BlockSpec((1, 1, tokens), lambda j, plan: (j, 0, 0)),
                    pl.BlockSpec(memory_space=pl.ANY),
                    pl.BlockSpec(memory_space=pl.ANY),
                ],
                [
                    pl.BlockSpec(rows, lambda j, plan: (plan[FIRST + j] + 1, 0, 0, 0)),
                    pl.BlockSpec(cols, lambda j, plan: (plan[FIRST + j], 0, 0)),
                ],
                [pltpu.VMEM((tall, tokens), f32), pltpu.VMEM((width, tokens), f32)],
            ),
            input_output_aliases={7: 0, 8: 1},
            compiler_params=params,
        )(plan, *around, second_rows, inv_second.reshape(2, 1, tokens), factor_a, factor_b)

    def block_grad(c, away):
        part = slice(c * half, (c + 1) * half)
        return lax.dot_general(
            factor_a[part, away % depth], factor_b[part], (((2,), (2,)), ((0,), (0,))), preferred_element_type=f32
        )

    with jax.named_scope("grad_sum"):
        last = depth // 2
        far = [z_step(block_grad(c, last).astype(bf16), 1 - 2 * c) for c in range(2)]
        chains = [[far[0], None], [None, far[1]]]
        for k in range(last - 1, 0, -1):
            for c in range(2):
                for side in range(2):
                    shift = 1 - 2 * side
                    total = block_grad(c, k * shift)
                    if chains[c][side] is not None:
                        total = total + chains[c][side].astype(f32)
                    chains[c][side] = z_step(total.astype(bf16), shift)
        totals = [block_grad(c, 0) + chains[c][0].astype(f32) + chains[c][1].astype(f32) for c in range(2)]
        swapped = [y_swap(t[:, fine:].astype(bf16)).astype(f32) for t in totals]
        return jnp.concatenate([t[:, :fine] + other for t, other in zip(totals, swapped)])


def solution(mesh):
    in_specs = (
        P("pipe", "section", None, "tensor"),
        P("pipe", "section", None, "tensor"),
        P(None, "pipe", "tensor"),
        P(),
        P(),
    )
    out_specs = P(None, ("pipe", "section"), "tensor")
    return jax.shard_map(shards, mesh=mesh, in_specs=in_specs, out_specs=out_specs, check_vma=False)
```

```python
import functools

import jax
import jax.numpy as jnp
from jax import lax
from jax.experimental import pallas as pl
from jax.experimental.pallas import tpu as pltpu
from jax.sharding import PartitionSpec as P

epsilon = 1e-05
bf16 = jnp.bfloat16
f32 = jnp.float32
extra_rows = 16

FIRST, LIVE, HOME, SELF = 0, 2, 4, 10
Z, LOW, SECTION, TENSOR = SELF, SELF + 1, SELF + 2, SELF + 3
PLAN = 16


def silu(values):
    return values * jax.nn.sigmoid(values)


def split_three(values):
    high = values.astype(bf16)
    rest = values - high.astype(f32)
    middle = rest.astype(bf16)
    low = (rest - middle.astype(f32)).astype(bf16)
    return high, middle, low


def plan_kernel(layers, sections, depth, cuts_ref, template_ref, self_ref, plan_ref):
    pipe, section, tensor = self_ref[0], self_ref[1], self_ref[2]
    template = template_ref[pipe]
    cuts = [cuts_ref[template, s] for s in range(sections + 1)]
    live = [jnp.where(cuts[s + 1] > cuts[s] + 1, 1, 0) for s in range(sections)]
    before = [sum(live[:s], jnp.int32(0)) for s in range(sections)]
    for j in range(2):
        here = [jnp.where((live[s] == 1) & (before[s] == j), 1, 0) for s in range(sections)]
        plan_ref[FIRST + j] = sum(here[s] * cuts[s] for s in range(sections))
        plan_ref[LIVE + j] = sum(here[s] * s for s in range(sections)) ^ section
    for layer in range(layers):
        own = [jnp.where((cuts[s] <= layer) & (layer < cuts[s + 1]), 1, 0) for s in range(sections)]
        plan_ref[HOME + layer] = sum(own[s] * s for s in range(sections)) ^ section
    plan_ref[Z] = pipe & (depth - 1)
    plan_ref[LOW] = jnp.where(pipe < depth, 0, 1)
    plan_ref[SECTION] = section
    plan_ref[TENSOR] = tensor


def row_of(plan_ref, tensor_index, part):
    z = (tensor_index & 1) * 4 + part
    return ((z - plan_ref[Z]) & 7) * 2 + ((tensor_index >> 1) ^ plan_ref[LOW])


def spread_rows(fine, piece, plan_ref, tensor_index, values, scratch):
    for part in range(piece // fine):
        at = pl.multiple_of(row_of(plan_ref, tensor_index, part) * fine, 8)
        scratch[pl.ds(at, fine), :] = values[part * fine : (part + 1) * fine]


def early_kernel(fine, piece, tensors, features, plan_ref, *refs):
    row_refs, cotan_refs, (a_out_ref, c_out_ref, scratch) = refs[:4], refs[4:8], refs[8:]
    chunks = [ref[0].astype(f32) for ref in row_refs]
    total = sum(c[piece : piece + 1] + c[piece + 1 : piece + 2] + c[piece + 2 : piece + 3] for c in chunks)
    inv = lax.rsqrt(total / features + epsilon)
    for away, chunk in enumerate(chunks):
        at_tensor = (plan_ref[TENSOR] + away) & (tensors - 1)
        spread_rows(fine, piece, plan_ref, at_tensor, silu(chunk[:piece] * inv), scratch)
    a_out_ref[0] = scratch[...].astype(bf16).reshape(a_out_ref.shape[1:])
    distance = plan_ref[HOME + pl.program_id(0)]
    for away in range(4):

        @pl.when(distance == away)
        def _(away=away):
            c_out_ref[...] = cotan_refs[away][...]


def late_kernel(fine, piece, tensors, plan_ref, *refs):
    piece_refs, row_refs, inv_ref = refs[:4], refs[4:8], refs[8]
    a_out_ref, c_out_ref, a_scratch, c_scratch = refs[-4:]
    per = piece // fine
    for away in range(4):
        at_section = plan_ref[SECTION] ^ away
        block = piece_refs[away][0].astype(f32)
        for q in range(per):
            at = pl.multiple_of((q * per + at_section) * fine, 8)
            c_scratch[pl.ds(at, fine), :] = block[q * fine : (q + 1) * fine]
    c_out_ref[0] = c_scratch[...].astype(bf16)
    for away in range(tensors):
        values = row_refs[away][0].astype(f32)
        spread_rows(fine, piece, plan_ref, plan_ref[TENSOR] ^ away, silu(values * inv_ref[0]), a_scratch)
    a_out_ref[0] = a_scratch[...].astype(bf16).reshape(a_out_ref.shape[1:])


def layers_kernel(fine, piece, tensors, plan_ref, w1_ref, w2_ref, a_ref, c_ref, h_ref, keep_ref, send_ref, h_out_ref, c_out_ref, own_ref, d_out_ref, scratch):
    per = piece // fine
    tall = w1_ref.shape[0] * w1_ref.shape[2]
    width, tokens = c_ref.shape[1:]
    active = a_ref[0].reshape(tall, tokens)
    scratch[...] = lax.dot_general(
        w1_ref[:, 0].reshape(tall, width), active, (((0,), (0,)), ((), ())), preferred_element_type=f32
    )
    for away in range(4):
        to = plan_ref[SECTION] ^ away
        parts = [scratch[pl.ds(pl.multiple_of((to + q * per) * fine, 8), fine), :] for q in range(width // piece)]
        block = jnp.concatenate(parts, axis=0)
        if away & 1:
            send_ref[away >> 1, 0] = block.astype(bf16)
        else:
            keep_ref[away >> 1, 0] = block
    h_out_ref[0] = h_ref[0][:piece]
    scratch[...] = c_ref[0].astype(f32)
    parts = [
        scratch[pl.ds(pl.multiple_of((plan_ref[SECTION] + q * per) * fine, 8), fine), :] for q in range(width // piece)
    ]
    c_out_ref[0] = jnp.concatenate(parts, axis=0)
    scratch[...] = jnp.dot(w2_ref[:, 0].reshape(tall, width), c_ref[0], preferred_element_type=f32)
    for away in range(tensors):
        to = (plan_ref[TENSOR] + away) & (tensors - 1)
        parts = [
            scratch[pl.ds(pl.multiple_of(row_of(plan_ref, to, part) * fine, 8), fine), :] for part in range(per)
        ]
        block = jnp.concatenate(parts, axis=0)
        if away:
            d_out_ref[away - 1, 0] = block.astype(bf16)
        else:
            own_ref[0] = block


def shards(section_input, section_cotan, weights, section_cuts, pipe_template):
    pipes = lax.axis_size("pipe")
    sections = lax.axis_size("section")
    tensors = lax.axis_size("tensor")
    layers, stored, width = weights.shape
    tokens = section_input.shape[2]
    features = width * tensors
    fine = stored // sections
    depth = pipes // 2
    tall = pipes * fine
    per_col = pipes // tensors
    piece = per_col * fine
    half = layers // 2
    pipe_idx = lax.axis_index("pipe")
    section_idx = lax.axis_index("section")
    tensor_idx = lax.axis_index("tensor")
    params = pltpu.CompilerParams(vmem_limit_bytes=48 * 1024 * 1024)

    def z_step(array, shift):
        pairs = [(y * depth + z, y * depth + (z + shift) % depth) for y in range(2) for z in range(depth)]
        return lax.ppermute(array, "pipe", pairs)

    def y_swap(array):
        return lax.ppermute(array, "pipe", [(p, (p + depth) % pipes) for p in range(pipes)])

    def x_step(array, shift):
        return lax.ppermute(array, "tensor", [(t, (t + shift) % tensors) for t in range(tensors)])

    def section_swap(array, bits):
        return lax.ppermute(array, "section", [(s, s ^ bits) for s in range(sections)])

    def x_swap(array, bits):
        return lax.ppermute(array, "tensor", [(t, t ^ bits) for t in range(tensors)])

    def sum_all(array):
        for swap, bits in ((x_swap, 1), (x_swap, 2), (section_swap, 1), (section_swap, 2)):
            array = array + swap(array, bits)
        return array

    def gather_section(chunk):
        other = section_swap(chunk, 2)
        return chunk, section_swap(jnp.concatenate([chunk, other]), 1), other

    def after(array, other):
        return lax.optimization_barrier((array, other))[0]

    def grid(steps, ins, outs, scratch=()):
        return pltpu.PrefetchScalarGridSpec(
            num_scalar_prefetch=1, grid=steps, in_specs=ins, out_specs=outs, scratch_shapes=list(scratch)
        )

    with jax.named_scope("plan"):
        me = jnp.stack([pipe_idx, section_idx, tensor_idx]).astype(jnp.int32)
        smem = pl.BlockSpec(memory_space=pltpu.SMEM)
        plan = pl.pallas_call(
            functools.partial(plan_kernel, layers, sections, depth),
            out_shape=jax.ShapeDtypeStruct((PLAN,), jnp.int32),
            in_specs=[smem, smem, smem],
            out_specs=smem,
        )(section_cuts, pipe_template, me)

    def place(buffer, chunk, layer, away):
        return lax.dynamic_update_slice(buffer, chunk[None], (away % depth, layer, 0, 0))

    shard = lax.dynamic_slice_in_dim(weights, section_idx * fine, fine, 1, allow_negative_indices=False)
    with jax.named_scope("weights_gather"):
        across = y_swap(shard)
        pair = jnp.concatenate([shard, across], axis=1)
        matrices = place(jnp.zeros((depth, layers, 2 * fine, width), bf16), pair, 0, 0)
        right = left = pair
        for k in range(1, depth // 2):
            right, left = z_step(right, 1), z_step(left, -1)
            matrices = place(place(matrices, right, 0, -k), left, 0, k)
            if k == 1:
                ring_runs = right
        far_right, far_left = z_step(right[:half], 1), z_step(left[half:], -1)

    with jax.named_scope("spread_inputs"):
        h_cols = section_input[0, 0].T
        h_wide = h_cols.astype(f32)
        squares = jnp.stack(split_three(jnp.sum(h_wide * h_wide, axis=0)))
        extra = jnp.concatenate([squares, jnp.zeros((extra_rows - 3, tokens), bf16)], axis=0)
        blocks = h_cols.reshape(per_col, sections, fine, tokens).transpose(1, 0, 2, 3)
        blocks = blocks.reshape(sections, piece, tokens)
        blocks = jnp.concatenate([blocks, jnp.broadcast_to(extra, (sections, extra_rows, tokens))], axis=1)
        blocks = after(blocks, across)
        block_for = [
            lax.dynamic_index_in_dim(blocks, section_idx ^ bits, 0, keepdims=False, allow_negative_indices=False)
            for bits in range(sections)
        ]
        other = section_swap(jnp.stack(block_for[2:]), 2)
        partner = section_swap(jnp.stack([block_for[1], other[1]]), 1)
        mine = jnp.stack([block_for[0], partner[0], other[0], partner[1]])
        right, left = x_step(mine, 1), x_step(mine, -1)
        spread = mine, left, x_step(right, 1), right
        cotans = gather_section(after(section_cotan, ring_runs)[0].transpose(0, 2, 1))

    wide = (depth, 1, 2 * fine, width)
    rows = (1, depth, 2 * fine, tokens)
    cols = (1, width, tokens)
    cut = (1, piece, tokens)
    with jax.named_scope("early_factors"):
        factor_a, factor_b = pl.pallas_call(
            functools.partial(early_kernel, fine, piece, tensors, features),
            out_shape=[
                jax.ShapeDtypeStruct((layers, depth, 2 * fine, tokens), bf16),
                jax.ShapeDtypeStruct((layers, width, tokens), bf16),
            ],
            grid_spec=grid(
                (layers,),
                [pl.BlockSpec((1, piece + extra_rows, tokens), lambda i, plan: (plan[HOME + i], 0, 0))] * 4
                + [
                    pl.BlockSpec(cols, lambda i, plan: (0, 0, 0)),
                    pl.BlockSpec(cols, lambda i, plan: (0, 0, 0)),
                    pl.BlockSpec(cols, lambda i, plan: (0, 0, 0)),
                    pl.BlockSpec(cols, lambda i, plan: (1, 0, 0)),
                ],
                [pl.BlockSpec(rows, lambda i, plan: (i, 0, 0, 0)), pl.BlockSpec(cols, lambda i, plan: (i, 0, 0))],
                [pltpu.VMEM((tall, tokens), f32)],
            ),
            compiler_params=params,
        )(plan, *spread, *cotans, cotans[1])

    with jax.named_scope("weights_gather"):
        far_right, far_left = after(far_right, factor_a), after(far_left, factor_a)
        matrices = place(place(matrices, far_right, 0, depth // 2), far_left, half, depth // 2)

    with jax.named_scope("layer_products"):
        keep, send, h_live, own_cotan, back_own, back = pl.pallas_call(
            functools.partial(layers_kernel, fine, piece, tensors),
            out_shape=[
                jax.ShapeDtypeStruct((2, 2, piece, tokens), f32),
                jax.ShapeDtypeStruct((2, 2, piece, tokens), bf16),
                jax.ShapeDtypeStruct((2, piece, tokens), bf16),
                jax.ShapeDtypeStruct((2, piece, tokens), f32),
                jax.ShapeDtypeStruct((2, piece, tokens), f32),
                jax.ShapeDtypeStruct((tensors - 1, 2, piece, tokens), bf16),
            ],
            grid_spec=grid(
                (2,),
                [
                    pl.BlockSpec(wide, lambda j, plan: (0, plan[FIRST + j], 0, 0)),
                    pl.BlockSpec(wide, lambda j, plan: (0, plan[FIRST + j] + 1, 0, 0)),
                    pl.BlockSpec(rows, lambda j, plan: (plan[FIRST + j], 0, 0, 0)),
                    pl.BlockSpec(cols, lambda j, plan: (plan[FIRST + j], 0, 0)),
                    pl.BlockSpec((1, piece + extra_rows, tokens), lambda j, plan: (plan[LIVE + j], 0, 0)),
                ],
                [
                    pl.BlockSpec((2, *cut), lambda j, plan: (0, j, 0, 0)),
                    pl.BlockSpec((2, *cut), lambda j, plan: (0, j, 0, 0)),
                    pl.BlockSpec(cut, lambda j, plan: (j, 0, 0)),
                    pl.BlockSpec(cut, lambda j, plan: (j, 0, 0)),
                    pl.BlockSpec(cut, lambda j, plan: (j, 0, 0)),
                    pl.BlockSpec((tensors - 1, *cut), lambda j, plan: (0, j, 0, 0)),
                ],
                [pltpu.VMEM((tall, tokens), f32)],
            ),
            compiler_params=params,
            cost_estimate=pl.CostEstimate(flops=8 * tall * width * tokens, bytes_accessed=4 * tall * width * 2, transcendentals=0),
        )(plan, matrices, matrices, factor_a, factor_b, mine)
    with jax.named_scope("forward_sum"):
        partial = keep + section_swap(send, 1).astype(f32)
        raised = partial[0] + section_swap(partial[1].astype(bf16), 2).astype(f32)
        h_low = (h_live.astype(f32) + raised).astype(bf16)
    with jax.named_scope("backward_sum"):
        summed = back_own + x_step(back[0], 1).astype(f32) + x_step(back[2], 3).astype(f32) + x_step(back[1], 2).astype(f32)

    h_second = h_low.astype(f32)
    with jax.named_scope("spread_second"):
        next_rows = x_swap(h_low, 1)
        far_rows = x_swap(jnp.concatenate([h_low, next_rows]), 2)
    with jax.named_scope("second_norm"):
        squares = after(jnp.sum(h_second * h_second, axis=1), summed)
        inv_second = lax.rsqrt(sum_all(squares) / features + epsilon)
    inv = inv_second[:, None, :]
    normed = h_second * inv
    gate = jax.nn.sigmoid(normed)
    d_norm = summed * gate * (1.0 + normed * (1.0 - gate))
    with jax.named_scope("mean_term"):
        mean_term = (sum_all(jnp.sum(h_second * d_norm, axis=1)) / features)[:, None, :]
    d_rows = inv * d_norm - h_second * inv * inv * inv * mean_term
    with jax.named_scope("spread_cotan"):
        around = gather_section((own_cotan + d_rows).astype(bf16))
    with jax.named_scope("late_factors"):
        factor_a, factor_b = pl.pallas_call(
            functools.partial(late_kernel, fine, piece, tensors),
            out_shape=[
                jax.ShapeDtypeStruct((layers, depth, 2 * fine, tokens), bf16),
                jax.ShapeDtypeStruct((layers, width, tokens), bf16),
            ],
            grid_spec=grid(
                (2,),
                [
                    *[pl.BlockSpec(cut, lambda j, plan: (j, 0, 0))] * 3,
                    pl.BlockSpec(cut, lambda j, plan: (2 + j, 0, 0)),
                ]
                * 2
                + [
                    pl.BlockSpec((1, 1, tokens), lambda j, plan: (j, 0, 0)),
                    pl.BlockSpec(memory_space=pl.ANY),
                    pl.BlockSpec(memory_space=pl.ANY),
                ],
                [
                    pl.BlockSpec(rows, lambda j, plan: (plan[FIRST + j] + 1, 0, 0, 0)),
                    pl.BlockSpec(cols, lambda j, plan: (plan[FIRST + j], 0, 0)),
                ],
                [pltpu.VMEM((tall, tokens), f32), pltpu.VMEM((width, tokens), f32)],
            ),
            input_output_aliases={10: 0, 11: 1},
            compiler_params=params,
        )(plan, *around, around[1], h_low, next_rows, far_rows, far_rows, inv_second.reshape(2, 1, tokens), factor_a, factor_b)

    def block_grad(away):
        return lax.dot_general(
            factor_a[:, away % depth], factor_b, (((2,), (2,)), ((0,), (0,))), preferred_element_type=f32
        )

    def parts(array):
        return array[:half], array[half:]

    with jax.named_scope("grad_sum"):
        last = depth // 2
        far = parts(block_grad(last).astype(bf16))
        far = [z_step(far[c], 1 - 2 * c) for c in range(2)]
        chains = [[far[0], None], [None, far[1]]]
        for k in range(last - 1, 0, -1):
            blocks = [parts(block_grad(k)), parts(block_grad(-k))]
            for c in range(2):
                for side in range(2):
                    total = blocks[side][c]
                    if chains[c][side] is not None:
                        total = total + chains[c][side].astype(f32)
                    chains[c][side] = z_step(total.astype(bf16), 1 - 2 * side)
        own = parts(block_grad(0))
        totals = [own[c] + chains[c][0].astype(f32) + chains[c][1].astype(f32) for c in range(2)]
        swapped = [y_swap(t[:, fine:].astype(bf16)).astype(f32) for t in totals]
        return jnp.concatenate([t[:, :fine] + other for t, other in zip(totals, swapped)])


def solution(mesh):
    in_specs = (
        P("pipe", "section", None, "tensor"),
        P("pipe", "section", None, "tensor"),
        P(None, "pipe", "tensor"),
        P(),
        P(),
    )
    out_specs = P(None, ("pipe", "section"), "tensor")
    return jax.shard_map(shards, mesh=mesh, in_specs=in_specs, out_specs=out_specs, check_vma=False)
```

```python
import functools

import jax
import jax.numpy as jnp
from jax import lax
from jax.experimental import pallas as pl
from jax.experimental.pallas import tpu as pltpu
from jax.sharding import PartitionSpec as P

epsilon = 1e-05
bf16 = jnp.bfloat16
f32 = jnp.float32
extra_rows = 16

FIRST, LIVE, HOME, SELF = 0, 2, 4, 10
Z, LOW, SECTION, TENSOR = SELF, SELF + 1, SELF + 2, SELF + 3
PLAN = 16


def silu(values):
    return values * jax.nn.sigmoid(values)


def split_three(values):
    high = values.astype(bf16)
    rest = values - high.astype(f32)
    middle = rest.astype(bf16)
    low = (rest - middle.astype(f32)).astype(bf16)
    return high, middle, low


def plan_kernel(layers, sections, depth, cuts_ref, template_ref, self_ref, plan_ref):
    pipe, section, tensor = self_ref[0], self_ref[1], self_ref[2]
    template = template_ref[pipe]
    cuts = [cuts_ref[template, s] for s in range(sections + 1)]
    live = [jnp.where(cuts[s + 1] > cuts[s] + 1, 1, 0) for s in range(sections)]
    before = [sum(live[:s], jnp.int32(0)) for s in range(sections)]
    for j in range(2):
        here = [jnp.where((live[s] == 1) & (before[s] == j), 1, 0) for s in range(sections)]
        plan_ref[FIRST + j] = sum(here[s] * cuts[s] for s in range(sections))
        plan_ref[LIVE + j] = sum(here[s] * s for s in range(sections)) ^ section
    for layer in range(layers):
        own = [jnp.where((cuts[s] <= layer) & (layer < cuts[s + 1]), 1, 0) for s in range(sections)]
        plan_ref[HOME + layer] = sum(own[s] * s for s in range(sections)) ^ section
    plan_ref[Z] = pipe & (depth - 1)
    plan_ref[LOW] = jnp.where(pipe < depth, 0, 1)
    plan_ref[SECTION] = section
    plan_ref[TENSOR] = tensor


def row_of(plan_ref, tensor_index, part):
    z = (tensor_index & 1) * 4 + part
    return ((z - plan_ref[Z]) & 7) * 2 + ((tensor_index >> 1) ^ plan_ref[LOW])


def spread_rows(fine, piece, plan_ref, tensor_index, values, scratch):
    for part in range(piece // fine):
        at = pl.multiple_of(row_of(plan_ref, tensor_index, part) * fine, 8)
        scratch[pl.ds(at, fine), :] = values[part * fine : (part + 1) * fine]


def early_kernel(fine, piece, tensors, features, plan_ref, *refs):
    row_refs, cotan_refs, (a_out_ref, c_out_ref, scratch) = refs[:4], refs[4:8], refs[8:]
    chunks = [ref[0].astype(f32) for ref in row_refs]
    total = sum(c[piece : piece + 1] + c[piece + 1 : piece + 2] + c[piece + 2 : piece + 3] for c in chunks)
    inv = lax.rsqrt(total / features + epsilon)
    for away, chunk in enumerate(chunks):
        at_tensor = (plan_ref[TENSOR] + away) & (tensors - 1)
        spread_rows(fine, piece, plan_ref, at_tensor, silu(chunk[:piece] * inv), scratch)
    a_out_ref[0] = scratch[...].astype(bf16).reshape(a_out_ref.shape[1:])
    distance = plan_ref[HOME + pl.program_id(0)]
    for away in range(4):

        @pl.when(distance == away)
        def _(away=away):
            c_out_ref[...] = cotan_refs[away][...]


def late_kernel(fine, piece, tensors, plan_ref, *refs):
    piece_refs, row_refs, inv_ref = refs[:4], refs[4:8], refs[8]
    a_out_ref, c_out_ref, a_scratch, c_scratch = refs[-4:]
    per = piece // fine
    for away in range(4):
        at_section = plan_ref[SECTION] ^ away
        block = piece_refs[away][0].astype(f32)
        for q in range(per):
            at = pl.multiple_of((q * per + at_section) * fine, 8)
            c_scratch[pl.ds(at, fine), :] = block[q * fine : (q + 1) * fine]
    c_out_ref[0] = c_scratch[...].astype(bf16)
    for away in range(tensors):
        values = row_refs[away][0].astype(f32)[:piece]
        spread_rows(fine, piece, plan_ref, plan_ref[TENSOR] ^ away, silu(values * inv_ref[0]), a_scratch)
    a_out_ref[0] = a_scratch[...].astype(bf16).reshape(a_out_ref.shape[1:])


def layers_kernel(fine, piece, tensors, plan_ref, w1_ref, w2_ref, a_ref, c_ref, h_ref, keep_ref, send_ref, h_out_ref, c_out_ref, d_keep_ref, d_send_ref, scratch):
    per = piece // fine
    tall = w1_ref.shape[0] * w1_ref.shape[2]
    width, tokens = c_ref.shape[1:]
    active = a_ref[0].reshape(tall, tokens)
    scratch[...] = lax.dot_general(
        w1_ref[:, 0].reshape(tall, width), active, (((0,), (0,)), ((), ())), preferred_element_type=f32
    )
    for away in range(4):
        to = plan_ref[SECTION] ^ away
        parts = [scratch[pl.ds(pl.multiple_of((to + q * per) * fine, 8), fine), :] for q in range(width // piece)]
        block = jnp.concatenate(parts, axis=0)
        if away & 1:
            send_ref[away >> 1, 0] = block.astype(bf16)
        else:
            keep_ref[away >> 1, 0] = block
    h_out_ref[0] = h_ref[0][:piece]
    scratch[...] = c_ref[0].astype(f32)
    parts = [
        scratch[pl.ds(pl.multiple_of((plan_ref[SECTION] + q * per) * fine, 8), fine), :] for q in range(width // piece)
    ]
    c_out_ref[0] = jnp.concatenate(parts, axis=0)
    scratch[...] = jnp.dot(w2_ref[:, 0].reshape(tall, width), c_ref[0], preferred_element_type=f32)
    for away in range(tensors):
        to = plan_ref[TENSOR] ^ away
        parts = [
            scratch[pl.ds(pl.multiple_of(row_of(plan_ref, to, part) * fine, 8), fine), :] for part in range(per)
        ]
        block = jnp.concatenate(parts, axis=0)
        if away & 2:
            d_send_ref[away & 1, 0] = block.astype(bf16)
        else:
            d_keep_ref[away, 0] = block


def shards(section_input, section_cotan, weights, section_cuts, pipe_template):
    pipes = lax.axis_size("pipe")
    sections = lax.axis_size("section")
    tensors = lax.axis_size("tensor")
    layers, stored, width = weights.shape
    tokens = section_input.shape[2]
    features = width * tensors
    fine = stored // sections
    depth = pipes // 2
    tall = pipes * fine
    per_col = pipes // tensors
    piece = per_col * fine
    half = layers // 2
    pipe_idx = lax.axis_index("pipe")
    section_idx = lax.axis_index("section")
    tensor_idx = lax.axis_index("tensor")
    params = pltpu.CompilerParams(vmem_limit_bytes=48 * 1024 * 1024)

    def z_step(array, shift):
        pairs = [(y * depth + z, y * depth + (z + shift) % depth) for y in range(2) for z in range(depth)]
        return lax.ppermute(array, "pipe", pairs)

    def y_swap(array):
        return lax.ppermute(array, "pipe", [(p, (p + depth) % pipes) for p in range(pipes)])

    def x_step(array, shift):
        return lax.ppermute(array, "tensor", [(t, (t + shift) % tensors) for t in range(tensors)])

    def section_swap(array, bits):
        return lax.ppermute(array, "section", [(s, s ^ bits) for s in range(sections)])

    def x_swap(array, bits):
        return lax.ppermute(array, "tensor", [(t, t ^ bits) for t in range(tensors)])

    def sum_rest(array):
        for swap, bits in ((x_swap, 2), (section_swap, 1), (section_swap, 2)):
            array = array + swap(array, bits)
        return array

    def gather_section(chunk, *before):
        other = section_swap(chunk, 2)
        return chunk, section_swap(after(jnp.concatenate([chunk, other]), before), 1), other

    def after(array, other):
        return lax.optimization_barrier((array, other))[0]

    def grid(steps, ins, outs, scratch=()):
        return pltpu.PrefetchScalarGridSpec(
            num_scalar_prefetch=1, grid=steps, in_specs=ins, out_specs=outs, scratch_shapes=list(scratch)
        )

    with jax.named_scope("plan"):
        me = jnp.stack([pipe_idx, section_idx, tensor_idx]).astype(jnp.int32)
        smem = pl.BlockSpec(memory_space=pltpu.SMEM)
        plan = pl.pallas_call(
            functools.partial(plan_kernel, layers, sections, depth),
            out_shape=jax.ShapeDtypeStruct((PLAN,), jnp.int32),
            in_specs=[smem, smem, smem],
            out_specs=smem,
        )(section_cuts, pipe_template, me)

    def place(buffer, chunk, layer, away):
        return lax.dynamic_update_slice(buffer, chunk[None], (away % depth, layer, 0, 0))

    shard = lax.dynamic_slice_in_dim(weights, section_idx * fine, fine, 1, allow_negative_indices=False)
    with jax.named_scope("weights_gather"):
        across = y_swap(shard)
        pair = jnp.concatenate([shard, across], axis=1)
        matrices = place(jnp.zeros((depth, layers, 2 * fine, width), bf16), pair, 0, 0)
        right = left = pair
        ring_steps = []
        for k in range(1, depth // 2):
            right, left = z_step(right, 1), z_step(left, -1)
            matrices = place(place(matrices, right, 0, -k), left, 0, k)
            ring_steps.append((right, left))
        far_right, far_left = z_step(right[:half], 1), z_step(left[half:], -1)

    with jax.named_scope("spread_inputs"):
        h_cols = section_input[0, 0].T
        h_wide = h_cols.astype(f32)
        squares = jnp.stack(split_three(jnp.sum(h_wide * h_wide, axis=0)))
        extra = jnp.concatenate([squares, jnp.zeros((extra_rows - 3, tokens), bf16)], axis=0)
        blocks = h_cols.reshape(per_col, sections, fine, tokens).transpose(1, 0, 2, 3)
        blocks = blocks.reshape(sections, piece, tokens)
        blocks = jnp.concatenate([blocks, jnp.broadcast_to(extra, (sections, extra_rows, tokens))], axis=1)
        blocks = after(blocks, across)
        block_for = [
            lax.dynamic_index_in_dim(blocks, section_idx ^ bits, 0, keepdims=False, allow_negative_indices=False)
            for bits in range(sections)
        ]
        other = section_swap(jnp.stack(block_for[2:]), 2)
        partner = section_swap(after(jnp.stack([block_for[1], other[1]]), ring_steps[0]), 1)
        mine = jnp.stack([block_for[0], partner[0], other[0], partner[1]])
        right, left = x_step(mine, 1), x_step(mine, -1)
        spread = mine, left, x_step(right, 1), right
        cotans = gather_section(after(section_cotan[0].transpose(0, 2, 1), across), ring_steps[1])

    wide = (depth, 1, 2 * fine, width)
    rows = (1, depth, 2 * fine, tokens)
    cols = (1, width, tokens)
    cut = (1, piece, tokens)
    with jax.named_scope("early_factors"):
        factor_a, factor_b = pl.pallas_call(
            functools.partial(early_kernel, fine, piece, tensors, features),
            out_shape=[
                jax.ShapeDtypeStruct((layers, depth, 2 * fine, tokens), bf16),
                jax.ShapeDtypeStruct((layers, width, tokens), bf16),
            ],
            grid_spec=grid(
                (layers,),
                [pl.BlockSpec((1, piece + extra_rows, tokens), lambda i, plan: (plan[HOME + i], 0, 0))] * 4
                + [
                    pl.BlockSpec(cols, lambda i, plan: (0, 0, 0)),
                    pl.BlockSpec(cols, lambda i, plan: (0, 0, 0)),
                    pl.BlockSpec(cols, lambda i, plan: (0, 0, 0)),
                    pl.BlockSpec(cols, lambda i, plan: (1, 0, 0)),
                ],
                [pl.BlockSpec(rows, lambda i, plan: (i, 0, 0, 0)), pl.BlockSpec(cols, lambda i, plan: (i, 0, 0))],
                [pltpu.VMEM((tall, tokens), f32)],
            ),
            compiler_params=params,
        )(plan, *spread, *cotans, cotans[1])

    with jax.named_scope("weights_gather"):
        far_right, far_left = after(far_right, factor_a), after(far_left, factor_a)
        matrices = place(place(matrices, far_right, 0, depth // 2), far_left, half, depth // 2)

    with jax.named_scope("layer_products"):
        keep, send, h_live, own_cotan, back_keep, back_send = pl.pallas_call(
            functools.partial(layers_kernel, fine, piece, tensors),
            out_shape=[
                jax.ShapeDtypeStruct((2, 2, piece, tokens), f32),
                jax.ShapeDtypeStruct((2, 2, piece, tokens), bf16),
                jax.ShapeDtypeStruct((2, piece, tokens), bf16),
                jax.ShapeDtypeStruct((2, piece, tokens), f32),
                jax.ShapeDtypeStruct((2, 2, piece, tokens), f32),
                jax.ShapeDtypeStruct((2, 2, piece, tokens), bf16),
            ],
            grid_spec=grid(
                (2,),
                [
                    pl.BlockSpec(wide, lambda j, plan: (0, plan[FIRST + j], 0, 0)),
                    pl.BlockSpec(wide, lambda j, plan: (0, plan[FIRST + j] + 1, 0, 0)),
                    pl.BlockSpec(rows, lambda j, plan: (plan[FIRST + j], 0, 0, 0)),
                    pl.BlockSpec(cols, lambda j, plan: (plan[FIRST + j], 0, 0)),
                    pl.BlockSpec((1, piece + extra_rows, tokens), lambda j, plan: (plan[LIVE + j], 0, 0)),
                ],
                [
                    pl.BlockSpec((2, *cut), lambda j, plan: (0, j, 0, 0)),
                    pl.BlockSpec((2, *cut), lambda j, plan: (0, j, 0, 0)),
                    pl.BlockSpec(cut, lambda j, plan: (j, 0, 0)),
                    pl.BlockSpec(cut, lambda j, plan: (j, 0, 0)),
                    pl.BlockSpec((2, *cut), lambda j, plan: (0, j, 0, 0)),
                    pl.BlockSpec((2, *cut), lambda j, plan: (0, j, 0, 0)),
                ],
                [pltpu.VMEM((tall, tokens), f32)],
            ),
            compiler_params=params,
            cost_estimate=pl.CostEstimate(flops=8 * tall * width * tokens, bytes_accessed=4 * tall * width * 2, transcendentals=0),
        )(plan, matrices, matrices, factor_a, factor_b, mine)
    with jax.named_scope("forward_sum"):
        partial = keep + section_swap(send, 1).astype(f32)
        raised = partial[0] + section_swap(partial[1].astype(bf16), 2).astype(f32)
        h_low = (h_live.astype(f32) + raised).astype(bf16)
    with jax.named_scope("backward_sum"):
        backs = back_keep + x_swap(back_send, 2).astype(f32)
        summed = backs[0] + x_swap(backs[1].astype(bf16), 1).astype(f32)

    h_second = h_low.astype(f32)
    with jax.named_scope("spread_second"):
        own_squares = jnp.sum(h_second * h_second, axis=1)
        extra = jnp.stack(split_three(own_squares), axis=1)
        extra = jnp.concatenate([extra, jnp.zeros((2, extra_rows - 3, tokens), bf16)], axis=1)
        own_rows = jnp.concatenate([h_low, extra], axis=1)
        next_rows = x_swap(own_rows, 1)
        far_rows = x_swap(jnp.concatenate([own_rows, next_rows]), 2)
    with jax.named_scope("second_norm"):
        squares = own_squares + jnp.sum(next_rows[:, piece : piece + 3].astype(f32), axis=1)
        inv_second = lax.rsqrt(sum_rest(after(squares, backs)) / features + epsilon)
    inv = inv_second[:, None, :]
    normed = h_second * inv
    gate = jax.nn.sigmoid(normed)
    d_norm = summed * gate * (1.0 + normed * (1.0 - gate))
    with jax.named_scope("mean_term"):
        sums = jnp.sum(h_second * d_norm, axis=1)
        mean_term = (sum_rest(sums + x_swap(sums, 1)) / features)[:, None, :]
    d_rows = inv * d_norm - h_second * inv * inv * inv * mean_term
    with jax.named_scope("spread_cotan"):
        around = gather_section((own_cotan + d_rows).astype(bf16), far_rows)
    with jax.named_scope("late_factors"):
        factor_a, factor_b = pl.pallas_call(
            functools.partial(late_kernel, fine, piece, tensors),
            out_shape=[
                jax.ShapeDtypeStruct((layers, depth, 2 * fine, tokens), bf16),
                jax.ShapeDtypeStruct((layers, width, tokens), bf16),
            ],
            grid_spec=grid(
                (2,),
                [
                    pl.BlockSpec((1, size, tokens), lambda j, plan, start=start: (start + j, 0, 0))
                    for size in (piece, piece + extra_rows)
                    for start in (0, 0, 0, 2)
                ]
                + [
                    pl.BlockSpec((1, 1, tokens), lambda j, plan: (j, 0, 0)),
                    pl.BlockSpec(memory_space=pl.ANY),
                    pl.BlockSpec(memory_space=pl.ANY),
                ],
                [
                    pl.BlockSpec(rows, lambda j, plan: (plan[FIRST + j] + 1, 0, 0, 0)),
                    pl.BlockSpec(cols, lambda j, plan: (plan[FIRST + j], 0, 0)),
                ],
                [pltpu.VMEM((tall, tokens), f32), pltpu.VMEM((width, tokens), f32)],
            ),
            input_output_aliases={10: 0, 11: 1},
            compiler_params=params,
        )(plan, *around, around[1], own_rows, next_rows, far_rows, far_rows, inv_second.reshape(2, 1, tokens), factor_a, factor_b)

    def block_grads(low, high, columns):
        rows = factor_a[:, low:high].reshape(layers, (high - low) * 2 * fine, tokens)
        grads = lax.dot_general(rows, columns, (((2,), (2,)), ((0,), (0,))), preferred_element_type=f32)
        grads = grads.reshape(layers, high - low, 2 * fine, width)
        return {(low + i): grads[:, i] for i in range(high - low)}

    def parts(array):
        return array[:half], array[half:]

    with jax.named_scope("grad_sum"):
        last = depth // 2
        grads = block_grads(last - 1, last + 2, factor_b)
        far = parts(grads[last].astype(bf16))
        columns = after(factor_b, far)
        grads |= block_grads(0, last - 1, columns) | block_grads(last + 2, depth, columns)
        far = [z_step(far[c], 1 - 2 * c) for c in range(2)]
        chains = [[far[0], None], [None, far[1]]]
        for k in range(last - 1, 0, -1):
            blocks = [parts(grads[k]), parts(grads[depth - k])]
            for c in range(2):
                for side in range(2):
                    total = blocks[side][c]
                    if chains[c][side] is not None:
                        total = total + chains[c][side].astype(f32)
                    chains[c][side] = z_step(total.astype(bf16), 1 - 2 * side)
        own = parts(grads[0])
        total = jnp.concatenate([own[c] + chains[c][0].astype(f32) + chains[c][1].astype(f32) for c in range(2)])
        return total[:, :fine] + y_swap(total[:, fine:].astype(bf16)).astype(f32)


def solution(mesh):
    in_specs = (
        P("pipe", "section", None, "tensor"),
        P("pipe", "section", None, "tensor"),
        P(None, "pipe", "tensor"),
        P(),
        P(),
    )
    out_specs = P(None, ("pipe", "section"), "tensor")
    return jax.shard_map(shards, mesh=mesh, in_specs=in_specs, out_specs=out_specs, check_vma=False)
```

```python
import functools

import jax
import jax.numpy as jnp
from jax import lax
from jax.experimental import pallas as pl
from jax.experimental.pallas import tpu as pltpu
from jax.sharding import PartitionSpec as P

epsilon = 1e-05
bf16 = jnp.bfloat16
f32 = jnp.float32
extra_rows = 16

FIRST, LIVE, HOME, SELF = 0, 2, 4, 10
Z, LOW, SECTION, TENSOR = SELF, SELF + 1, SELF + 2, SELF + 3
PLAN = 16


def silu(values):
    return values * jax.nn.sigmoid(values)


def split_three(values):
    high = values.astype(bf16)
    rest = values - high.astype(f32)
    middle = rest.astype(bf16)
    low = (rest - middle.astype(f32)).astype(bf16)
    return high, middle, low


def plan_kernel(layers, sections, depth, cuts_ref, template_ref, self_ref, plan_ref):
    pipe, section, tensor = self_ref[0], self_ref[1], self_ref[2]
    template = template_ref[pipe]
    cuts = [cuts_ref[template, s] for s in range(sections + 1)]
    live = [jnp.where(cuts[s + 1] > cuts[s] + 1, 1, 0) for s in range(sections)]
    before = [sum(live[:s], jnp.int32(0)) for s in range(sections)]
    for j in range(2):
        here = [jnp.where((live[s] == 1) & (before[s] == j), 1, 0) for s in range(sections)]
        plan_ref[FIRST + j] = sum(here[s] * cuts[s] for s in range(sections))
        plan_ref[LIVE + j] = sum(here[s] * s for s in range(sections)) ^ section
    for layer in range(layers):
        own = [jnp.where((cuts[s] <= layer) & (layer < cuts[s + 1]), 1, 0) for s in range(sections)]
        plan_ref[HOME + layer] = sum(own[s] * s for s in range(sections)) ^ section
    plan_ref[Z] = pipe & (depth - 1)
    plan_ref[LOW] = jnp.where(pipe < depth, 0, 1)
    plan_ref[SECTION] = section
    plan_ref[TENSOR] = tensor


def row_of(plan_ref, tensor_index, part):
    z = (tensor_index & 1) * 4 + part
    return ((z - plan_ref[Z]) & 7) * 2 + ((tensor_index >> 1) ^ plan_ref[LOW])


def spread_rows(fine, piece, plan_ref, tensor_index, values, scratch):
    for part in range(piece // fine):
        at = pl.multiple_of(row_of(plan_ref, tensor_index, part) * fine, 8)
        scratch[pl.ds(at, fine), :] = values[part * fine : (part + 1) * fine]


def early_kernel(fine, piece, tensors, features, plan_ref, *refs):
    row_refs, cotan_refs, (a_out_ref, c_out_ref, scratch) = refs[:4], refs[4:8], refs[8:]
    chunks = [ref[0].astype(f32) for ref in row_refs]
    total = sum(c[piece : piece + 1] + c[piece + 1 : piece + 2] + c[piece + 2 : piece + 3] for c in chunks)
    inv = lax.rsqrt(total / features + epsilon)
    for away, chunk in enumerate(chunks):
        at_tensor = (plan_ref[TENSOR] + away) & (tensors - 1)
        spread_rows(fine, piece, plan_ref, at_tensor, silu(chunk[:piece] * inv), scratch)
    a_out_ref[0] = scratch[...].astype(bf16).reshape(a_out_ref.shape[1:])
    distance = plan_ref[HOME + pl.program_id(0)]
    for away in range(4):

        @pl.when(distance == away)
        def _(away=away):
            c_out_ref[...] = cotan_refs[away][...]


def late_kernel(fine, piece, tensors, plan_ref, *refs):
    piece_refs, row_refs, inv_ref = refs[:4], refs[4:8], refs[8]
    a_out_ref, c_out_ref, a_scratch, c_scratch = refs[-4:]
    per = piece // fine
    for away in range(4):
        at_section = plan_ref[SECTION] ^ away
        block = piece_refs[away][0].astype(f32)
        for q in range(per):
            at = pl.multiple_of((q * per + at_section) * fine, 8)
            c_scratch[pl.ds(at, fine), :] = block[q * fine : (q + 1) * fine]
    c_out_ref[0] = c_scratch[...].astype(bf16)
    for away in range(tensors):
        values = row_refs[away][0].astype(f32)[:piece]
        spread_rows(fine, piece, plan_ref, plan_ref[TENSOR] ^ away, silu(values * inv_ref[0]), a_scratch)
    a_out_ref[0] = a_scratch[...].astype(bf16).reshape(a_out_ref.shape[1:])


def layers_kernel(fine, piece, tensors, plan_ref, w1_ref, w2_ref, a_ref, c_ref, h_ref, keep_ref, send_ref, h_out_ref, c_out_ref, d_keep_ref, d_send_ref, scratch):
    per = piece // fine
    tall = w1_ref.shape[0] * w1_ref.shape[2]
    width, tokens = c_ref.shape[1:]
    active = a_ref[0].reshape(tall, tokens)
    scratch[...] = lax.dot_general(
        w1_ref[:, 0].reshape(tall, width), active, (((0,), (0,)), ((), ())), preferred_element_type=f32
    )
    for away in range(4):
        to = plan_ref[SECTION] ^ away
        parts = [scratch[pl.ds(pl.multiple_of((to + q * per) * fine, 8), fine), :] for q in range(width // piece)]
        block = jnp.concatenate(parts, axis=0)
        if away & 1:
            send_ref[away >> 1, 0] = block.astype(bf16)
        else:
            keep_ref[away >> 1, 0] = block
    h_out_ref[0] = h_ref[0][:piece]
    scratch[...] = c_ref[0].astype(f32)
    parts = [
        scratch[pl.ds(pl.multiple_of((plan_ref[SECTION] + q * per) * fine, 8), fine), :] for q in range(width // piece)
    ]
    c_out_ref[0] = jnp.concatenate(parts, axis=0)
    scratch[...] = jnp.dot(w2_ref[:, 0].reshape(tall, width), c_ref[0], preferred_element_type=f32)
    for away in range(tensors):
        to = plan_ref[TENSOR] ^ away
        parts = [
            scratch[pl.ds(pl.multiple_of(row_of(plan_ref, to, part) * fine, 8), fine), :] for part in range(per)
        ]
        block = jnp.concatenate(parts, axis=0)
        if away & 2:
            d_send_ref[away & 1, 0] = block.astype(bf16)
        else:
            d_keep_ref[away, 0] = block


def shards(section_input, section_cotan, weights, section_cuts, pipe_template):
    pipes = lax.axis_size("pipe")
    sections = lax.axis_size("section")
    tensors = lax.axis_size("tensor")
    layers, stored, width = weights.shape
    tokens = section_input.shape[2]
    features = width * tensors
    fine = stored // sections
    depth = pipes // 2
    tall = pipes * fine
    per_col = pipes // tensors
    piece = per_col * fine
    half = layers // 2
    pipe_idx = lax.axis_index("pipe")
    section_idx = lax.axis_index("section")
    tensor_idx = lax.axis_index("tensor")
    params = pltpu.CompilerParams(vmem_limit_bytes=48 * 1024 * 1024)

    def z_step(array, shift):
        pairs = [(y * depth + z, y * depth + (z + shift) % depth) for y in range(2) for z in range(depth)]
        return lax.ppermute(array, "pipe", pairs)

    def y_swap(array):
        return lax.ppermute(array, "pipe", [(p, (p + depth) % pipes) for p in range(pipes)])

    def x_step(array, shift):
        return lax.ppermute(array, "tensor", [(t, (t + shift) % tensors) for t in range(tensors)])

    def section_swap(array, bits):
        return lax.ppermute(array, "section", [(s, s ^ bits) for s in range(sections)])

    def x_swap(array, bits):
        return lax.ppermute(array, "tensor", [(t, t ^ bits) for t in range(tensors)])

    def sum_rest(array, before=()):
        for swap, bits in ((x_swap, 2), (section_swap, 1)):
            array = array + swap(array, bits)
        array = after(array, before)
        return array + section_swap(array, 2)

    def gather_section(chunk, *before):
        other = section_swap(chunk, 2)
        return chunk, section_swap(after(jnp.concatenate([chunk, other]), before), 1), other

    def after(array, other):
        return lax.optimization_barrier((array, other))[0]

    def grid(steps, ins, outs, scratch=()):
        return pltpu.PrefetchScalarGridSpec(
            num_scalar_prefetch=1, grid=steps, in_specs=ins, out_specs=outs, scratch_shapes=list(scratch)
        )

    with jax.named_scope("plan"):
        me = jnp.stack([pipe_idx, section_idx, tensor_idx]).astype(jnp.int32)
        smem = pl.BlockSpec(memory_space=pltpu.SMEM)
        plan = pl.pallas_call(
            functools.partial(plan_kernel, layers, sections, depth),
            out_shape=jax.ShapeDtypeStruct((PLAN,), jnp.int32),
            in_specs=[smem, smem, smem],
            out_specs=smem,
        )(section_cuts, pipe_template, me)

    def place(buffer, chunk, layer, away):
        return lax.dynamic_update_slice(buffer, chunk[None], (away % depth, layer, 0, 0))

    shard = lax.dynamic_slice_in_dim(weights, section_idx * fine, fine, 1, allow_negative_indices=False)
    with jax.named_scope("weights_gather"):
        across = y_swap(shard)
        pair = jnp.concatenate([shard, across], axis=1)
        matrices = place(jnp.zeros((depth, layers, 2 * fine, width), bf16), pair, 0, 0)
        right = left = pair
        ring_steps = []
        for k in range(1, depth // 2):
            right, left = z_step(right, 1), z_step(left, -1)
            matrices = place(place(matrices, right, 0, -k), left, 0, k)
            ring_steps.append((right, left))
        far_right, far_left = z_step(right[:half], 1), z_step(left[half:], -1)

    with jax.named_scope("spread_inputs"):
        h_cols = section_input[0, 0].T
        h_wide = h_cols.astype(f32)
        squares = jnp.stack(split_three(jnp.sum(h_wide * h_wide, axis=0)))
        extra = jnp.concatenate([squares, jnp.zeros((extra_rows - 3, tokens), bf16)], axis=0)
        blocks = h_cols.reshape(per_col, sections, fine, tokens).transpose(1, 0, 2, 3)
        blocks = blocks.reshape(sections, piece, tokens)
        blocks = jnp.concatenate([blocks, jnp.broadcast_to(extra, (sections, extra_rows, tokens))], axis=1)
        blocks = after(blocks, across)
        block_for = [
            lax.dynamic_index_in_dim(blocks, section_idx ^ bits, 0, keepdims=False, allow_negative_indices=False)
            for bits in range(sections)
        ]
        other = section_swap(jnp.stack(block_for[2:]), 2)
        partner = section_swap(after(jnp.stack([block_for[1], other[1]]), ring_steps[0]), 1)
        mine = jnp.stack([block_for[0], partner[0], other[0], partner[1]])
        right, left = x_step(mine, 1), x_step(mine, -1)
        spread = mine, left, x_step(right, 1), right
        cotans = gather_section(after(section_cotan[0].transpose(0, 2, 1), across), ring_steps[1])

    wide = (depth, 1, 2 * fine, width)
    rows = (1, depth, 2 * fine, tokens)
    cols = (1, width, tokens)
    cut = (1, piece, tokens)
    with jax.named_scope("early_factors"):
        factor_a, factor_b = pl.pallas_call(
            functools.partial(early_kernel, fine, piece, tensors, features),
            out_shape=[
                jax.ShapeDtypeStruct((layers, depth, 2 * fine, tokens), bf16),
                jax.ShapeDtypeStruct((layers, width, tokens), bf16),
            ],
            grid_spec=grid(
                (layers,),
                [pl.BlockSpec((1, piece + extra_rows, tokens), lambda i, plan: (plan[HOME + i], 0, 0))] * 4
                + [
                    pl.BlockSpec(cols, lambda i, plan: (0, 0, 0)),
                    pl.BlockSpec(cols, lambda i, plan: (0, 0, 0)),
                    pl.BlockSpec(cols, lambda i, plan: (0, 0, 0)),
                    pl.BlockSpec(cols, lambda i, plan: (1, 0, 0)),
                ],
                [pl.BlockSpec(rows, lambda i, plan: (i, 0, 0, 0)), pl.BlockSpec(cols, lambda i, plan: (i, 0, 0))],
                [pltpu.VMEM((tall, tokens), f32)],
            ),
            compiler_params=params,
        )(plan, *spread, *cotans, cotans[1])

    with jax.named_scope("weights_gather"):
        far_right, far_left = after(far_right, factor_a), after(far_left, factor_a)
        matrices = place(place(matrices, far_right, 0, depth // 2), far_left, half, depth // 2)

    with jax.named_scope("layer_products"):
        keep, send, h_live, own_cotan, back_keep, back_send = pl.pallas_call(
            functools.partial(layers_kernel, fine, piece, tensors),
            out_shape=[
                jax.ShapeDtypeStruct((2, 2, piece, tokens), f32),
                jax.ShapeDtypeStruct((2, 2, piece, tokens), bf16),
                jax.ShapeDtypeStruct((2, piece, tokens), bf16),
                jax.ShapeDtypeStruct((2, piece, tokens), f32),
                jax.ShapeDtypeStruct((2, 2, piece, tokens), f32),
                jax.ShapeDtypeStruct((2, 2, piece, tokens), bf16),
            ],
            grid_spec=grid(
                (2,),
                [
                    pl.BlockSpec(wide, lambda j, plan: (0, plan[FIRST + j], 0, 0)),
                    pl.BlockSpec(wide, lambda j, plan: (0, plan[FIRST + j] + 1, 0, 0)),
                    pl.BlockSpec(rows, lambda j, plan: (plan[FIRST + j], 0, 0, 0)),
                    pl.BlockSpec(cols, lambda j, plan: (plan[FIRST + j], 0, 0)),
                    pl.BlockSpec((1, piece + extra_rows, tokens), lambda j, plan: (plan[LIVE + j], 0, 0)),
                ],
                [
                    pl.BlockSpec((2, *cut), lambda j, plan: (0, j, 0, 0)),
                    pl.BlockSpec((2, *cut), lambda j, plan: (0, j, 0, 0)),
                    pl.BlockSpec(cut, lambda j, plan: (j, 0, 0)),
                    pl.BlockSpec(cut, lambda j, plan: (j, 0, 0)),
                    pl.BlockSpec((2, *cut), lambda j, plan: (0, j, 0, 0)),
                    pl.BlockSpec((2, *cut), lambda j, plan: (0, j, 0, 0)),
                ],
                [pltpu.VMEM((tall, tokens), f32)],
            ),
            compiler_params=params,
            cost_estimate=pl.CostEstimate(flops=8 * tall * width * tokens, bytes_accessed=4 * tall * width * 2, transcendentals=0),
        )(plan, matrices, matrices, factor_a, factor_b, mine)
    with jax.named_scope("forward_sum"):
        partial = keep + section_swap(send, 1).astype(f32)
        raised = partial[0] + section_swap(partial[1].astype(bf16), 2).astype(f32)
        h_low = (h_live.astype(f32) + raised).astype(bf16)
    with jax.named_scope("backward_sum"):
        backs = back_keep + x_swap(back_send, 2).astype(f32)
        summed = backs[0] + x_swap(backs[1].astype(bf16), 1).astype(f32)

    h_second = h_low.astype(f32)
    with jax.named_scope("spread_second"):
        own_squares = jnp.sum(h_second * h_second, axis=1)
        extra = jnp.stack(split_three(own_squares), axis=1)
        extra = jnp.concatenate([extra, jnp.zeros((2, extra_rows - 3, tokens), bf16)], axis=1)
        own_rows = jnp.concatenate([h_low, extra], axis=1)
        next_rows = x_swap(own_rows, 1)
        far_rows = x_swap(jnp.concatenate([own_rows, next_rows]), 2)
    with jax.named_scope("second_norm"):
        squares = own_squares + jnp.sum(next_rows[:, piece : piece + 3].astype(f32), axis=1)
        inv_second = lax.rsqrt(sum_rest(after(squares, backs)) / features + epsilon)
    inv = inv_second[:, None, :]
    normed = h_second * inv
    gate = jax.nn.sigmoid(normed)
    d_norm = summed * gate * (1.0 + normed * (1.0 - gate))
    with jax.named_scope("mean_term"):
        sums = jnp.sum(h_second * d_norm, axis=1)
        mean_term = (sum_rest(sums + x_swap(sums, 1), far_rows) / features)[:, None, :]
    d_rows = inv * d_norm - h_second * inv * inv * inv * mean_term
    with jax.named_scope("spread_cotan"):
        around = gather_section((own_cotan + d_rows).astype(bf16))
    with jax.named_scope("late_factors"):
        factor_a, factor_b = pl.pallas_call(
            functools.partial(late_kernel, fine, piece, tensors),
            out_shape=[
                jax.ShapeDtypeStruct((layers, depth, 2 * fine, tokens), bf16),
                jax.ShapeDtypeStruct((layers, width, tokens), bf16),
            ],
            grid_spec=grid(
                (2,),
                [
                    pl.BlockSpec((1, size, tokens), lambda j, plan, start=start: (start + j, 0, 0))
                    for size in (piece, piece + extra_rows)
                    for start in (0, 0, 0, 2)
                ]
                + [
                    pl.BlockSpec((1, 1, tokens), lambda j, plan: (j, 0, 0)),
                    pl.BlockSpec(memory_space=pl.ANY),
                    pl.BlockSpec(memory_space=pl.ANY),
                ],
                [
                    pl.BlockSpec(rows, lambda j, plan: (plan[FIRST + j] + 1, 0, 0, 0)),
                    pl.BlockSpec(cols, lambda j, plan: (plan[FIRST + j], 0, 0)),
                ],
                [pltpu.VMEM((tall, tokens), f32), pltpu.VMEM((width, tokens), f32)],
            ),
            input_output_aliases={10: 0, 11: 1},
            compiler_params=params,
        )(plan, *around, around[1], own_rows, next_rows, far_rows, far_rows, inv_second.reshape(2, 1, tokens), factor_a, factor_b)

    def block_grad(c, away):
        part = slice(c * half, (c + 1) * half)
        return lax.dot_general(
            factor_a[part, away % depth], factor_b[part], (((2,), (2,)), ((0,), (0,))), preferred_element_type=f32
        )

    with jax.named_scope("grad_sum"):
        last = depth // 2
        far = [z_step(block_grad(c, last).astype(bf16), 1 - 2 * c) for c in range(2)]
        chains = [[far[0], None], [None, far[1]]]
        for k in range(last - 1, 0, -1):
            for c in range(2):
                for side in range(2):
                    shift = 1 - 2 * side
                    total = block_grad(c, k * shift)
                    if chains[c][side] is not None:
                        total = total + chains[c][side].astype(f32)
                    chains[c][side] = z_step(total.astype(bf16), shift)
        totals = [block_grad(c, 0) + chains[c][0].astype(f32) + chains[c][1].astype(f32) for c in range(2)]
        swapped = [y_swap(t[:, fine:].astype(bf16)).astype(f32) for t in totals]
        return jnp.concatenate([t[:, :fine] + other for t, other in zip(totals, swapped)])


def solution(mesh):
    in_specs = (
        P("pipe", "section", None, "tensor"),
        P("pipe", "section", None, "tensor"),
        P(None, "pipe", "tensor"),
        P(),
        P(),
    )
    out_specs = P(None, ("pipe", "section"), "tensor")
    return jax.shard_map(shards, mesh=mesh, in_specs=in_specs, out_specs=out_specs, check_vma=False)
```

```python
import functools

import jax
import jax.numpy as jnp
from jax import lax
from jax.experimental import pallas as pl
from jax.experimental.pallas import tpu as pltpu
from jax.sharding import PartitionSpec as P

epsilon = 1e-05
bf16 = jnp.bfloat16
f32 = jnp.float32
extra_rows = 16

FIRST, LIVE, HOME, SELF = 0, 2, 4, 10
Z, LOW, SECTION, TENSOR = SELF, SELF + 1, SELF + 2, SELF + 3
PLAN = 16


def silu(values):
    return values * jax.nn.sigmoid(values)


def split_three(values):
    high = values.astype(bf16)
    rest = values - high.astype(f32)
    middle = rest.astype(bf16)
    low = (rest - middle.astype(f32)).astype(bf16)
    return high, middle, low


def plan_kernel(layers, sections, depth, cuts_ref, template_ref, self_ref, plan_ref):
    pipe, section, tensor = self_ref[0], self_ref[1], self_ref[2]
    template = template_ref[pipe]
    cuts = [cuts_ref[template, s] for s in range(sections + 1)]
    live = [jnp.where(cuts[s + 1] > cuts[s] + 1, 1, 0) for s in range(sections)]
    before = [sum(live[:s], jnp.int32(0)) for s in range(sections)]
    for j in range(2):
        here = [jnp.where((live[s] == 1) & (before[s] == j), 1, 0) for s in range(sections)]
        plan_ref[FIRST + j] = sum(here[s] * cuts[s] for s in range(sections))
        plan_ref[LIVE + j] = sum(here[s] * s for s in range(sections)) ^ section
    for layer in range(layers):
        own = [jnp.where((cuts[s] <= layer) & (layer < cuts[s + 1]), 1, 0) for s in range(sections)]
        plan_ref[HOME + layer] = sum(own[s] * s for s in range(sections)) ^ section
    plan_ref[Z] = pipe & (depth - 1)
    plan_ref[LOW] = jnp.where(pipe < depth, 0, 1)
    plan_ref[SECTION] = section
    plan_ref[TENSOR] = tensor


def row_of(plan_ref, tensor_index, part):
    z = (tensor_index & 1) * 4 + part
    return ((z - plan_ref[Z]) & 7) * 2 + ((tensor_index >> 1) ^ plan_ref[LOW])


def spread_rows(fine, piece, plan_ref, tensor_index, values, scratch):
    for part in range(piece // fine):
        at = pl.multiple_of(row_of(plan_ref, tensor_index, part) * fine, 8)
        scratch[pl.ds(at, fine), :] = values[part * fine : (part + 1) * fine]


def early_kernel(fine, piece, tensors, features, plan_ref, *refs):
    row_refs, cotan_refs, (a_out_ref, c_out_ref, scratch) = refs[:4], refs[4:8], refs[8:]
    chunks = [ref[0].astype(f32) for ref in row_refs]
    total = sum(c[piece : piece + 1] + c[piece + 1 : piece + 2] + c[piece + 2 : piece + 3] for c in chunks)
    inv = lax.rsqrt(total / features + epsilon)
    for away, chunk in enumerate(chunks):
        at_tensor = (plan_ref[TENSOR] + away) & (tensors - 1)
        spread_rows(fine, piece, plan_ref, at_tensor, silu(chunk[:piece] * inv), scratch)
    a_out_ref[0] = scratch[...].astype(bf16).reshape(a_out_ref.shape[1:])
    distance = plan_ref[HOME + pl.program_id(0)]
    for away in range(4):

        @pl.when(distance == away)
        def _(away=away):
            c_out_ref[...] = cotan_refs[away][...]


def late_kernel(fine, piece, tensors, plan_ref, *refs):
    piece_refs, row_refs, inv_ref = refs[:4], refs[4:8], refs[8]
    a_out_ref, c_out_ref, a_scratch, c_scratch = refs[-4:]
    per = piece // fine
    for away in range(4):
        at_section = plan_ref[SECTION] ^ away
        block = piece_refs[away][0].astype(f32)
        for q in range(per):
            at = pl.multiple_of((q * per + at_section) * fine, 8)
            c_scratch[pl.ds(at, fine), :] = block[q * fine : (q + 1) * fine]
    c_out_ref[0] = c_scratch[...].astype(bf16)
    for away in range(tensors):
        values = row_refs[away][0].astype(f32)[:piece]
        spread_rows(fine, piece, plan_ref, plan_ref[TENSOR] ^ away, silu(values * inv_ref[0]), a_scratch)
    a_out_ref[0] = a_scratch[...].astype(bf16).reshape(a_out_ref.shape[1:])


def layers_kernel(fine, piece, tensors, plan_ref, w1_ref, w2_ref, a_ref, c_ref, h_ref, keep_ref, send_ref, h_out_ref, c_out_ref, d_keep_ref, d_send_ref, scratch):
    per = piece // fine
    tall = w1_ref.shape[0] * w1_ref.shape[2]
    width, tokens = c_ref.shape[1:]
    active = a_ref[0].reshape(tall, tokens)
    scratch[...] = lax.dot_general(
        w1_ref[:, 0].reshape(tall, width), active, (((0,), (0,)), ((), ())), preferred_element_type=f32
    )
    for away in range(4):
        to = plan_ref[SECTION] ^ away
        parts = [scratch[pl.ds(pl.multiple_of((to + q * per) * fine, 8), fine), :] for q in range(width // piece)]
        block = jnp.concatenate(parts, axis=0)
        if away & 1:
            send_ref[away >> 1, 0] = block.astype(bf16)
        else:
            keep_ref[away >> 1, 0] = block
    h_out_ref[0] = h_ref[0][:piece]
    scratch[...] = c_ref[0].astype(f32)
    parts = [
        scratch[pl.ds(pl.multiple_of((plan_ref[SECTION] + q * per) * fine, 8), fine), :] for q in range(width // piece)
    ]
    c_out_ref[0] = jnp.concatenate(parts, axis=0)
    scratch[...] = jnp.dot(w2_ref[:, 0].reshape(tall, width), c_ref[0], preferred_element_type=f32)
    for away in range(tensors):
        to = plan_ref[TENSOR] ^ away
        parts = [
            scratch[pl.ds(pl.multiple_of(row_of(plan_ref, to, part) * fine, 8), fine), :] for part in range(per)
        ]
        block = jnp.concatenate(parts, axis=0)
        if away & 2:
            d_send_ref[away & 1, 0] = block.astype(bf16)
        else:
            d_keep_ref[away, 0] = block


def shards(section_input, section_cotan, weights, section_cuts, pipe_template):
    pipes = lax.axis_size("pipe")
    sections = lax.axis_size("section")
    tensors = lax.axis_size("tensor")
    layers, stored, width = weights.shape
    tokens = section_input.shape[2]
    features = width * tensors
    fine = stored // sections
    depth = pipes // 2
    tall = pipes * fine
    per_col = pipes // tensors
    piece = per_col * fine
    half = layers // 2
    pipe_idx = lax.axis_index("pipe")
    section_idx = lax.axis_index("section")
    tensor_idx = lax.axis_index("tensor")
    params = pltpu.CompilerParams(vmem_limit_bytes=48 * 1024 * 1024)

    def z_step(array, shift):
        pairs = [(y * depth + z, y * depth + (z + shift) % depth) for y in range(2) for z in range(depth)]
        return lax.ppermute(array, "pipe", pairs)

    def y_swap(array):
        return lax.ppermute(array, "pipe", [(p, (p + depth) % pipes) for p in range(pipes)])

    def x_step(array, shift):
        return lax.ppermute(array, "tensor", [(t, (t + shift) % tensors) for t in range(tensors)])

    def section_swap(array, bits):
        return lax.ppermute(array, "section", [(s, s ^ bits) for s in range(sections)])

    def x_swap(array, bits):
        return lax.ppermute(array, "tensor", [(t, t ^ bits) for t in range(tensors)])

    def sum_rest(array):
        for swap, bits in ((x_swap, 2), (section_swap, 1), (section_swap, 2)):
            array = array + swap(array, bits)
        return array

    def gather_section(chunk, *before):
        other = section_swap(chunk, 2)
        return chunk, section_swap(after(jnp.concatenate([chunk, other]), before), 1), other

    def after(array, other):
        return lax.optimization_barrier((array, other))[0]

    def grid(steps, ins, outs, scratch=()):
        return pltpu.PrefetchScalarGridSpec(
            num_scalar_prefetch=1, grid=steps, in_specs=ins, out_specs=outs, scratch_shapes=list(scratch)
        )

    with jax.named_scope("plan"):
        me = jnp.stack([pipe_idx, section_idx, tensor_idx]).astype(jnp.int32)
        smem = pl.BlockSpec(memory_space=pltpu.SMEM)
        plan = pl.pallas_call(
            functools.partial(plan_kernel, layers, sections, depth),
            out_shape=jax.ShapeDtypeStruct((PLAN,), jnp.int32),
            in_specs=[smem, smem, smem],
            out_specs=smem,
        )(section_cuts, pipe_template, me)

    def place(buffer, chunk, low, away):
        return lax.dynamic_update_slice(buffer, chunk[None], (away % depth, 0, low * fine, 0))

    shard = lax.dynamic_slice_in_dim(weights, section_idx * fine, fine, 1, allow_negative_indices=False)
    with jax.named_scope("weights_gather"):
        across = y_swap(shard)
        matrices = jnp.zeros((depth, layers, 2 * fine, width), bf16)
        chains = [(shard, shard), (across, across)]
        ring_steps = []
        for k in range(1, depth // 2):
            for low, (right, left) in enumerate(chains):
                right, left = z_step(right, 1), z_step(left, -1)
                chains[low] = right, left
                matrices = place(place(matrices, right, low, -k), left, low, k)
            ring_steps.append(chains[0])
        far_right, far_left = z_step(chains[0][0], 1), z_step(chains[1][1], -1)
        matrices = place(place(matrices, shard, 0, 0), across, 1, 0)

    with jax.named_scope("spread_inputs"):
        h_cols = section_input[0, 0].T
        h_wide = h_cols.astype(f32)
        squares = jnp.stack(split_three(jnp.sum(h_wide * h_wide, axis=0)))
        extra = jnp.concatenate([squares, jnp.zeros((extra_rows - 3, tokens), bf16)], axis=0)
        blocks = h_cols.reshape(per_col, sections, fine, tokens).transpose(1, 0, 2, 3)
        blocks = blocks.reshape(sections, piece, tokens)
        blocks = jnp.concatenate([blocks, jnp.broadcast_to(extra, (sections, extra_rows, tokens))], axis=1)
        blocks = after(blocks, across)
        block_for = [
            lax.dynamic_index_in_dim(blocks, section_idx ^ bits, 0, keepdims=False, allow_negative_indices=False)
            for bits in range(sections)
        ]
        other = section_swap(jnp.stack(block_for[2:]), 2)
        partner = section_swap(after(jnp.stack([block_for[1], other[1]]), ring_steps[0]), 1)
        mine = jnp.stack([block_for[0], partner[0], other[0], partner[1]])
        right, left = x_step(mine, 1), x_step(mine, -1)
        spread = mine, left, x_step(right, 1), right
        cotans = gather_section(after(section_cotan[0].transpose(0, 2, 1), across), ring_steps[1])

    wide = (depth, 1, 2 * fine, width)
    rows = (1, depth, 2 * fine, tokens)
    cols = (1, width, tokens)
    cut = (1, piece, tokens)
    with jax.named_scope("early_factors"):
        factor_a, factor_b = pl.pallas_call(
            functools.partial(early_kernel, fine, piece, tensors, features),
            out_shape=[
                jax.ShapeDtypeStruct((layers, depth, 2 * fine, tokens), bf16),
                jax.ShapeDtypeStruct((layers, width, tokens), bf16),
            ],
            grid_spec=grid(
                (layers,),
                [pl.BlockSpec((1, piece + extra_rows, tokens), lambda i, plan: (plan[HOME + i], 0, 0))] * 4
                + [
                    pl.BlockSpec(cols, lambda i, plan: (0, 0, 0)),
                    pl.BlockSpec(cols, lambda i, plan: (0, 0, 0)),
                    pl.BlockSpec(cols, lambda i, plan: (0, 0, 0)),
                    pl.BlockSpec(cols, lambda i, plan: (1, 0, 0)),
                ],
                [pl.BlockSpec(rows, lambda i, plan: (i, 0, 0, 0)), pl.BlockSpec(cols, lambda i, plan: (i, 0, 0))],
                [pltpu.VMEM((tall, tokens), f32)],
            ),
            compiler_params=params,
        )(plan, *spread, *cotans, cotans[1])

    with jax.named_scope("weights_gather"):
        far_right, far_left = after(far_right, factor_a), after(far_left, factor_a)
        matrices = place(place(matrices, far_right, 0, depth // 2), far_left, 1, depth // 2)

    with jax.named_scope("layer_products"):
        keep, send, h_live, own_cotan, back_keep, back_send = pl.pallas_call(
            functools.partial(layers_kernel, fine, piece, tensors),
            out_shape=[
                jax.ShapeDtypeStruct((2, 2, piece, tokens), f32),
                jax.ShapeDtypeStruct((2, 2, piece, tokens), bf16),
                jax.ShapeDtypeStruct((2, piece, tokens), bf16),
                jax.ShapeDtypeStruct((2, piece, tokens), f32),
                jax.ShapeDtypeStruct((2, 2, piece, tokens), f32),
                jax.ShapeDtypeStruct((2, 2, piece, tokens), bf16),
            ],
            grid_spec=grid(
                (2,),
                [
                    pl.BlockSpec(wide, lambda j, plan: (0, plan[FIRST + j], 0, 0)),
                    pl.BlockSpec(wide, lambda j, plan: (0, plan[FIRST + j] + 1, 0, 0)),
                    pl.BlockSpec(rows, lambda j, plan: (plan[FIRST + j], 0, 0, 0)),
                    pl.BlockSpec(cols, lambda j, plan: (plan[FIRST + j], 0, 0)),
                    pl.BlockSpec((1, piece + extra_rows, tokens), lambda j, plan: (plan[LIVE + j], 0, 0)),
                ],
                [
                    pl.BlockSpec((2, *cut), lambda j, plan: (0, j, 0, 0)),
                    pl.BlockSpec((2, *cut), lambda j, plan: (0, j, 0, 0)),
                    pl.BlockSpec(cut, lambda j, plan: (j, 0, 0)),
                    pl.BlockSpec(cut, lambda j, plan: (j, 0, 0)),
                    pl.BlockSpec((2, *cut), lambda j, plan: (0, j, 0, 0)),
                    pl.BlockSpec((2, *cut), lambda j, plan: (0, j, 0, 0)),
                ],
                [pltpu.VMEM((tall, tokens), f32)],
            ),
            compiler_params=params,
            cost_estimate=pl.CostEstimate(flops=8 * tall * width * tokens, bytes_accessed=4 * tall * width * 2, transcendentals=0),
        )(plan, matrices, matrices, factor_a, factor_b, mine)
    with jax.named_scope("forward_sum"):
        partial = keep + section_swap(send, 1).astype(f32)
        raised = partial[0] + section_swap(partial[1].astype(bf16), 2).astype(f32)
        h_low = (h_live.astype(f32) + raised).astype(bf16)
    with jax.named_scope("backward_sum"):
        backs = back_keep + x_swap(back_send, 2).astype(f32)
        summed = backs[0] + x_swap(backs[1].astype(bf16), 1).astype(f32)

    h_second = h_low.astype(f32)
    with jax.named_scope("spread_second"):
        own_squares = jnp.sum(h_second * h_second, axis=1)
        extra = jnp.stack(split_three(own_squares), axis=1)
        extra = jnp.concatenate([extra, jnp.zeros((2, extra_rows - 3, tokens), bf16)], axis=1)
        own_rows = jnp.concatenate([h_low, extra], axis=1)
        next_rows = x_swap(own_rows, 1)
    with jax.named_scope("second_norm"):
        squares = own_squares + jnp.sum(next_rows[:, piece : piece + 3].astype(f32), axis=1)
        inv_second = lax.rsqrt(sum_rest(after(squares, backs)) / features + epsilon)
    inv = inv_second[:, None, :]
    normed = h_second * inv
    gate = jax.nn.sigmoid(normed)
    d_norm = summed * gate * (1.0 + normed * (1.0 - gate))
    with jax.named_scope("mean_term"):
        sums = jnp.sum(h_second * d_norm, axis=1)
        sums = sums + x_swap(sums, 1)
        sums = sums + x_swap(sums, 2)
        far_rows = x_swap(after(jnp.concatenate([h_low, next_rows[:, :piece]]), sums), 2)
        sums = sums + section_swap(sums, 1)
        mean_term = ((sums + section_swap(sums, 2)) / features)[:, None, :]
    d_rows = inv * d_norm - h_second * inv * inv * inv * mean_term
    with jax.named_scope("spread_cotan"):
        around = gather_section((own_cotan + d_rows).astype(bf16), far_rows)
    with jax.named_scope("late_factors"):
        factor_a, factor_b = pl.pallas_call(
            functools.partial(late_kernel, fine, piece, tensors),
            out_shape=[
                jax.ShapeDtypeStruct((layers, depth, 2 * fine, tokens), bf16),
                jax.ShapeDtypeStruct((layers, width, tokens), bf16),
            ],
            grid_spec=grid(
                (2,),
                [
                    pl.BlockSpec((1, size, tokens), lambda j, plan, start=start: (start + j, 0, 0))
                    for size, start in zip([piece] * 5 + [piece + extra_rows] + [piece] * 2, (0, 0, 0, 2) * 2)
                ]
                + [
                    pl.BlockSpec((1, 1, tokens), lambda j, plan: (j, 0, 0)),
                    pl.BlockSpec(memory_space=pl.ANY),
                    pl.BlockSpec(memory_space=pl.ANY),
                ],
                [
                    pl.BlockSpec(rows, lambda j, plan: (plan[FIRST + j] + 1, 0, 0, 0)),
                    pl.BlockSpec(cols, lambda j, plan: (plan[FIRST + j], 0, 0)),
                ],
                [pltpu.VMEM((tall, tokens), f32), pltpu.VMEM((width, tokens), f32)],
            ),
            input_output_aliases={10: 0, 11: 1},
            compiler_params=params,
        )(plan, *around, around[1], h_low, next_rows, far_rows, far_rows, inv_second.reshape(2, 1, tokens), factor_a, factor_b)

    def block_grad(c, away):
        part = slice(c * half, (c + 1) * half)
        return lax.dot_general(
            factor_a[part, away % depth], factor_b[part], (((2,), (2,)), ((0,), (0,))), preferred_element_type=f32
        )

    with jax.named_scope("grad_sum"):
        last = depth // 2
        far = lax.dot_general(
            factor_a[:, last], factor_b, (((2,), (2,)), ((0,), (0,))), preferred_element_type=f32
        ).astype(bf16)
        far = [z_step(far[c * half : (c + 1) * half], 1 - 2 * c) for c in range(2)]
        chains = [[far[0], None], [None, far[1]]]
        for k in range(last - 1, 0, -1):
            for c in range(2):
                for side in range(2):
                    shift = 1 - 2 * side
                    total = block_grad(c, k * shift)
                    if chains[c][side] is not None:
                        total = total + chains[c][side].astype(f32)
                    chains[c][side] = z_step(total.astype(bf16), shift)
        totals = [block_grad(c, 0) + chains[c][0].astype(f32) + chains[c][1].astype(f32) for c in range(2)]
        swapped = [y_swap(t[:, fine:].astype(bf16)).astype(f32) for t in totals]
        return jnp.concatenate([t[:, :fine] + other for t, other in zip(totals, swapped)])


def solution(mesh):
    in_specs = (
        P("pipe", "section", None, "tensor"),
        P("pipe", "section", None, "tensor"),
        P(None, "pipe", "tensor"),
        P(),
        P(),
    )
    out_specs = P(None, ("pipe", "section"), "tensor")
    return jax.shard_map(shards, mesh=mesh, in_specs=in_specs, out_specs=out_specs, check_vma=False)
```

```python
import functools

import jax
import jax.numpy as jnp
from jax import lax
from jax.experimental import pallas as pl
from jax.experimental.pallas import tpu as pltpu
from jax.sharding import PartitionSpec as P

epsilon = 1e-05
bf16 = jnp.bfloat16
f32 = jnp.float32
extra_rows = 16

FIRST, LIVE, HOME, SELF = 0, 2, 4, 10
Z, LOW, SECTION, TENSOR = SELF, SELF + 1, SELF + 2, SELF + 3
PLAN = 16


def silu(values):
    return values * jax.nn.sigmoid(values)


def split_three(values):
    high = values.astype(bf16)
    rest = values - high.astype(f32)
    middle = rest.astype(bf16)
    low = (rest - middle.astype(f32)).astype(bf16)
    return high, middle, low


def plan_kernel(layers, sections, depth, cuts_ref, template_ref, self_ref, plan_ref):
    pipe, section, tensor = self_ref[0], self_ref[1], self_ref[2]
    template = template_ref[pipe]
    cuts = [cuts_ref[template, s] for s in range(sections + 1)]
    live = [jnp.where(cuts[s + 1] > cuts[s] + 1, 1, 0) for s in range(sections)]
    before = [sum(live[:s], jnp.int32(0)) for s in range(sections)]
    for j in range(2):
        here = [jnp.where((live[s] == 1) & (before[s] == j), 1, 0) for s in range(sections)]
        plan_ref[FIRST + j] = sum(here[s] * cuts[s] for s in range(sections))
        plan_ref[LIVE + j] = sum(here[s] * s for s in range(sections)) ^ section
    for layer in range(layers):
        own = [jnp.where((cuts[s] <= layer) & (layer < cuts[s + 1]), 1, 0) for s in range(sections)]
        plan_ref[HOME + layer] = sum(own[s] * s for s in range(sections)) ^ section
    plan_ref[Z] = pipe & (depth - 1)
    plan_ref[LOW] = jnp.where(pipe < depth, 0, 1)
    plan_ref[SECTION] = section
    plan_ref[TENSOR] = tensor


def row_of(plan_ref, tensor_index, part):
    z = (tensor_index & 1) * 4 + part
    return ((z - plan_ref[Z]) & 7) * 2 + ((tensor_index >> 1) ^ plan_ref[LOW])


def spread_rows(fine, piece, plan_ref, tensor_index, values, scratch):
    for part in range(piece // fine):
        at = pl.multiple_of(row_of(plan_ref, tensor_index, part) * fine, 8)
        scratch[pl.ds(at, fine), :] = values[part * fine : (part + 1) * fine]


def early_kernel(fine, piece, tensors, features, plan_ref, *refs):
    row_refs, cotan_refs, (a_out_ref, c_out_ref, scratch) = refs[:4], refs[4:8], refs[8:]
    chunks = [ref[0].astype(f32) for ref in row_refs]
    total = sum(c[piece : piece + 1] + c[piece + 1 : piece + 2] + c[piece + 2 : piece + 3] for c in chunks)
    inv = lax.rsqrt(total / features + epsilon)
    for away, chunk in enumerate(chunks):
        at_tensor = (plan_ref[TENSOR] + away) & (tensors - 1)
        spread_rows(fine, piece, plan_ref, at_tensor, silu(chunk[:piece] * inv), scratch)
    a_out_ref[0] = scratch[...].astype(bf16).reshape(a_out_ref.shape[1:])
    distance = plan_ref[HOME + pl.program_id(0)]
    for away in range(4):

        @pl.when(distance == away)
        def _(away=away):
            c_out_ref[...] = cotan_refs[away][...]


def late_kernel(fine, piece, tensors, plan_ref, *refs):
    piece_refs, row_refs, inv_ref = refs[:4], refs[4:8], refs[8]
    a_out_ref, c_out_ref, a_scratch, c_scratch = refs[-4:]
    per = piece // fine
    for away in range(4):
        at_section = plan_ref[SECTION] ^ away
        block = piece_refs[away][0].astype(f32)
        for q in range(per):
            at = pl.multiple_of((q * per + at_section) * fine, 8)
            c_scratch[pl.ds(at, fine), :] = block[q * fine : (q + 1) * fine]
    c_out_ref[0] = c_scratch[...].astype(bf16)
    for away in range(tensors):
        values = row_refs[away][0].astype(f32)[:piece]
        spread_rows(fine, piece, plan_ref, plan_ref[TENSOR] ^ away, silu(values * inv_ref[0]), a_scratch)
    a_out_ref[0] = a_scratch[...].astype(bf16).reshape(a_out_ref.shape[1:])


def layers_kernel(fine, piece, tensors, plan_ref, w1_ref, w2_ref, a_ref, c_ref, h_ref, keep_ref, send_ref, h_out_ref, c_out_ref, d_keep_ref, d_send_ref, scratch):
    per = piece // fine
    tall = w1_ref.shape[0] * w1_ref.shape[2]
    width, tokens = c_ref.shape[1:]
    active = a_ref[0].reshape(tall, tokens)
    scratch[...] = lax.dot_general(
        w1_ref[:, 0].reshape(tall, width), active, (((0,), (0,)), ((), ())), preferred_element_type=f32
    )
    for away in range(4):
        to = plan_ref[SECTION] ^ away
        parts = [scratch[pl.ds(pl.multiple_of((to + q * per) * fine, 8), fine), :] for q in range(width // piece)]
        block = jnp.concatenate(parts, axis=0)
        if away & 1:
            send_ref[away >> 1, 0] = block.astype(bf16)
        else:
            keep_ref[away >> 1, 0] = block
    h_out_ref[0] = h_ref[0][:piece]
    scratch[...] = c_ref[0].astype(f32)
    parts = [
        scratch[pl.ds(pl.multiple_of((plan_ref[SECTION] + q * per) * fine, 8), fine), :] for q in range(width // piece)
    ]
    c_out_ref[0] = jnp.concatenate(parts, axis=0)
    scratch[...] = jnp.dot(w2_ref[:, 0].reshape(tall, width), c_ref[0], preferred_element_type=f32)
    for away in range(tensors):
        to = plan_ref[TENSOR] ^ away
        parts = [
            scratch[pl.ds(pl.multiple_of(row_of(plan_ref, to, part) * fine, 8), fine), :] for part in range(per)
        ]
        block = jnp.concatenate(parts, axis=0)
        if away & 2:
            d_send_ref[away & 1, 0] = block.astype(bf16)
        else:
            d_keep_ref[away, 0] = block


def shards(section_input, section_cotan, weights, section_cuts, pipe_template):
    pipes = lax.axis_size("pipe")
    sections = lax.axis_size("section")
    tensors = lax.axis_size("tensor")
    layers, stored, width = weights.shape
    tokens = section_input.shape[2]
    features = width * tensors
    fine = stored // sections
    depth = pipes // 2
    tall = pipes * fine
    per_col = pipes // tensors
    piece = per_col * fine
    half = layers // 2
    pipe_idx = lax.axis_index("pipe")
    section_idx = lax.axis_index("section")
    tensor_idx = lax.axis_index("tensor")
    params = pltpu.CompilerParams(vmem_limit_bytes=48 * 1024 * 1024)

    def z_step(array, shift):
        pairs = [(y * depth + z, y * depth + (z + shift) % depth) for y in range(2) for z in range(depth)]
        return lax.ppermute(array, "pipe", pairs)

    def y_swap(array):
        return lax.ppermute(array, "pipe", [(p, (p + depth) % pipes) for p in range(pipes)])

    def x_step(array, shift):
        return lax.ppermute(array, "tensor", [(t, (t + shift) % tensors) for t in range(tensors)])

    def section_swap(array, bits):
        return lax.ppermute(array, "section", [(s, s ^ bits) for s in range(sections)])

    def x_swap(array, bits):
        return lax.ppermute(array, "tensor", [(t, t ^ bits) for t in range(tensors)])

    def sum_rest(array):
        for swap, bits in ((x_swap, 2), (section_swap, 1), (section_swap, 2)):
            array = array + swap(array, bits)
        return array

    def gather_section(chunk, *before):
        other = section_swap(chunk, 2)
        return chunk, section_swap(after(jnp.concatenate([chunk, other]), before), 1), other

    def after(array, other):
        return lax.optimization_barrier((array, other))[0]

    def grid(steps, ins, outs, scratch=()):
        return pltpu.PrefetchScalarGridSpec(
            num_scalar_prefetch=1, grid=steps, in_specs=ins, out_specs=outs, scratch_shapes=list(scratch)
        )

    with jax.named_scope("plan"):
        me = jnp.stack([pipe_idx, section_idx, tensor_idx]).astype(jnp.int32)
        smem = pl.BlockSpec(memory_space=pltpu.SMEM)
        plan = pl.pallas_call(
            functools.partial(plan_kernel, layers, sections, depth),
            out_shape=jax.ShapeDtypeStruct((PLAN,), jnp.int32),
            in_specs=[smem, smem, smem],
            out_specs=smem,
        )(section_cuts, pipe_template, me)

    def place(buffer, chunk, low, away):
        return lax.dynamic_update_slice(buffer, chunk[None], (away % depth, 0, low * fine, 0))

    shard = lax.dynamic_slice_in_dim(weights, section_idx * fine, fine, 1, allow_negative_indices=False)
    with jax.named_scope("weights_gather"):
        across = y_swap(shard)
        matrices = jnp.zeros((depth, layers, 2 * fine, width), bf16)
        chains = [(shard, shard), (across, across)]
        ring_steps = []
        for k in range(1, depth // 2):
            for low, (right, left) in enumerate(chains):
                right, left = z_step(right, 1), z_step(left, -1)
                chains[low] = right, left
                matrices = place(place(matrices, right, low, -k), left, low, k)
            ring_steps.append(chains[0])
        far_right, far_left = z_step(chains[0][0], 1), z_step(chains[1][1], -1)
        matrices = place(place(matrices, shard, 0, 0), across, 1, 0)

    with jax.named_scope("spread_inputs"):
        h_cols = section_input[0, 0].T
        h_wide = h_cols.astype(f32)
        squares = jnp.stack(split_three(jnp.sum(h_wide * h_wide, axis=0)))
        extra = jnp.concatenate([squares, jnp.zeros((extra_rows - 3, tokens), bf16)], axis=0)
        blocks = h_cols.reshape(per_col, sections, fine, tokens).transpose(1, 0, 2, 3)
        blocks = blocks.reshape(sections, piece, tokens)
        blocks = jnp.concatenate([blocks, jnp.broadcast_to(extra, (sections, extra_rows, tokens))], axis=1)
        blocks = after(blocks, across)
        block_for = [
            lax.dynamic_index_in_dim(blocks, section_idx ^ bits, 0, keepdims=False, allow_negative_indices=False)
            for bits in range(sections)
        ]
        other = section_swap(jnp.stack(block_for[2:]), 2)
        partner = section_swap(jnp.stack([block_for[1], other[1]]), 1)
        mine = jnp.stack([block_for[0], partner[0], other[0], partner[1]])
        right, left = x_step(mine, 1), x_step(mine, -1)
        spread = mine, left, x_step(right, 1), right
        cotans = gather_section(after(section_cotan[0].transpose(0, 2, 1), across), ring_steps[1])

    wide = (depth, 1, 2 * fine, width)
    rows = (1, depth, 2 * fine, tokens)
    cols = (1, width, tokens)
    cut = (1, piece, tokens)
    with jax.named_scope("early_factors"):
        factor_a, factor_b = pl.pallas_call(
            functools.partial(early_kernel, fine, piece, tensors, features),
            out_shape=[
                jax.ShapeDtypeStruct((layers, depth, 2 * fine, tokens), bf16),
                jax.ShapeDtypeStruct((layers, width, tokens), bf16),
            ],
            grid_spec=grid(
                (layers,),
                [pl.BlockSpec((1, piece + extra_rows, tokens), lambda i, plan: (plan[HOME + i], 0, 0))] * 4
                + [
                    pl.BlockSpec(cols, lambda i, plan: (0, 0, 0)),
                    pl.BlockSpec(cols, lambda i, plan: (0, 0, 0)),
                    pl.BlockSpec(cols, lambda i, plan: (0, 0, 0)),
                    pl.BlockSpec(cols, lambda i, plan: (1, 0, 0)),
                ],
                [pl.BlockSpec(rows, lambda i, plan: (i, 0, 0, 0)), pl.BlockSpec(cols, lambda i, plan: (i, 0, 0))],
                [pltpu.VMEM((tall, tokens), f32)],
            ),
            compiler_params=params,
        )(plan, *spread, *cotans, cotans[1])

    with jax.named_scope("weights_gather"):
        far_right, far_left = after(far_right, factor_a), after(far_left, factor_a)
        matrices = place(place(matrices, far_right, 0, depth // 2), far_left, 1, depth // 2)

    with jax.named_scope("layer_products"):
        keep, send, h_live, own_cotan, back_keep, back_send = pl.pallas_call(
            functools.partial(layers_kernel, fine, piece, tensors),
            out_shape=[
                jax.ShapeDtypeStruct((2, 2, piece, tokens), f32),
                jax.ShapeDtypeStruct((2, 2, piece, tokens), bf16),
                jax.ShapeDtypeStruct((2, piece, tokens), bf16),
                jax.ShapeDtypeStruct((2, piece, tokens), f32),
                jax.ShapeDtypeStruct((2, 2, piece, tokens), f32),
                jax.ShapeDtypeStruct((2, 2, piece, tokens), bf16),
            ],
            grid_spec=grid(
                (2,),
                [
                    pl.BlockSpec(wide, lambda j, plan: (0, plan[FIRST + j], 0, 0)),
                    pl.BlockSpec(wide, lambda j, plan: (0, plan[FIRST + j] + 1, 0, 0)),
                    pl.BlockSpec(rows, lambda j, plan: (plan[FIRST + j], 0, 0, 0)),
                    pl.BlockSpec(cols, lambda j, plan: (plan[FIRST + j], 0, 0)),
                    pl.BlockSpec((1, piece + extra_rows, tokens), lambda j, plan: (plan[LIVE + j], 0, 0)),
                ],
                [
                    pl.BlockSpec((2, *cut), lambda j, plan: (0, j, 0, 0)),
                    pl.BlockSpec((2, *cut), lambda j, plan: (0, j, 0, 0)),
                    pl.BlockSpec(cut, lambda j, plan: (j, 0, 0)),
                    pl.BlockSpec(cut, lambda j, plan: (j, 0, 0)),
                    pl.BlockSpec((2, *cut), lambda j, plan: (0, j, 0, 0)),
                    pl.BlockSpec((2, *cut), lambda j, plan: (0, j, 0, 0)),
                ],
                [pltpu.VMEM((tall, tokens), f32)],
            ),
            compiler_params=params,
            cost_estimate=pl.CostEstimate(flops=8 * tall * width * tokens, bytes_accessed=4 * tall * width * 2, transcendentals=0),
        )(plan, matrices, matrices, factor_a, factor_b, mine)
    with jax.named_scope("forward_sum"):
        partial = keep + section_swap(send, 1).astype(f32)
        raised = partial[0] + section_swap(partial[1].astype(bf16), 2).astype(f32)
        h_low = (h_live.astype(f32) + raised).astype(bf16)
    with jax.named_scope("backward_sum"):
        backs = back_keep + x_swap(back_send, 2).astype(f32)
        summed = backs[0] + x_swap(backs[1].astype(bf16), 1).astype(f32)

    h_second = h_low.astype(f32)
    with jax.named_scope("spread_second"):
        own_squares = jnp.sum(h_second * h_second, axis=1)
        extra = jnp.stack(split_three(own_squares), axis=1)
        extra = jnp.concatenate([extra, jnp.zeros((2, extra_rows - 3, tokens), bf16)], axis=1)
        own_rows = jnp.concatenate([h_low, extra], axis=1)
        next_rows = x_swap(own_rows, 1)
    with jax.named_scope("second_norm"):
        squares = own_squares + jnp.sum(next_rows[:, piece : piece + 3].astype(f32), axis=1)
        inv_second = lax.rsqrt(sum_rest(after(squares, backs)) / features + epsilon)
    inv = inv_second[:, None, :]
    normed = h_second * inv
    gate = jax.nn.sigmoid(normed)
    d_norm = summed * gate * (1.0 + normed * (1.0 - gate))
    with jax.named_scope("mean_term"):
        sums = jnp.sum(h_second * d_norm, axis=1)
        sums = sums + x_swap(sums, 1)
        sums = sums + x_swap(sums, 2)
        far_rows = x_swap(after(jnp.concatenate([h_low, next_rows[:, :piece]]), sums), 2)
        sums = sums + section_swap(sums, 1)
        mean_term = ((sums + section_swap(sums, 2)) / features)[:, None, :]
    d_rows = inv * d_norm - h_second * inv * inv * inv * mean_term
    with jax.named_scope("spread_cotan"):
        around = gather_section((own_cotan + d_rows).astype(bf16), far_rows)
    with jax.named_scope("late_factors"):
        factor_a, factor_b = pl.pallas_call(
            functools.partial(late_kernel, fine, piece, tensors),
            out_shape=[
                jax.ShapeDtypeStruct((layers, depth, 2 * fine, tokens), bf16),
                jax.ShapeDtypeStruct((layers, width, tokens), bf16),
            ],
            grid_spec=grid(
                (2,),
                [
                    pl.BlockSpec((1, size, tokens), lambda j, plan, start=start: (start + j, 0, 0))
                    for size, start in zip([piece] * 5 + [piece + extra_rows] + [piece] * 2, (0, 0, 0, 2) * 2)
                ]
                + [
                    pl.BlockSpec((1, 1, tokens), lambda j, plan: (j, 0, 0)),
                    pl.BlockSpec(memory_space=pl.ANY),
                    pl.BlockSpec(memory_space=pl.ANY),
                ],
                [
                    pl.BlockSpec(rows, lambda j, plan: (plan[FIRST + j] + 1, 0, 0, 0)),
                    pl.BlockSpec(cols, lambda j, plan: (plan[FIRST + j], 0, 0)),
                ],
                [pltpu.VMEM((tall, tokens), f32), pltpu.VMEM((width, tokens), f32)],
            ),
            input_output_aliases={10: 0, 11: 1},
            compiler_params=params,
        )(plan, *around, around[1], h_low, next_rows, far_rows, far_rows, inv_second.reshape(2, 1, tokens), factor_a, factor_b)

    def block_grad(c, away):
        part = slice(c * half, (c + 1) * half)
        return lax.dot_general(
            factor_a[part, away % depth], factor_b[part], (((2,), (2,)), ((0,), (0,))), preferred_element_type=f32
        )

    with jax.named_scope("grad_sum"):
        last = depth // 2
        far = lax.dot_general(
            factor_a[:, last], factor_b, (((2,), (2,)), ((0,), (0,))), preferred_element_type=f32
        ).astype(bf16)
        far = [z_step(far[c * half : (c + 1) * half], 1 - 2 * c) for c in range(2)]
        chains = [[far[0], None], [None, far[1]]]
        for k in range(last - 1, 0, -1):
            for c in range(2):
                for side in range(2):
                    shift = 1 - 2 * side
                    total = block_grad(c, k * shift)
                    if chains[c][side] is not None:
                        total = total + chains[c][side].astype(f32)
                    chains[c][side] = z_step(total.astype(bf16), shift)
        totals = [block_grad(c, 0) + chains[c][0].astype(f32) + chains[c][1].astype(f32) for c in range(2)]
        swapped = [y_swap(t[:, fine:].astype(bf16)).astype(f32) for t in totals]
        return jnp.concatenate([t[:, :fine] + other for t, other in zip(totals, swapped)])


def solution(mesh):
    in_specs = (
        P("pipe", "section", None, "tensor"),
        P("pipe", "section", None, "tensor"),
        P(None, "pipe", "tensor"),
        P(),
        P(),
    )
    out_specs = P(None, ("pipe", "section"), "tensor")
    return jax.shard_map(shards, mesh=mesh, in_specs=in_specs, out_specs=out_specs, check_vma=False)
```
